32 devices in a mesh: dp: 4 (over x, core), heads: 8 (over z, y).
Axes of the slice: x: 2, y: 2, z: 4, core: 2. Of those that a mesh axis runs over, the one named last changes fastest.
Arguments:
- hidden: bfloat16 [4096, 2048], P(('dp', 'heads')), may hold values from -6 to 6
- seq_lens: int32 [4, 3], P('dp'), may hold values from 1 to 1021, as said below
- norm_w: bfloat16 [2048], P(('dp', 'heads')), may hold values from 0.5 to 1.5
- w_in: bfloat16 [2048, 8512], P(('dp', 'heads')), may hold values from -0.125 to 0.125
- conv_w: bfloat16 [4, 4352], P(None, ('dp', 'heads')), may hold values from -3 to 3
- conv_b: bfloat16 [4352], P(('dp', 'heads')), may hold values from -2 to 2
- dt_bias: float32 [64], P('heads'), may hold values from -6.9 to -2.3
- a_log: float32 [64], P('heads'), may hold values from -2 to 1
- skip_gain: float32 [64], P('heads'), may hold values from 0.5 to 1.5
- gate_w: bfloat16 [4096], P(('dp', 'heads')), may hold values from 0.5 to 1.5
- w_out: bfloat16 [4096, 2048], P(('dp', 'heads')), may hold values from -0.09375 to 0.09375
- cotangent: bfloat16 [4096, 2048], P(('dp', 'heads')), may hold values from -6 to 6
Outputs:
- output: bfloat16 [4096, 2048], P(('dp', 'heads'))
- input_grad: float32 [4096, 2048], P(('dp', 'heads'))
- norm_w_grad: float32 [2048], P(('dp', 'heads'))
- w_in_grad: float32 [2048, 8512], P(('dp', 'heads'))
- conv_w_grad: float32 [4, 4352], P(None, ('dp', 'heads'))
- conv_b_grad: float32 [4352], P(('dp', 'heads'))
- dt_bias_grad: float32 [64], P('heads')
- a_log_grad: float32 [64], P('heads')
- skip_gain_grad: float32 [64], P('heads')
- gate_w_grad: float32 [4096], P(('dp', 'heads'))
- w_out_grad: float32 [4096, 2048], P(('dp', 'heads'))
The draws below stay inside these ranges and needn't reach their ends.
Inputs may be any that keep to these rules, and one draw needn't show every extreme that they name: `seq_lens`: row g holds the lengths of the 3 sequences that lie one after another from the first token of data group g; padding fills the rest of the group's 1024 tokens and is at least one token.
All inputs are finite; a program needn't handle non-finite values.
Results may differ from the reference program's by a relative error of at most 0.012.
Values may be sent and summed in bfloat16 or wider, within the bound.
No kernel may reach another device: no remote copies, remote signals or barrier semaphores. Data moves between devices by JAX's collectives and lax.ppermute only.
A program may use at most 448 MiB of HBM per device.

```python
import jax
import jax.numpy as jnp
from jax import lax

D = 2048
NH = 64
P_SIZE = 64
N = 128
CONV_K = 4
BLOCK_LEN = 256
SEQS = 3
TOK_DEV = 128
DI = 4096
CONV_CH = 4352
IN_W = 8512
TOKENS = 4096
N_DP = 4
N_HEADS = 8


def draw_seq_lens(key, part):
    key = jax.random.fold_in(key, 11)
    key_pad, key_first, key_second, key_group, key_slot = jax.random.split(key, 5)
    group_len = TOK_DEV * N_HEADS
    padding = jax.random.randint(key_pad, (N_DP,), 1, group_len // 8 + 1).astype(jnp.int32)
    live_len = (group_len - padding).astype(jnp.int32)
    first_cut = jax.random.randint(key_first, (N_DP,), 1, live_len).astype(jnp.int32)
    second_raw = jax.random.randint(key_second, (N_DP,), 1, live_len - 1).astype(jnp.int32)
    second_cut = (second_raw + (second_raw >= first_cut).astype(jnp.int32)).astype(jnp.int32)
    lower_cut = jnp.minimum(first_cut, second_cut).astype(jnp.int32)
    upper_cut = jnp.maximum(first_cut, second_cut).astype(jnp.int32)
    spread = jnp.stack([lower_cut, upper_cut - lower_cut, live_len - upper_cut], axis=1).astype(jnp.int32)
    chosen_group = jax.random.randint(key_group, (), 0, N_DP).astype(jnp.int32)
    long_slot = jax.random.randint(key_slot, (), 0, SEQS).astype(jnp.int32)
    slot_index = jnp.arange(SEQS, dtype=jnp.int32)
    extreme = jnp.where(slot_index == long_slot, group_len - SEQS, 1).astype(jnp.int32)
    group_index = jnp.arange(N_DP, dtype=jnp.int32)
    return jnp.where((group_index == chosen_group)[:, None], extreme[None, :], spread).astype(jnp.int32)


def raised(values, own_key, source, target, shards_of, factor):
    def block_of(position):
        return (jnp.arange(values.shape[position]) // (values.shape[position] // shards_of)).reshape((-1,) + (1,) * (values.ndim - 1 - position))

    near = jax.random.permutation(own_key, shards_of)[block_of(target)]
    far = (block_of(target) + shards_of // 2) % shards_of
    return jnp.where((block_of(source) == near) | (block_of(source) == far), factor * values, values)


def block_scale(rng, dims, pieces, low, high):
    factor_of, own = 1.0, jax.random.fold_in(rng, 6)
    for dim, parts in pieces:
        draws = jnp.exp(jax.random.uniform(jax.random.fold_in(own, dim), (parts,), jnp.float32, low / len(pieces), high / len(pieces)))
        factor_of = factor_of * jnp.repeat(draws, dims[dim] // parts).reshape([-1 if axis == dim else 1 for axis in range(len(dims))])
    return factor_of


def normal_values(stream_key, extent, width, limit, shards=(), held_as=jnp.bfloat16):
    values = jax.random.normal(stream_key, extent, jnp.float32) * width
    if len(shards) > 0:
        values = block_scale(stream_key, extent, shards, -0.22, 0.18) * values
    return jnp.clip(values, min=-limit, max=limit).astype(held_as)


def bell_draw_with(own_key, shape, deviation, reach, pieces, heavy, held_as=jnp.bfloat16):
    entries = deviation * jax.random.normal(own_key, shape, jnp.float32)
    if pieces:
        entries = entries * block_scale(own_key, shape, pieces, -0.22, 0.18)
    return jnp.clip(raised(entries, jax.random.fold_in(own_key, 3), *heavy), -reach, reach).astype(held_as)


def setup_inputs(seed: int = 0) -> dict:
    key_of = jax.random.split(jax.random.key(seed), 13)
    hidden = bell_draw_with(key_of[0], (TOKENS, D), 1.0, 6.0, ((0, 32),), (0, 1, 32, 2.75))
    seq_lens = draw_seq_lens(jax.random.fold_in(key_of[12], 71), 0)
    norm_w = jnp.clip(1.0 + 0.1 * jax.random.normal(key_of[2], (D,), jnp.float32), 0.5, 1.5).astype(jnp.bfloat16)
    w_in = normal_values(key_of[3], (D, IN_W), D ** -0.5, 0.125, ((0, 32),))
    conv_w = normal_values(key_of[4], (CONV_K, CONV_CH), 0.5, 3.0, ((1, 32),))
    conv_b = normal_values(key_of[5], (CONV_CH,), 0.3, 2.0, ((0, 32),))
    dt_bias = jnp.clip(-6.9 + 4.6000001430511475 * jax.random.uniform(key_of[6], (NH,), jnp.float32) ** block_scale(key_of[6], (NH,), ((0, 8),), -0.2, 0.2), -6.9, -2.3)
    a_log = jnp.clip(-2.0 + 3.0 * jax.random.uniform(key_of[7], (NH,), jnp.float32) ** block_scale(key_of[7], (NH,), ((0, 8),), -0.2, 0.2), -2.0, 1.0)
    skip_gain = jnp.clip(0.5 + 1.0 * jax.random.uniform(key_of[8], (NH,), jnp.float32) ** block_scale(key_of[8], (NH,), ((0, 8),), -0.2, 0.2), 0.5, 1.5)
    gate_w = jnp.clip(1.0 + 0.1 * jax.random.normal(key_of[9], (DI,), jnp.float32), 0.5, 1.5).astype(jnp.bfloat16)
    w_out = normal_values(key_of[10], (DI, D), DI ** -0.5, 0.09375, ((0, 32),))
    cotangent = normal_values(key_of[11], (TOKENS, D), 1.0, 6.0, ((0, 32),))
    return dict(hidden=hidden, seq_lens=seq_lens, norm_w=norm_w, w_in=w_in, conv_w=conv_w, conv_b=conv_b, dt_bias=dt_bias, a_log=a_log, skip_gain=skip_gain, gate_w=gate_w, w_out=w_out, cotangent=cotangent)


EPS = 1e-05

@jax.custom_vjp
def low(v):
    return lax.optimization_barrier(v.astype(jnp.bfloat16)).astype(jnp.float32)

@jax.custom_vjp
def low_back(v):
    return v

def low_keep(v):
    return (low(v), None)

def low_pass(kept, grad):
    return (grad,)

def back_keep(v):
    return (v, None)

def back_low(kept, grad):
    return (low(grad),)
low.defvjp(low_keep, low_pass)
low_back.defvjp(back_keep, back_low)

def rms_norm(values, gain_row):
    return values * lax.rsqrt(lax.optimization_barrier(jnp.mean(values * values, axis=-1, keepdims=True)) + EPS) * gain_row

def segment_of(positions, seq_ends):
    counted = lax.optimization_barrier(jnp.sum((positions[:, None] >= seq_ends[None, :]).astype(jnp.int32), axis=1)).astype(jnp.int32)
    return jnp.where(positions < 0, -1, counted).astype(jnp.int32)

def conv_apply(extended, seg_ext, conv_taps, conv_bias):
    row_count = extended.shape[0] - (CONV_K - 1)
    own_seg = seg_ext[CONV_K - 1:]
    total = jnp.zeros((row_count, extended.shape[1]), extended.dtype) + conv_bias[None, :]
    for tap_index in range(CONV_K):
        same_seg = (seg_ext[tap_index:tap_index + row_count] == own_seg)[:, None]
        total = total + jnp.where(same_seg, conv_taps[tap_index][None, :] * extended[tap_index:tap_index + row_count], 0.0)
    return jax.nn.silu(total)

def ssd_scan(x_heads, dt_heads, a_neg, b_state, c_state, seg_group, skip_part):
    highest = lax.Precision.HIGHEST
    length, head_count, head_width = x_heads.shape
    blocks = length // BLOCK_LEN
    x_block = x_heads.reshape(blocks, BLOCK_LEN, head_count, head_width)
    dt_block = dt_heads.reshape(blocks, BLOCK_LEN, head_count)
    cum_decay = jnp.cumsum(dt_block * a_neg[None, None, :], axis=1)
    b_block = b_state.reshape(blocks, BLOCK_LEN, b_state.shape[1])
    c_block = c_state.reshape(blocks, BLOCK_LEN, c_state.shape[1])
    seg_block = seg_group.reshape(blocks, BLOCK_LEN)
    positions_in = jnp.arange(BLOCK_LEN, dtype=jnp.int32)
    linked = (seg_block[:, :, None] == seg_block[:, None, :]) & (positions_in[:, None] >= positions_in[None, :])[None]
    linked = linked[..., None]
    log_gaps = cum_decay[:, :, None, :] - cum_decay[:, None, :, :]
    decays = jnp.where(linked, jnp.exp(jnp.where(linked, log_gaps, 0.0)), 0.0)
    scores = jnp.einsum('cqn,csn->cqs', c_block, b_block, precision=highest)
    mixing = scores[..., None] * decays * dt_block[:, None, :, :]
    inner_part = jnp.einsum('cqsh,cshp->cqhp', mixing, x_block, precision=highest)
    last_seg = seg_block[:, -1:]
    tail_weight = jnp.where((seg_block == last_seg)[..., None], jnp.exp(cum_decay[:, -1:, :] - cum_decay), 0.0) * dt_block
    states = jnp.einsum('csn,csh,cshp->chpn', b_block, tail_weight, x_block, precision=highest)
    prev_end = jnp.concatenate([jnp.full((1,), -1, jnp.int32), seg_block[:-1, -1]])
    carry_keep = jnp.where((seg_block[:, -1] == prev_end)[:, None], jnp.exp(cum_decay[:, -1, :]), 0.0)

    def advance(carried, inputs):
        block_state, block_keep = inputs
        return (block_state + block_keep[:, None, None] * carried, carried)
    start_state = jnp.zeros(states.shape[1:], states.dtype)
    _, entering = lax.scan(advance, start_state, (states, carry_keep))
    enter_weight = jnp.where((seg_block == prev_end[:, None])[..., None], jnp.exp(cum_decay), 0.0)
    outer_part = jnp.einsum('cqn,chpn->cqhp', c_block, entering, precision=highest) * enter_weight[..., None]
    result = inner_part + outer_part + skip_part[None, None, :, None] * x_block
    return result.reshape(length, head_count, head_width)

def reference(hidden, seq_lens, norm_w, w_in, conv_w, conv_b, dt_bias, a_log, skip_gain, gate_w, w_out, cotangent):
    group_len = TOK_DEV * N_HEADS
    seq_ends = jnp.cumsum(seq_lens, axis=1).astype(jnp.int32)
    positions = jnp.arange(group_len, dtype=jnp.int32)
    seg_all = jax.vmap(lambda ends_row: segment_of(positions, ends_row))(seq_ends)
    highest = lax.Precision.HIGHEST

    def forward(hidden_f, norm_f, w_in_f, conv_wf, conv_bf, dt_bias_f, a_log_f, skip_f, gate_f, w_out_f):

        def one_group(group_pair):
            group_in, group_seg = group_pair
            normed = low(rms_norm(group_in, norm_f))
            projected = low_back(jnp.dot(normed, w_in_f, precision=highest))
            gate_part = projected[:, :DI]
            conv_in = projected[:, DI:DI + CONV_CH]
            dt_raw = low_back(low(projected[:, DI + CONV_CH:]))
            seg_ext = jnp.concatenate([jnp.full((CONV_K - 1,), -1, jnp.int32), group_seg])
            extended = jnp.concatenate([jnp.zeros((CONV_K - 1, CONV_CH), conv_in.dtype), conv_in], axis=0)
            conv_out = conv_apply(extended, seg_ext, conv_wf, conv_bf)
            x_flat = low_back(low(conv_out[:, :DI]))
            b_state = low(conv_out[:, DI:DI + N])
            c_state = low(conv_out[:, DI + N:])
            steps_dt = jax.nn.softplus(dt_raw + dt_bias_f[None, :])
            a_neg = -jnp.exp(a_log_f)
            head_block = min(8, NH)
            nblocks = NH // head_block
            x_split = x_flat.reshape(group_len, nblocks, head_block, P_SIZE).transpose(1, 0, 2, 3)
            dt_split = steps_dt.reshape(group_len, nblocks, head_block).transpose(1, 0, 2)

            def head_group(head_items):
                x_part, dt_part, a_part, skip_part = head_items
                return ssd_scan(x_part, dt_part, a_part, b_state, c_state, group_seg, skip_part)
            mixed_heads = lax.map(jax.checkpoint(head_group), (x_split, dt_split, a_neg.reshape(nblocks, head_block), skip_f.reshape(nblocks, head_block)))
            scanned = mixed_heads.transpose(1, 0, 2, 3).reshape(group_len, DI)
            scanned = low_back(low(scanned))
            gated = low(rms_norm(scanned * jax.nn.silu(gate_part), gate_f))
            branch = jnp.dot(gated, w_out_f, precision=highest)
            return group_in + jnp.where((group_seg < SEQS)[:, None], branch, 0.0)
        groups_out = lax.map(jax.checkpoint(one_group), (hidden_f.reshape(N_DP, group_len, D), seg_all))
        return groups_out.reshape(N_DP * group_len, D)
    output, pullback = jax.vjp(forward, hidden.astype(jnp.float32), norm_w.astype(jnp.float32), w_in.astype(jnp.float32), conv_w.astype(jnp.float32), conv_b.astype(jnp.float32), dt_bias.astype(jnp.float32), a_log.astype(jnp.float32), skip_gain.astype(jnp.float32), gate_w.astype(jnp.float32), w_out.astype(jnp.float32))
    gradients = pullback(cotangent.astype(jnp.float32))
    return (output.astype(jnp.bfloat16), gradients[0], gradients[1], gradients[2], gradients[3], gradients[4], gradients[5], gradients[6], gradients[7], gradients[8], gradients[9])
```

```python
import numpy as np

import jax
import jax.numpy as jnp
from jax import lax
from jax.sharding import PartitionSpec as P

P_SIZE = 64
N = 128
CONV_K = 4
BLOCK_LEN = 256
SEQS = 3
DI = 4096
CONV_CH = 4352
LANE = 128
EPS = 1e-05

BF = jnp.bfloat16
F32 = jnp.float32


def ring_order(n):
    return list(range(0, n, 2)) + list(range(n - 1, 0, -2))


def ring_place(n):
    order = ring_order(n)
    place = np.zeros(n, np.int32)
    for position, index in enumerate(order):
        place[index] = position
    return np.array(order, np.int32), place


def ring_route(n, step):
    order = ring_order(n)
    return [(order[i], order[(i + step) % n]) for i in range(n)]


def xor_route(n, bits):
    return [(i, i ^ bits) for i in range(n)]


def gather_ring(block, axis, finish):
    n = lax.axis_size(axis)
    order, place = ring_place(n)
    order, mine = jnp.asarray(order), jnp.asarray(place)[lax.axis_index(axis)]
    half = n // 2
    results = [finish(block, lax.axis_index(axis))]
    ahead = behind = block
    for step in range(1, half + 1):
        ahead = lax.ppermute(ahead, axis, ring_route(n, 1))
        results.append(finish(ahead, order[(mine - step) % n]))
        if step < n - half:
            behind = lax.ppermute(behind, axis, ring_route(n, -1))
            results.append(finish(behind, order[(mine + step) % n]))
    return results


def gather_heads(block, axis):
    n = lax.axis_size(axis)
    out = jnp.zeros((n,) + block.shape, block.dtype)
    for part, owner in gather_ring(block, axis, lambda part, owner: (part, owner)):
        out = lax.dynamic_update_slice(out, part[None], (owner, 0, 0))
    return out


def scatter_ring(parts, axis):
    n = lax.axis_size(axis)
    order, place = ring_place(n)
    order, mine = jnp.asarray(order), jnp.asarray(place)[lax.axis_index(axis)]
    half = n // 2

    def shard(position):
        return lax.dynamic_index_in_dim(parts, order[position % n], 0, False)

    ahead, behind = shard(mine + half), shard(mine - (n - half - 1))
    for step in range(1, half + 1):
        ahead = lax.ppermute(ahead, axis, ring_route(n, 1))
        if step < half:
            term = shard(mine + half - step)
            ahead = (ahead.astype(F32) + term.astype(F32)).astype(parts.dtype)
    for step in range(1, n - half):
        behind = lax.ppermute(behind, axis, ring_route(n, -1))
        if step < n - half - 1:
            term = shard(mine - (n - half - 1) + step)
            behind = (behind.astype(F32) + term.astype(F32)).astype(parts.dtype)
    return shard(mine).astype(F32) + ahead.astype(F32) + behind.astype(F32)


def gather_dp(block):
    n = lax.axis_size("dp")
    me = lax.axis_index("dp")
    out = jnp.zeros((n,) + block.shape, block.dtype)
    moving = block
    for step in range(n // 2):
        if step:
            moving = lax.ppermute(moving, "dp", [(i, (i + 2) % n) for i in range(n)])
        other = lax.ppermute(moving, "dp", xor_route(n, 1))
        owner = (me - 2 * step) % n
        out = lax.dynamic_update_slice(out, moving[None], (owner, 0, 0))
        out = lax.dynamic_update_slice(out, other[None], (owner ^ 1, 0, 0))
    return out


def scatter_dp(parts):
    n = lax.axis_size("dp")
    me = lax.axis_index("dp")
    chips = n // 2
    paired = parts.reshape((chips, 2) + parts.shape[1:])
    kept = lax.dynamic_index_in_dim(paired, me % 2, 1, False)
    given = lax.dynamic_index_in_dim(paired, 1 - me % 2, 1, False)
    summed = kept.astype(F32) + lax.ppermute(given, "dp", xor_route(n, 1)).astype(F32)

    def shard(position):
        return lax.dynamic_index_in_dim(summed, position % chips, 0, False)

    chip = me // 2
    moving = shard(chip - 1 + chips)
    for step in range(1, chips):
        arrived = lax.ppermute(moving.astype(parts.dtype), "dp", [(i, (i + 2) % n) for i in range(n)])
        moving = arrived.astype(F32) + shard(chip - 1 - step + 2 * chips)
    return moving


def gather_small(block, axis):
    n = lax.axis_size(axis)
    me = lax.axis_index(axis)
    held = block[None]
    bits = 1
    while bits < n:
        other = lax.ppermute(held, axis, xor_route(n, bits))
        upper = (me & bits) > 0
        held = jnp.where(upper, jnp.concatenate([other, held]), jnp.concatenate([held, other]))
        bits *= 2
    return held


def sum_small(block, axis):
    n = lax.axis_size(axis)
    block = block + lax.ppermute(block, axis, xor_route(n, 1))
    total = block
    for bits in range(2, n, 2):
        total = total + lax.ppermute(block, axis, xor_route(n, bits))
    return total


def packed(arrays):
    flat = jnp.concatenate([a.astype(F32).reshape(-1) for a in arrays])
    flat = jnp.pad(flat, (0, -flat.shape[0] % LANE))
    return flat.reshape(-1, LANE)


def segment_of(positions, seq_ends):
    return jnp.sum((positions[:, None] >= seq_ends[None, :]).astype(jnp.int32), axis=1)


def conv_apply(conv_in, seg, conv_taps, conv_bias):
    rows = conv_in.shape[0]
    extended = jnp.pad(conv_in, ((CONV_K - 1, 0), (0, 0)))
    seg_ext = jnp.pad(seg, (CONV_K - 1, 0), constant_values=-1)
    total = jnp.zeros((rows, conv_in.shape[1]), conv_in.dtype) + conv_bias[None, :]
    for tap_index in range(CONV_K):
        same_seg = (seg_ext[tap_index : tap_index + rows] == seg)[:, None]
        total = total + jnp.where(
            same_seg, conv_taps[tap_index][None, :] * extended[tap_index : tap_index + rows], 0.0
        )
    return jax.nn.silu(total)


def ssd_scan(x_heads, dt_heads, a_neg, b_state, c_state, seg_group, skip_part):
    length, head_count, head_width = x_heads.shape
    blocks = length // BLOCK_LEN
    x_block = x_heads.reshape(blocks, BLOCK_LEN, head_count, head_width)
    dt_block = dt_heads.reshape(blocks, BLOCK_LEN, head_count)
    cum_decay = jnp.cumsum(dt_block * a_neg[None, None, :], axis=1)
    b_block = b_state.reshape(blocks, BLOCK_LEN, b_state.shape[1])
    c_block = c_state.reshape(blocks, BLOCK_LEN, c_state.shape[1])
    seg_block = seg_group.reshape(blocks, BLOCK_LEN)
    positions_in = jnp.arange(BLOCK_LEN, dtype=jnp.int32)
    linked = (seg_block[:, :, None] == seg_block[:, None, :]) & (
        positions_in[:, None] >= positions_in[None, :]
    )[None]
    linked = linked[..., None]
    log_gaps = cum_decay[:, :, None, :] - cum_decay[:, None, :, :]
    decays = jnp.where(linked, jnp.exp(jnp.where(linked, log_gaps, 0.0)), 0.0)
    scores = jnp.einsum("cqn,csn->cqs", c_block, b_block)
    mixing = scores[..., None] * decays * dt_block[:, None, :, :]
    inner_part = jnp.einsum("cqsh,cshp->cqhp", mixing, x_block)
    last_seg = seg_block[:, -1:]
    tail_weight = (
        jnp.where(
            (seg_block == last_seg)[..., None], jnp.exp(cum_decay[:, -1:, :] - cum_decay), 0.0
        )
        * dt_block
    )
    states = jnp.einsum("csn,csh,cshp->chpn", b_block, tail_weight, x_block)
    prev_end = jnp.concatenate([jnp.full((1,), -1, jnp.int32), seg_block[:-1, -1]])
    carry_keep = jnp.where(
        (seg_block[:, -1] == prev_end)[:, None], jnp.exp(cum_decay[:, -1, :]), 0.0
    )

    def advance(carried, inputs):
        block_state, block_keep = inputs
        return (block_state + block_keep[:, None, None] * carried, carried)

    start_state = jnp.zeros(states.shape[1:], states.dtype)
    _, entering = lax.scan(advance, start_state, (states, carry_keep))
    enter_weight = jnp.where((seg_block == prev_end[:, None])[..., None], jnp.exp(cum_decay), 0.0)
    outer_part = jnp.einsum("cqn,chpn->cqhp", c_block, entering) * enter_weight[..., None]
    result = inner_part + outer_part + skip_part[None, None, :, None] * x_block
    return result.reshape(length, head_count, head_width)


def after(value, *others):
    return lax.optimization_barrier((value,) + others)[0]


def shards(
    hidden, seq_lens, norm_w, w_in, conv_w, conv_b, dt_bias, a_log, skip_gain, gate_w, w_out, cotangent
):
    dp, heads = lax.axis_size("dp"), lax.axis_size("heads")
    my_dp, my_head = lax.axis_index("dp"), lax.axis_index("heads")
    me = my_dp * heads + my_head
    rows_dev, width = hidden.shape
    length = rows_dev * heads
    w_rows = w_in.shape[0]
    out_rows = w_out.shape[0]
    own = DI // heads
    own_heads = own // P_SIZE
    taps_dev = conv_b.shape[0]
    striped = out_rows % P_SIZE == 0
    per_block = own_heads // dp if striped else 0

    def split_own(array, size):
        rows = array.shape[0]
        if striped:
            cut = array.reshape(rows, dp, heads, per_block * size).transpose(2, 0, 1, 3)
        else:
            cut = array.reshape(rows, heads, own_heads * size).transpose(1, 0, 2)
        return cut.reshape(heads, rows, own_heads * size)

    def join_own(array, size):
        rows = array.shape[1]
        if striped:
            cut = array.reshape(heads, rows, dp, per_block * size).transpose(1, 2, 0, 3)
        else:
            cut = array.transpose(1, 0, 2)
        return cut.reshape(rows, heads * own_heads * size)

    def pick_own(row, size):
        return lax.dynamic_index_in_dim(split_own(row.reshape(1, -1), size), my_head, 0, False)[0]

    small = packed([conv_w, conv_b, norm_w, gate_w, dt_bias, a_log, skip_gain])
    small_all = gather_small(gather_small(small, "heads").reshape(-1, LANE), "dp")
    small_all = small_all.reshape(dp * heads, -1)
    marks = np.cumsum([0, 4 * taps_dev, taps_dev, w_rows, out_rows] + 3 * [dt_bias.shape[0]])
    pieces = [small_all[:, marks[i] : marks[i + 1]] for i in range(7)]
    taps_full = pieces[0].reshape(-1, CONV_K, taps_dev).transpose(1, 0, 2).reshape(CONV_K, CONV_CH)
    bias_full = pieces[1].reshape(-1)
    norm_full = pieces[2].reshape(-1)
    gate_gain = pick_own(pieces[3], P_SIZE)
    head_params = [pick_own(p[:heads], 1) for p in pieces[4:]]

    def pick_channels(array):
        split = split_own(array[:, :DI], P_SIZE)
        mine = lax.dynamic_index_in_dim(split, my_head, 0, False)
        return jnp.concatenate([mine, array[:, DI:]], axis=1)

    taps_own = pick_channels(taps_full)
    bias_own = pick_channels(bias_full[None])[0]

    pad = LANE - own_heads
    w_gate_cut = split_own(w_in[:, :DI], P_SIZE)
    w_mix_cut = jnp.concatenate(
        [
            split_own(w_in[:, DI : 2 * DI], P_SIZE),
            jnp.broadcast_to(w_in[None, :, 2 * DI : DI + CONV_CH], (heads, w_rows, 2 * N)),
            split_own(w_in[:, DI + CONV_CH :], 1),
            jnp.zeros((heads, w_rows, pad), BF),
        ],
        axis=2,
    )

    def spread(cut):
        got = lax.all_to_all(cut, "heads", split_axis=0, concat_axis=0, tiled=True)
        return gather_dp(got.reshape(heads * w_rows, -1)).reshape(width, -1)

    w_mix = spread(w_mix_cut)
    hidden_all = gather_heads(hidden, "heads").reshape(length, width)
    w_gate = spread(after(w_gate_cut, w_mix))
    if striped:
        w_out_own = gather_dp(w_out).reshape(own, width)
    else:
        route = [(q, (q % dp) * heads + q // dp) for q in range(dp * heads)]
        w_out_own = gather_dp(lax.ppermute(w_out, ("dp", "heads"), route)).reshape(own, width)
    cot_all = gather_heads(after(cotangent, hidden_all), "heads").reshape(length, width)

    seq_ends = jnp.cumsum(seq_lens[0])
    seg = segment_of(jnp.arange(length, dtype=jnp.int32), seq_ends)
    seg_mine = lax.dynamic_slice(seg, (my_head * rows_dev,), (rows_dev,))
    live = (seg < SEQS)[:, None]
    live_mine = (seg_mine < SEQS)[:, None]

    hidden_f = hidden_all.astype(F32)
    scale = lax.rsqrt(jnp.mean(hidden_f * hidden_f, axis=-1, keepdims=True) + EPS)
    normed = (hidden_f * scale * norm_full[None]).astype(BF)
    mix = jnp.dot(normed, w_mix, preferred_element_type=F32)
    conv_in = mix[:, : own + 2 * N]
    dt_low = mix[:, own + 2 * N : own + 2 * N + own_heads].astype(BF)

    def conv_local(rows_in, taps_in, bias_in):
        return conv_apply(rows_in, seg, taps_in, bias_in)

    conv_out, conv_pull = jax.vjp(conv_local, conv_in, taps_own, bias_own)
    conv_low = conv_out.astype(BF).astype(F32)

    def scan_local(conv_rows, dt_in, bias_in, log_in, skip_in):
        mixed = ssd_scan(
            conv_rows[:, :own].reshape(length, own_heads, P_SIZE),
            jax.nn.softplus(dt_in + bias_in[None, :]),
            -jnp.exp(log_in),
            conv_rows[:, own : own + N],
            conv_rows[:, own + N :],
            seg,
            skip_in,
        )
        return mixed.reshape(length, own)

    scanned, scan_pull = jax.vjp(scan_local, conv_low, dt_low.astype(F32), *head_params)
    scanned = scanned.astype(BF).astype(F32)
    gate_part = jnp.dot(normed, w_gate, preferred_element_type=F32)
    gate_sig = jax.nn.sigmoid(gate_part)
    gate_act = gate_part * gate_sig
    inner = scanned * gate_act
    raw = (inner * gate_gain[None]).astype(BF)
    branch = jnp.dot(raw, w_out_own, preferred_element_type=F32).astype(BF)
    branch_mine = scatter_ring(branch.reshape(heads, rows_dev, width), "heads")

    grad_branch = jnp.where(live, cot_all, jnp.zeros_like(cot_all))
    grad_gated = lax.dot_general(
        grad_branch, w_out_own, (((1,), (1,)), ((), ())), preferred_element_type=F32
    )
    weighted = grad_gated * gate_gain[None]
    sums = jnp.stack([jnp.sum(inner * inner, axis=1), jnp.sum(inner * weighted, axis=1)])
    sums = sum_small(sums.reshape(-1, LANE), "heads").reshape(2, length)
    ratio = lax.rsqrt(sums[0] / DI + EPS)
    pull = ratio * ratio * ratio * sums[1] / DI
    ratio_mine = lax.dynamic_slice(ratio, (my_head * rows_dev,), (rows_dev,))[:, None]
    ratio, pull = ratio[:, None], pull[:, None]
    output = (hidden.astype(F32) + jnp.where(live_mine, branch_mine * ratio_mine, 0.0)).astype(BF)
    gated = (inner * ratio * gate_gain[None]).astype(BF)
    contract_first = (((0,), (0,)), ((), ()))
    w_out_term = lax.dot_general(gated, grad_branch, contract_first, preferred_element_type=F32)
    w_out_grad = scatter_dp(w_out_term.astype(BF).reshape(dp, out_rows, width))
    if not striped:
        back = [(dst, src) for src, dst in route]
        w_out_grad = lax.ppermute(w_out_grad, ("dp", "heads"), back)
    gate_w_grad = jnp.sum(w_out.astype(F32) * w_out_grad, axis=1) / gate_w.astype(F32)
    grad_inner = ratio * weighted - inner * pull
    grad_scan = (grad_inner * gate_act).astype(BF)
    grad_gate = (grad_inner * scanned * gate_sig * (1.0 + gate_part * (1.0 - gate_sig))).astype(BF)

    grad_conv, grad_dt, grad_bias, grad_log, grad_skip = scan_pull(grad_scan.astype(F32))
    grad_x = grad_conv[:, :own].astype(BF).astype(F32)
    grad_conv = jnp.concatenate([grad_x, grad_conv[:, own:]], axis=1)
    grad_conv_in, grad_taps, grad_biases = conv_pull(grad_conv)
    grad_mix = jnp.concatenate(
        [grad_conv_in, grad_dt, jnp.zeros((length, pad), F32)], axis=1
    ).astype(BF)

    contract_last = (((1,), (1,)), ((), ()))

    def to_rows(term):
        cols = term.shape[1]
        summed = scatter_dp(term.astype(BF).reshape(dp, heads * w_rows, cols)).astype(BF)
        cut = summed.reshape(heads, w_rows, cols)
        return lax.all_to_all(cut, "heads", split_axis=0, concat_axis=0, tiled=True).astype(F32)

    gate_cols = to_rows(lax.dot_general(normed, grad_gate, contract_first, preferred_element_type=F32))
    grad_normed = lax.dot_general(
        grad_gate, w_gate, contract_last, preferred_element_type=F32
    ) + lax.dot_general(grad_mix, w_mix, contract_last, preferred_element_type=F32)
    grad_mine = scatter_ring(grad_normed.astype(BF).reshape(heads, rows_dev, width), "heads")
    mix_cols = to_rows(lax.dot_general(normed, grad_mix, contract_first, preferred_element_type=F32))
    w_in_grad = jnp.concatenate(
        [
            join_own(gate_cols, P_SIZE),
            join_own(mix_cols[:, :, :own], P_SIZE),
            jnp.sum(mix_cols[:, :, own : own + 2 * N], axis=0),
            join_own(mix_cols[:, :, own + 2 * N : own + 2 * N + own_heads], 1),
        ],
        axis=1,
    )
    norm_w_grad = jnp.sum(w_in.astype(F32) * w_in_grad, axis=1) / norm_w.astype(F32)

    residual = hidden.astype(F32)
    scale_mine = lax.rsqrt(jnp.mean(residual * residual, axis=-1, keepdims=True) + EPS)
    grad_mine = grad_mine * norm_full[None]
    along = jnp.mean(residual * grad_mine, axis=-1, keepdims=True)
    input_grad = cotangent.astype(F32) + scale_mine * (
        grad_mine - residual * (scale_mine * scale_mine * along)
    )

    sent = packed([grad_taps, grad_biases, grad_bias, grad_log, grad_skip])
    summed = sum_small(sent, "dp")
    collected = gather_small(summed, "heads").reshape(heads, -1)
    mine_ch = own + 2 * N
    conv_grads = collected[:, : (CONV_K + 1) * mine_ch].reshape(heads, CONV_K + 1, mine_ch)
    conv_grads = jnp.concatenate(
        [join_own(conv_grads[:, :, :own], P_SIZE), jnp.sum(conv_grads[:, :, own:], axis=0)], axis=1
    )
    conv_grads = lax.dynamic_slice(conv_grads, (0, me * taps_dev), (CONV_K + 1, taps_dev))
    at = (CONV_K + 1) * mine_ch
    head_grads = collected[:, at : at + 3 * own_heads].reshape(heads, 3, own_heads)
    head_grads = join_own(head_grads, 1)
    head_grads = lax.dynamic_slice(head_grads, (0, my_head * own_heads), (3, own_heads))
    return (
        output,
        input_grad,
        norm_w_grad,
        w_in_grad,
        conv_grads[:CONV_K],
        conv_grads[CONV_K],
        head_grads[0],
        head_grads[1],
        head_grads[2],
        gate_w_grad,
        w_out_grad,
    )


def solution(mesh):
    both = ("dp", "heads")
    placed = (
        P(both, None),
        P("dp", None),
        P(both),
        P(both, None),
        P(None, both),
        P(both),
        P("heads"),
        P("heads"),
        P("heads"),
        P(both),
        P(both, None),
        P(both, None),
    )
    return jax.shard_map(
        shards,
        mesh=mesh,
        in_specs=placed,
        out_specs=(
            P(both, None),
            P(both, None),
            P(both),
            P(both, None),
            P(None, both),
            P(both),
            P("heads"),
            P("heads"),
            P("heads"),
            P(both),
            P(both, None),
        ),
        check_vma=False,
    )
```

```python
import functools

import numpy as np

import jax
import jax.numpy as jnp
from jax import lax
from jax.experimental import pallas as pl
from jax.experimental.pallas import tpu as pltpu
from jax.sharding import PartitionSpec as P

P_SIZE = 64
N = 128
CONV_K = 4
BLOCK_LEN = 256
SEQS = 3
DI = 4096
CONV_CH = 4352
LANE = 128
EPS = 1e-05
ROWS = 512
RING = SEQS
SCAN_VMEM = 20 * 2**20

NO_COST = pl.CostEstimate(flops=0, bytes_accessed=0, transcendentals=0)
BF = jnp.bfloat16
F32 = jnp.float32


def ring_order(n):
    return list(range(0, n, 2)) + list(range(n - 1, 0, -2))


def where_vector(ends):
    heads, dp = lax.axis_size("heads"), lax.axis_size("dp")
    order = ring_order(heads)
    ring = np.zeros((heads, heads), np.int32)
    for position, index in enumerate(order):
        ring[index] = [order[(position + distance) % heads] for distance in range(heads)]
    owners = np.array([dp_owners(dp, me) for me in range(dp)], np.int32)
    return jnp.concatenate(
        [ends, jnp.asarray(ring)[lax.axis_index("heads")], jnp.asarray(owners)[lax.axis_index("dp")]]
    )


def ring_route(n, step):
    order = ring_order(n)
    return [(order[i], order[(i + step) % n]) for i in range(n)]


def xor_route(n, bits):
    return [(i, i ^ bits) for i in range(n)]


class Line:
    def __init__(self):
        self.last = ()

    def take(self, *values):
        values, _ = lax.optimization_barrier((values, self.last))
        self.last = (values[0],)
        return values if len(values) > 1 else values[0]

    def take_with(self, main, others):
        taken, _ = lax.optimization_barrier(((list(main.values()), list(others)), self.last))
        self.last = (taken[0][0],)
        return dict(zip(main, taken[0])), taken[1]

    def mark(self, value):
        self.last = (value,)
        return value


class GatherRing:
    def __init__(self, rows, axis):
        self.axis, self.n = axis, lax.axis_size(axis)
        self.half = self.n // 2
        self.step = 0
        self.arrived = {0: [rows]}
        self.moving = {way: self.sent(rows, way) for way in (1, -1)}

    def sent(self, value, way):
        return lax.ppermute(value, self.axis, ring_route(self.n, way))

    def advance(self, line, *others):
        self.step += 1
        moving, others = line.take_with(self.moving, others)
        self.moving = {}
        if self.step == self.half:
            self.arrived[self.half] = [moving[1], moving[-1]]
            return others
        for way, value in moving.items():
            self.arrived[-way * self.step % self.n] = [value]
            if self.step == self.half - 1:
                middle = value.shape[0] // 2
                value = value[:middle] if way == 1 else value[middle:]
            self.moving[way] = self.sent(value, way)
        return others

    def all(self):
        return [self.arrived[d] for d in range(self.n)]


class ScatterRing:
    def __init__(self, parts, axis):
        self.axis, self.n = axis, lax.axis_size(axis)
        self.half = self.n // 2
        self.parts = parts
        self.left = self.half
        self.moving = {1: self.sent(parts[self.half][0], 1), -1: self.sent(parts[self.half][1], -1)}

    def sent(self, value, way):
        return lax.ppermute(value, self.axis, ring_route(self.n, way))

    def advance(self, line, *others):
        self.left -= 1
        moving, others = line.take_with(self.moving, others)
        if not self.left:
            self.sums = [moving[1], moving[-1]]
            return others
        for way, value in moving.items():
            (part,) = self.parts[way * self.left % self.n]
            total = add_rows(value, part, 0 if way == 1 else part.shape[0] - value.shape[0])
            self.moving[way] = self.sent(total, way)
        return others


class ScatterRings:
    def __init__(self, parts, axis):
        self.axis, self.n = axis, lax.axis_size(axis)
        self.half = self.n // 2
        self.parts = parts
        self.left = self.half
        self.sums = [[], []]
        self.moving = {}
        for chunk, way in ((0, 1), (1, -1)):
            self.send(chunk, way, parts[self.half][chunk])

    def send(self, chunk, way, value):
        self.moving[chunk, way] = lax.ppermute(value, self.axis, ring_route(self.n, way))

    def advance(self, line, *others):
        self.left -= 1
        moving, others = line.take_with(self.moving, others)
        self.moving = {}
        for (chunk, way), value in moving.items():
            if self.left:
                value = add_rows(value, self.parts[way * self.left % self.n][chunk], 0)
                self.send(chunk, way, value)
            else:
                self.sums[chunk].append(value)
        if self.left == self.half - 1:
            for chunk, way in ((1, 1), (0, -1)):
                self.send(chunk, way, self.parts[way * self.left % self.n][chunk])
        return others


def dp_owners(n, me):
    return [((me - 2 * s) % n) ^ b for b in range(2) for s in range(n // 2)]


def next_chip(value):
    n = lax.axis_size("dp")
    return lax.ppermute(value, "dp", [(i, (i + 2) % n) for i in range(n)])


def other_core(value):
    return lax.ppermute(value, "dp", xor_route(lax.axis_size("dp"), 1))


class GatherDp:
    def __init__(self, block):
        self.chips = lax.axis_size("dp") // 2
        self.near, self.far = [block], [other_core(block)]
        self.moving = [next_chip(block)] if self.chips > 1 else []

    def relay(self, line, arrived):
        for step in range(1, self.chips):
            (value,) = arrived if step == 1 else (line.take(self.moving[0]),)
            self.near.append(value)
            self.far.append(other_core(value))
            self.moving = [next_chip(value)] if step + 1 < self.chips else []

    def all(self, arrived):
        return self.near + list(arrived)


class ScatterDp:
    def __init__(self, kept, given):
        self.chips = lax.axis_size("dp") // 2
        self.kept = kept
        self.moving = [other_core(given)]

    def relay(self, line, arrived):
        self.sums = add_core(self.kept, arrived[0], self.chips)
        self.moving = [next_chip(self.sums[1])] if self.chips > 1 else []
        for step in range(2, self.chips):
            value = line.take(self.moving[0]).astype(F32)
            self.moving = [next_chip((value + self.sums[step]).astype(BF))]

    def all(self, arrived, dtype):
        if self.chips == 1:
            return self.sums[0].astype(dtype)
        return add_last(arrived[0], self.sums[0], dtype)


def doubled(block, axis, bits):
    return jnp.concatenate([block, lax.ppermute(block, axis, xor_route(lax.axis_size(axis), bits))])


def powers(axis):
    return [1 << k for k in range(lax.axis_size(axis).bit_length() - 1)]


def vmem_of(arrays, specs, rest):
    total = rest
    for array, spec in zip(arrays, specs):
        if spec.block_shape is not None:
            copies = 1 if spec.pipeline_mode else 2
            total += copies * int(np.prod(spec.block_shape)) * array.dtype.itemsize
    return total


def call_kernel(body, scalars, grid, ins, in_specs, outs, out_specs, name, scratch=(), flops=0, rest=6 * 2**20):
    bytes_moved = sum(int(np.prod(a.shape)) * a.dtype.itemsize for a in outs)
    return pl.pallas_call(
        body,
        grid_spec=pltpu.PrefetchScalarGridSpec(
            num_scalar_prefetch=1, grid=grid, in_specs=in_specs, out_specs=out_specs, scratch_shapes=scratch
        ),
        out_shape=outs,
        compiler_params=pltpu.CompilerParams(
            vmem_limit_bytes=vmem_of((*ins, *outs), (*in_specs, *out_specs), rest)
        ),
        cost_estimate=NO_COST,
        name=name,
    )(scalars, *ins)


def whole(array):
    return pl.BlockSpec(array.shape, lambda *i: (0, 0))


def once(array):
    return pl.BlockSpec(array.shape, lambda *i: (0, 0), pipeline_mode=pl.Buffered(1))


def rows_of(width, rows=ROWS):
    return pl.BlockSpec((rows, width), lambda i, s: (i, 0))


def call_whole(body, ins, outs, name, rest=2**20):
    specs = [pl.BlockSpec(memory_space=pltpu.VMEM)] * len(ins), [pl.BlockSpec(memory_space=pltpu.VMEM)] * len(outs)
    held = sum(int(np.prod(a.shape)) * a.dtype.itemsize for a in (*ins, *outs))
    return pl.pallas_call(
        body,
        in_specs=specs[0],
        out_specs=specs[1],
        out_shape=outs,
        compiler_params=pltpu.CompilerParams(vmem_limit_bytes=held + rest),
        cost_estimate=NO_COST,
        name=name,
    )(*ins)


def add_rows_kernel(place, sent, part, out):
    rows = sent.shape[0]
    if rows < out.shape[0]:
        out[...] = part[...]
    at = slice(place, place + rows)
    out[at, :] = (sent[...].astype(F32) + part[at, :].astype(F32)).astype(BF)


def add_rows(sent, part, place):
    body = functools.partial(add_rows_kernel, place)
    return call_whole(body, (sent, part), [jax.ShapeDtypeStruct(part.shape, BF)], "add_rows")[0]


def add_core_kernel(kept, given, *outs):
    rows = outs[0].shape[0]
    for k, out in enumerate(outs):
        at = slice(k * rows, (k + 1) * rows)
        out[...] = (kept[at, :].astype(F32) + given[at, :].astype(F32)).astype(out.dtype)


def add_core(kept, given, chips):
    rows, cols = kept.shape[0] // chips, kept.shape[1]
    outs = [jax.ShapeDtypeStruct((rows, cols), BF if k == 1 else F32) for k in range(chips)]
    return call_whole(add_core_kernel, (kept, given), outs, "add_core")


def add_last_kernel(arrived, kept, out):
    out[...] = (arrived[...].astype(F32) + kept[...]).astype(out.dtype)


def add_last(arrived, kept, dtype):
    return call_whole(add_last_kernel, (arrived, kept), [jax.ShapeDtypeStruct(kept.shape, dtype)], "add_last")[0]


def weight_term_kernel(half, where, left, right, kept, given):
    product = mm(left[...], right[...], ((0,), (0,))).astype(BF)

    @pl.when(pl.program_id(0) < half)
    def _():
        kept[...] = product

    @pl.when(pl.program_id(0) >= half)
    def _():
        given[...] = product


def weight_term(where, left, right, block, steps, column):
    length, cols = right.shape
    half = steps // 2
    out = jax.ShapeDtypeStruct((half * block, cols), BF)
    return call_kernel(
        functools.partial(weight_term_kernel, half),
        where,
        (steps,),
        (left, right),
        [pl.BlockSpec((length, block), lambda i, s: (0, column(i, s))), once(right)],
        [out, out],
        [
            pl.BlockSpec((block, cols), lambda i, s: (jnp.minimum(i, half - 1), 0)),
            pl.BlockSpec((block, cols), lambda i, s: (jnp.maximum(i - half, 0), 0)),
        ],
        "weight_term",
        rest=12 * 2**20,
    )


class Small:
    BIAS, NORM, GATE, HEADS = CONV_K, CONV_K + 1, CONV_K + 2, CONV_K + 3
    SKIP_GRAD, BIAS_GRAD, LOG_GRAD = CONV_K + 1, CONV_K + 2, CONV_K + 3


def pack_small(conv_w, conv_b, norm_w, gate_w, dt_bias, a_log, skip_gain):
    per_head = jnp.concatenate([dt_bias, a_log, skip_gain])
    rows = [conv_w] + [row.reshape(1, -1) for row in (conv_b, norm_w, gate_w, per_head)]
    lanes = max(row.shape[1] for row in rows)
    lanes = -(-lanes // LANE) * LANE
    return jnp.concatenate([jnp.pad(row.astype(F32), ((0, 0), (0, lanes - row.shape[1]))) for row in rows])


def lanes_of(width):
    return lax.broadcasted_iota(jnp.int32, (8, width), 1)


def own_blocks(dp, heads, head, own, striped):
    if striped:
        size = own // dp
        return [(j * heads + head) * size for j in range(dp)], size
    return [head * own], own


def unpack_kernel(dp, heads, per_device, striped, where, table, taps, gate, norm, head_rows, skip):
    own = gate.shape[1]
    my_head, my_dp = where[RING], where[RING + heads]
    lanes = table.shape[1]

    def tile(at_dp, at_head):
        slot = at_head * dp + (at_dp ^ my_dp)
        return table[pl.ds(pl.multiple_of(slot * 8, 8), 8), :]

    def run(first, width):
        lane = lanes_of(LANE)
        start = first // width
        shift = first - start * width
        total = jnp.zeros((8, LANE), F32)
        for k in range((LANE + width - 2) // width + 1):
            device = jnp.minimum(start + k, dp * heads - 1)
            moved = pltpu.roll(tile(device // heads, device % heads), (k * width - shift) % lanes, 1)[:, :LANE]
            source = lane - k * width + shift
            total = jnp.where((source >= 0) & (source < width), moved, total)
        return total

    blocks, size = own_blocks(dp, heads, my_head, own, striped)
    conv_width, norm_width, gate_width = per_device
    at = 0
    for first in blocks:
        for more in range(0, size, LANE):
            taps[:, at : at + LANE] = run(first + more, conv_width)
            gate[:, at : at + LANE] = run(first + more, gate_width)
            at += LANE
    for more in range(0, 2 * N, LANE):
        taps[:, own + more : own + more + LANE] = run(jnp.int32(DI + more), conv_width)
    for more in range(0, norm.shape[1], LANE):
        norm[:, more : more + LANE] = run(jnp.int32(more), norm_width)
    lane = lanes_of(LANE)
    own_heads = own // P_SIZE
    found = [jnp.zeros((8, LANE), F32)] * 3
    for k in range(own_heads):
        each = own_heads // len(blocks)
        head = blocks[k // each] // P_SIZE + k % each
        device = head // own_heads
        values = tile(my_dp, device)
        for kind in range(3):
            source = kind * own_heads + head - device * own_heads
            moved = pltpu.roll(values, (k - source + lanes) % lanes, 1)[:, :LANE]
            found[kind] = jnp.where(lane == k, moved, found[kind])
    row = slice(Small.HEADS, Small.HEADS + 1)
    head_rows[...] = jnp.zeros_like(head_rows)
    head_rows[0:1, :] = found[0][row, :]
    head_rows[1:2, :] = jnp.where(lane[0:1, :] < own_heads, -jnp.exp(found[1][row, :]), 0.0)
    head_of = lax.broadcasted_iota(jnp.int32, (LANE, own), 1) // P_SIZE
    spread = (head_of == lax.broadcasted_iota(jnp.int32, (LANE, own), 0)).astype(F32).astype(BF)
    skip[...] = split_times(found[2], spread, 3)


def unpack(where, dp, heads, striped, own, width, per_device, table):
    outs = [jax.ShapeDtypeStruct((8, w), F32) for w in (own + 2 * N, own, width, LANE, own)]
    return call_kernel(
        functools.partial(unpack_kernel, dp, heads, per_device, striped),
        where,
        (1,),
        (table,),
        [whole(table)],
        outs,
        [whole(o) for o in outs],
        "unpack",
    )


def collect_kernel(dp, heads, striped, taps_dev, where, table, taps, bias, head_out, full, by_head):
    chans = table.shape[1]
    own = chans - 2 * N
    own_heads = own // P_SIZE
    my_head, my_dp = where[RING], where[RING + heads]

    def slot(at_head):
        return at_head * 8

    full[...] = jnp.zeros_like(full)
    shared = jnp.zeros((8, 2 * N), F32)
    chan_head = lax.broadcasted_iota(jnp.int32, (own, LANE), 0) // P_SIZE
    gather = (chan_head == lax.broadcasted_iota(jnp.int32, (own, LANE), 1)).astype(F32).astype(BF)
    row = lax.broadcasted_iota(jnp.int32, (8, LANE), 0)
    for head in range(heads):
        tile = table[pl.ds(slot(head), 8), :]
        blocks, size = own_blocks(dp, heads, head, own, striped)
        for k, first in enumerate(blocks):
            full[:, first : first + size] = tile[:, k * size : (k + 1) * size]
        shared = shared + tile[:, own:]
        summed = split_times(tile[:, :own], gather, 3)
        by_head[head * 8 : (head + 1) * 8, :] = jnp.where(row == Small.SKIP_GRAD, summed, tile[:, :LANE])
    full[:, DI : DI + 2 * N] = shared
    first = (my_dp * heads + my_head) * taps_dev
    start = first // LANE
    window = -(-(taps_dev + LANE) // LANE) * LANE
    rows = full[:, pl.ds(pl.multiple_of(start * LANE, LANE), window)]
    rows = pltpu.roll(rows, (window - (first - start * LANE)) % window, 1)[:, :taps_dev]
    taps[...] = rows[:CONV_K, :]
    bias[...] = rows[CONV_K : CONV_K + 1, :]
    lane = lanes_of(LANE)
    total = jnp.zeros((8, LANE), F32)
    per_block = own_heads // dp if striped else own_heads
    for k in range(own_heads):
        head = my_head * own_heads + k
        block = head // per_block
        owner = block % heads
        source = block // heads * per_block + head % per_block
        values = by_head[pl.ds(pl.multiple_of(owner * 8, 8), 8), :]
        total = jnp.where(lane == k, pltpu.roll(values, (k - source + LANE) % LANE, 1), total)
    head_out[...] = total


def collect(where, dp, heads, striped, taps_dev, table):
    outs = [jax.ShapeDtypeStruct(shape, F32) for shape in ((CONV_K, taps_dev), (1, taps_dev), (8, LANE))]
    window = -(-(taps_dev + LANE) // LANE) * LANE
    return call_kernel(
        functools.partial(collect_kernel, dp, heads, striped, taps_dev),
        where,
        (1,),
        (table,),
        [whole(table)],
        outs,
        [whole(o) for o in outs],
        "collect",
        scratch=[pltpu.VMEM((8, CONV_CH + window), F32), pltpu.VMEM((8 * heads, LANE), F32)],
    )


def ring_rows(arrived):
    found = []
    for distance, arrays in enumerate(arrived):
        first = 0
        for array in arrays:
            found.append((distance, first, array))
            first += array.shape[0]
    return found


def project_kernel(heads, dp, places, where, gain, *refs):
    count = len(places)
    chunks, pieces, (normed, out) = refs[:count], refs[count : count + dp], refs[-2:]
    rows_dev = normed.shape[0] // heads
    width = normed.shape[1]
    piece = width // dp

    @pl.when(pl.program_id(0) == 0)
    def _():
        for (distance, first), ref in zip(places, chunks):
            rows = ref.shape[0]
            values = ref[...].astype(F32)
            scale = lax.rsqrt(jnp.sum(values * values, axis=-1, keepdims=True) / width + EPS)
            to = pl.ds(pl.multiple_of(where[RING + distance] * rows_dev + first, rows), rows)
            for b in range(dp):
                at = pl.ds(pl.multiple_of(where[RING + heads + b] * piece, LANE), piece)
                low = (ref[:, at].astype(F32) * scale * gain[Small.NORM : Small.NORM + 1, at]).astype(BF)
                normed[to, b * piece : (b + 1) * piece] = low

    block = out.shape[0]
    mine = pl.ds(pl.multiple_of(pl.program_id(0) * block, block), block)
    cols = out.shape[1]
    total = mm(normed[mine, :piece], pieces[0][:, :cols])
    for b in range(1, dp):
        total = total + mm(normed[mine, b * piece : (b + 1) * piece], pieces[b][:, :cols])
    out[...] = total


def project(where, gain, arrived, pieces, cols):
    found = ring_rows(arrived)
    places, chunks = [f[:2] for f in found], [f[2] for f in found]
    heads, dp = len(arrived), len(pieces)
    length, width = heads * chunks[0].shape[0], chunks[0].shape[1]

    def body(*refs):
        project_kernel(heads, dp, places, *refs)

    normed = jax.ShapeDtypeStruct((length, width), BF)
    return call_kernel(
        body,
        where,
        (length // ROWS,),
        (gain, *chunks, *pieces),
        [once(a) for a in (gain, *chunks, *pieces)],
        [normed, jax.ShapeDtypeStruct((length, cols), F32)],
        [once(normed), rows_of(cols)],
        "project",
        flops=2 * length * width * cols,
    )


def gate_forward_kernel(dp, first, places, where, rows, scan, gain, *refs):
    in_pieces, out_pieces, (gate_out, w_full, *parts) = refs[:dp], refs[dp : 2 * dp], refs[2 * dp :]
    depth, each = in_pieces[0].shape[0], out_pieces[0].shape[0]
    first_col = in_pieces[0].shape[1] - scan.shape[1]

    @pl.when(pl.program_id(0) == 0)
    def _():
        for k in range(dp):
            w_full[pl.ds(pl.multiple_of(where[first + k] * each, each), each), :] = out_pieces[k][...]

    gate = mm(rows[:, :depth], in_pieces[0][:, first_col:])
    for k in range(1, dp):
        gate = gate + mm(rows[:, k * depth : (k + 1) * depth], in_pieces[k][:, first_col:])
    gate_out[...] = gate
    inner = scan[...].astype(F32) * (gate / (1.0 + jnp.exp(-gate)))
    branch = mm((inner * gain[Small.GATE : Small.GATE + 1, :]).astype(BF), w_full[...]).astype(BF)
    put_parts(where, branch, parts, places)


def part_places(heads, rows_dev, halves):
    places = []
    for distance in range(heads):
        count = 2 if distance in halves else 1
        places += [(distance, k * rows_dev // count, rows_dev // count) for k in range(count)]
    return places


def by_distance(places, parts):
    found = {}
    for (distance, _, _), part in zip(places, parts):
        found.setdefault(distance, []).append(part)
    return found


def put_parts(where, block, parts, places):
    size = block.shape[0]
    rows_dev = max(first + rows for _, first, rows in places)
    for (distance, first, rows), part in zip(places, parts):
        start = where[RING + distance] * rows_dev + first - pl.program_id(0) * size
        for at in range(0, size, rows):

            @pl.when(start == at)
            def _(part=part, at=at, rows=rows):
                part[...] = block[at : at + rows, :]


def gate_forward(where, heads, normed, scanned, gain, in_pieces, out_pieces):
    length, width = normed.shape
    own, cols = scanned.shape[1], out_pieces[0].shape[1]
    dp = len(in_pieces)
    full = jax.ShapeDtypeStruct((own, cols), BF)
    first = where.shape[0] - dp
    places = part_places(heads, length // heads, (heads // 2,))
    parts = [jax.ShapeDtypeStruct((rows, cols), BF) for _, _, rows in places]

    gate, full, *parts = call_kernel(
        functools.partial(gate_forward_kernel, dp, first, places),
        where,
        (length // ROWS,),
        (normed, scanned, gain, *in_pieces, *out_pieces),
        [rows_of(width), rows_of(own)] + [once(a) for a in (gain, *in_pieces, *out_pieces)],
        [jax.ShapeDtypeStruct((length, own), F32), full, *parts],
        [rows_of(own)] + [once(a) for a in (full, *parts)],
        "gate_forward",
        rest=10 * 2**20,
    )
    return gate, full, by_distance(places, parts)


def gate_sums_kernel(heads, places, where, w_full, scan, gate_in, gain, *refs):
    chunks, (cot, weighted_out, sums) = refs[: len(places)], refs[-3:]
    rows_dev = cot.shape[0] // heads
    block = scan.shape[0]

    @pl.when(pl.program_id(0) == 0)
    def _():
        for (distance, first), ref in zip(places, chunks):
            rows = ref.shape[0]
            to = pl.multiple_of(where[RING + distance] * rows_dev + first, rows)
            live = to + row_ids(rows) < where[SEQS - 1]
            values = ref[...]
            cot[pl.ds(to, rows), :] = jnp.where(live, values, jnp.zeros_like(values))

    mine = pl.ds(pl.multiple_of(pl.program_id(0) * block, block), block)
    weighted = mm(cot[mine, :], w_full[...], ((1,), (1,))) * gain[Small.GATE : Small.GATE + 1, :]
    weighted_out[...] = weighted
    gate = gate_in[...]
    inner = scan[...].astype(F32) * (gate / (1.0 + jnp.exp(-gate)))
    lane = lax.broadcasted_iota(jnp.int32, (1, LANE), 1)
    squares = jnp.sum(inner * inner, axis=1, keepdims=True)
    along = jnp.sum(inner * weighted, axis=1, keepdims=True)
    both = jnp.where(lane == 0, squares, jnp.where(lane == 1, along, 0.0))
    sums[...] = both.T[0:8, :]


def gate_sums(where, arrived, w_full, scanned, gate, gain):
    found = ring_rows(arrived)
    places, chunks = [f[:2] for f in found], [f[2] for f in found]
    own, cols = w_full.shape
    length = scanned.shape[0]
    heads = len(arrived)

    def body(*refs):
        gate_sums_kernel(heads, places, *refs)

    cot = jax.ShapeDtypeStruct((length, cols), BF)
    return call_kernel(
        body,
        where,
        (length // ROWS,),
        (w_full, scanned, gate, gain, *chunks),
        [once(w_full), rows_of(own), rows_of(own), once(gain)] + [once(c) for c in chunks],
        [cot, jax.ShapeDtypeStruct((length, own), F32), jax.ShapeDtypeStruct((8, length), F32)],
        [once(cot), rows_of(own), pl.BlockSpec((8, ROWS), lambda i, s: (0, i))],
        "gate_sums",
        flops=2 * length * own * cols,
    )


def gate_backward_kernel(scalars, sums, weighted, scan, gate_in, gain, scan_out, gate_out, gated):
    columns = sums[...].T
    ratio = lax.rsqrt(columns[:, 0:1] / DI + EPS)
    pull = ratio * ratio * ratio * columns[:, 1:2] / DI
    gate = gate_in[...]
    sig = 1.0 / (1.0 + jnp.exp(-gate))
    act = gate * sig
    scanned = scan[...].astype(F32)
    inner = scanned * act
    grad = ratio * weighted[...] - pull * inner
    scan_out[...] = (grad * act).astype(BF)
    gate_out[...] = (grad * scanned * (sig * (1.0 + gate * (1.0 - sig)))).astype(BF)
    gated[...] = (ratio * inner * gain[Small.GATE : Small.GATE + 1, :]).astype(BF)


def gate_backward(where, sums, weighted, scanned, gate, gain):
    length, own = scanned.shape
    return call_kernel(
        gate_backward_kernel,
        where,
        (length // ROWS,),
        (sums, weighted, scanned, gate, gain),
        [pl.BlockSpec((8, ROWS), lambda i, s: (0, i))] + [rows_of(own)] * 3 + [whole(gain)],
        [jax.ShapeDtypeStruct((length, own), BF)] * 3,
        [rows_of(own)] * 3,
        "gate_backward",
    )


def project_back_kernel(dp, places, where, gate_rows, mix_rows, *refs):
    pieces, parts, out = refs[:dp], refs[dp:-1], refs[-1]
    depth = pieces[0].shape[0]
    cols = mix_rows.shape[1]
    for k in range(dp):
        total = mm(mix_rows[...], pieces[k][:, :cols], ((1,), (1,)))
        total = total + mm(gate_rows[...], pieces[k][:, cols:], ((1,), (1,)))
        out[:, k * depth : (k + 1) * depth] = total.astype(BF)
    put_parts(where, out, parts, places)


def project_back(where, heads, grad_gate, grad_mix, pieces):
    length, own = grad_gate.shape
    cols = grad_mix.shape[1]
    dp = len(pieces)
    width = dp * pieces[0].shape[0]
    places = part_places(heads, length // heads, range(heads))
    parts = [jax.ShapeDtypeStruct((rows, width), BF) for _, _, rows in places]
    parts = call_kernel(
        functools.partial(project_back_kernel, dp, places),
        where,
        (length // ROWS,),
        (grad_gate, grad_mix, *pieces),
        [rows_of(own), rows_of(cols)] + [once(p) for p in pieces],
        parts,
        [once(p) for p in parts],
        "project_back",
        scratch=[pltpu.VMEM((ROWS, width), BF)],
        rest=10 * 2**20,
    )
    return by_distance(places, parts)


def input_grad_kernel(dp, first, where, *refs):
    parts, (hidden, cot, gain, out, total) = refs[:-5], refs[-5:]
    rows, width = parts[0].shape
    piece = width // dp
    for k in range(2):
        at = slice(k * rows, (k + 1) * rows)
        own, ahead, behind = parts[3 * k : 3 * k + 3]
        grad = own[...].astype(F32) + ahead[...].astype(F32) + behind[...].astype(F32)
        for b in range(dp):
            to = pl.ds(pl.multiple_of(where[first + b] * piece, LANE), piece)
            total[at, to] = grad[:, b * piece : (b + 1) * piece]
    values = hidden[...].astype(F32)
    scale = lax.rsqrt(jnp.sum(values * values, axis=-1, keepdims=True) / width + EPS)
    grad = total[...] * gain[Small.NORM : Small.NORM + 1, :]
    along = jnp.sum(values * grad, axis=-1, keepdims=True) / width
    out[...] = cot[...].astype(F32) + scale * (grad - values * (scale * scale * along))


def input_grad_of(where, dp, parts, hidden, cot, gain):
    first = where.shape[0] - dp
    ins = (*parts, hidden, cot, gain)
    return call_kernel(
        functools.partial(input_grad_kernel, dp, first),
        where,
        (1,),
        ins,
        [once(a) for a in ins],
        [jax.ShapeDtypeStruct(hidden.shape, F32)],
        [once(hidden)],
        "input_grad",
        scratch=[pltpu.VMEM(hidden.shape, F32)],
    )[0]


def output_kernel(where, sums, hidden, own, ahead, behind, out):
    rows = hidden.shape[0]
    branch = own[...].astype(F32) + ahead[...].astype(F32) + behind[...].astype(F32)
    live = where[RING] * rows + row_ids(rows) < where[SEQS - 1]
    ratio = jnp.where(live, lax.rsqrt(sums[...].T[:, 0:1] / DI + EPS), 0.0)
    out[...] = (hidden[...].astype(F32) + ratio * branch).astype(BF)


def output_of(where, sums, hidden, parts):
    rows = hidden.shape[0]
    return call_kernel(
        output_kernel,
        where,
        (1,),
        (sums, hidden, *parts),
        [pl.BlockSpec((8, rows), lambda i, s: (0, s[RING]))] + [once(a) for a in (hidden, *parts)],
        [jax.ShapeDtypeStruct(hidden.shape, BF)],
        [once(hidden)],
        "output",
    )[0]


def out_grad_kernel(arrived, kept, w_out, out, sums):
    total = arrived[...].astype(F32) + kept[...]
    out[...] = total
    sums[...] = jnp.sum(total * w_out[...].astype(F32), axis=1, keepdims=True) + jnp.zeros(sums.shape, F32)


def out_grad_of(arrived, kept, w_out):
    outs = [jax.ShapeDtypeStruct(w_out.shape, F32), jax.ShapeDtypeStruct((w_out.shape[0], LANE), F32)]
    return call_whole(out_grad_kernel, (arrived, kept, w_out), outs, "out_grad", rest=4 * 2**20)


def weight_rows_kernel(dp, striped, gate_cols, mix_cols, w_in, out, norm_out):
    heads, rows, own = gate_cols.shape
    own_heads = own // P_SIZE
    chans = own + 2 * N
    norm = jnp.zeros((rows, 1), F32)

    def put(first, values):
        nonlocal norm
        at = slice(first, first + values.shape[1])
        out[:, at] = values
        norm = norm + jnp.sum(values * w_in[:, at].astype(F32), axis=1, keepdims=True)

    shared = mix_cols[0, :, own:chans].astype(F32)
    for head in range(1, heads):
        shared = shared + mix_cols[head, :, own:chans].astype(F32)
    put(2 * DI, shared)
    steps = jnp.zeros((rows, heads * own_heads), F32)
    source = lax.broadcasted_iota(jnp.int32, (LANE, heads * own_heads), 0)
    target = lax.broadcasted_iota(jnp.int32, (LANE, heads * own_heads), 1)
    count = dp if striped else 1
    for head in range(heads):
        for block in range(count):
            size = own // count
            at = slice(block * size, (block + 1) * size)
            put((block * heads + head) * size, gate_cols[head, :, at].astype(F32))
            put(DI + (block * heads + head) * size, mix_cols[head, :, at].astype(F32))
        each = own_heads // count
        to = (source // each * heads + head) * each + source % each
        picked = ((to == target) & (source < own_heads)).astype(F32).astype(BF)
        steps = steps + mm(mix_cols[head, :, chans:], picked)
    put(DI + CONV_CH, steps)
    norm_out[...] = norm + jnp.zeros(norm_out.shape, F32)


def weight_rows(dp, striped, gate_cols, mix_cols, w_in):
    rows = w_in.shape[0]
    ins = (gate_cols, mix_cols, w_in)

    def body(*refs):
        weight_rows_kernel(dp, striped, *refs)

    return pl.pallas_call(
        body,
        out_shape=[jax.ShapeDtypeStruct(w_in.shape, F32), jax.ShapeDtypeStruct((rows, LANE), F32)],
        compiler_params=pltpu.CompilerParams(vmem_limit_bytes=SCAN_VMEM),
        cost_estimate=NO_COST,
        name="weight_rows",
    )(*ins)


FAR = -1e30


def mm(left, right, contract=((1,), (0,))):
    return lax.dot_general(left, right, (contract, ((), ())), preferred_element_type=F32)


def row_ids(rows):
    return lax.broadcasted_iota(jnp.int32, (rows, 1), 0)


def split_sum(ones, values, count):
    parts, rest = [], values
    for _ in range(count):
        part = rest.astype(BF)
        parts.append(part)
        rest = rest - part.astype(F32)
    product = mm(ones, jnp.concatenate(parts, axis=1))
    width = values.shape[1]
    total = product[:, :width]
    for k in range(1, count):
        total = total + product[:, k * width : (k + 1) * width]
    return total


def split_times(values, ones, count):
    total, rest = jnp.zeros((values.shape[0], ones.shape[1]), F32), values
    for _ in range(count):
        part = rest.astype(BF)
        total = total + mm(part, ones)
        rest = rest - part.astype(F32)
    return total


def widen(values, spread2):
    high = values.astype(BF)
    low = (values - high.astype(F32)).astype(BF)
    return mm(jnp.concatenate([high, low], axis=1), spread2)


def segment_at(position, ends_ref):
    seg = jnp.zeros_like(position)
    start = jnp.zeros_like(position)
    for k in range(SEQS):
        end = ends_ref[k]
        seg = seg + (position >= end).astype(jnp.int32)
        start = jnp.where(position >= end, end, start)
    return seg, start


def scalar_segment(position, ends_ref):
    seg = jnp.int32(0)
    for k in range(SEQS):
        seg = seg + (position >= ends_ref[k]).astype(jnp.int32)
    return jnp.where(position < 0, -1, seg)


class Block:
    def __init__(self, index, ends_ref, dt_part, head_ref, own):
        rows = BLOCK_LEN
        first = index * rows
        seg, self.start = segment_at(first + row_ids(rows), ends_ref)
        self.position = first + row_ids(rows)
        col = lax.broadcasted_iota(jnp.int32, (1, rows), 1)
        seg_row, _ = segment_at(first + col, ends_ref)
        causal = row_ids(rows) >= col
        self.lower = jnp.where(causal, 1.0, 0.0).astype(BF)
        same = seg == seg_row
        self.penalty = jnp.where(causal & same, 0.0, FAR)
        before = scalar_segment(first - 1, ends_ref)
        last = scalar_segment(first + rows - 1, ends_ref)
        self.raw = dt_part.astype(BF).astype(F32) + head_ref[0:1, :]
        self.decay = head_ref[1:2, :]
        self.dt = jnp.maximum(self.raw, 0.0) + jnp.log1p(jnp.exp(-jnp.abs(self.raw)))
        self.cum = split_sum(self.lower, self.dt * self.decay, 3)
        final = self.cum[rows - 1 : rows, :]
        self.enter = jnp.where(seg == before, jnp.exp(self.cum), 0.0)
        self.tail = jnp.where(seg == last, jnp.exp(final - self.cum), 0.0)
        self.keep = jnp.where(before == last, jnp.exp(final), 0.0)
        head_of = lax.broadcasted_iota(jnp.int32, (LANE, own), 1) // P_SIZE
        self.spread = (head_of == lax.broadcasted_iota(jnp.int32, (LANE, own), 0)).astype(F32).astype(BF)
        spread2 = jnp.concatenate([self.spread, self.spread], axis=0)
        self.dt_wide = widen(self.dt, spread2)
        self.enter_wide = widen(self.enter, spread2)
        self.tail_wide = widen(self.tail, spread2)
        self.cum_row = self.cum.T
        chan_head = lax.broadcasted_iota(jnp.int32, (own, LANE), 0) // P_SIZE
        self.gather = (chan_head == lax.broadcasted_iota(jnp.int32, (own, LANE), 1)).astype(F32)
        self.keep_chan = jnp.sum(self.gather * self.keep, axis=1, keepdims=True)

    def gap(self, head):
        return self.cum[:, head : head + 1] - self.cum_row[head : head + 1, :]


def scan_forward_kernel(ends_ref, mix_ref, taps_ref, head_ref, skip_ref, state_in, rim_in, *refs, base):
    pre_ref, scan_ref, enter_ref, state, rim, ext = refs[-6:]
    index = base + pl.program_id(0)
    chans = pre_ref.shape[1]
    own = chans - 2 * N
    rows = BLOCK_LEN

    @pl.when(pl.program_id(0) == 0)
    def _():
        rim[...] = rim_in[...]
        state[...] = state_in[...]

    ext[0:8, :] = rim[...]
    ext[8:, :] = mix_ref[:, :chans]
    blk = Block(index, ends_ref, mix_ref[:, chans:], head_ref, own)
    total = taps_ref[CONV_K : CONV_K + 1, :] + taps_ref[CONV_K - 1 : CONV_K, :] * ext[8:, :]
    for lag in range(1, CONV_K):
        linked = (blk.position - lag >= blk.start).astype(F32)
        tap = taps_ref[CONV_K - 1 - lag : CONV_K - lag, :]
        total = total + tap * (linked * ext[8 - lag : 8 - lag + rows, :])
    rim[...] = ext[rows : rows + 8, :]
    pre_ref[...] = total
    low = (total / (1.0 + jnp.exp(-total))).astype(BF)
    x_low, b_low, c_low = low[:, :own], low[:, own : own + N], low[:, own + N :]
    x_wide = x_low.astype(F32)
    x_dt = (x_wide * blk.dt_wide).astype(BF)
    scores = mm(c_low, b_low, ((1,), (1,)))
    lane = lax.broadcasted_iota(jnp.int32, (1, LANE), 1)
    entering = state[...]
    enter_ref[...] = entering
    outer = mm(c_low, entering.astype(BF), ((1,), (1,))) * blk.enter_wide + skip_ref[Small.HEADS : Small.HEADS + 1, :] * x_wide
    for pair in range(own // LANE):
        both = x_dt[:, pair * LANE : (pair + 1) * LANE]
        parts = []
        for head in (2 * pair, 2 * pair + 1):
            mixing = scores * jnp.exp(blk.gap(head) + blk.penalty)
            parts.append(mm(mixing.astype(BF), both))
        inner = jnp.where(lane < P_SIZE, parts[0], parts[1])
        at = slice(pair * LANE, (pair + 1) * LANE)
        scan_ref[:, at] = (inner + outer[:, at]).astype(BF)
    added = mm((x_wide * blk.dt_wide * blk.tail_wide).astype(BF), b_low, ((0,), (0,)))
    state[...] = blk.keep_chan * entering + added


def scan_forward(ends, mix, taps, head_rows, skip_row, calls):
    length, cols = mix.shape
    chans = cols - LANE
    own = chans - 2 * N
    blocks = length // BLOCK_LEN
    each = blocks // calls
    state, rim, kept = jnp.zeros((own, N), F32), jnp.zeros((8, chans), F32), ()
    for call in range(calls):

        def rows_of(width, base=call * each, rows=BLOCK_LEN):
            return pl.BlockSpec((rows, width), lambda i, ends: (base + i, 0))

        def whole(array):
            return pl.BlockSpec(array.shape, lambda i, ends: (0, 0))

        *kept, state, rim = pl.pallas_call(
            functools.partial(scan_forward_kernel, base=call * each),
            grid_spec=pltpu.PrefetchScalarGridSpec(
                num_scalar_prefetch=1,
                grid=(each,),
                in_specs=[rows_of(cols)]
                + [whole(a) for a in (taps, head_rows, skip_row, state, rim)]
                + [pl.BlockSpec(memory_space=pl.ANY)] * len(kept),
                out_specs=[rows_of(chans), rows_of(own), rows_of(N, rows=own), whole(state), whole(rim)],
                scratch_shapes=[pltpu.VMEM((BLOCK_LEN + 8, chans), F32)],
            ),
            out_shape=[
                jax.ShapeDtypeStruct((length, chans), F32),
                jax.ShapeDtypeStruct((length, own), BF),
                jax.ShapeDtypeStruct((blocks * own, N), F32),
                jax.ShapeDtypeStruct(state.shape, F32),
                jax.ShapeDtypeStruct(rim.shape, F32),
            ],
            input_output_aliases={7 + k: k for k in range(len(kept))},
            compiler_params=pltpu.CompilerParams(vmem_limit_bytes=SCAN_VMEM),
            cost_estimate=NO_COST,
            name="scan_forward",
        )(ends, mix, taps, head_rows, skip_row, state, rim, *kept)
    return kept


def scan_backward_kernel(
    ends_ref, pre_ref, mix_ref, dy_ref, enter_ref, taps_ref, head_ref, skip_ref, *refs, base
):
    carried, (grad_ref, *carries, ext) = refs[:3], refs[-5:]
    state, rim, small_ref = carries
    index = base - pl.program_id(0)
    chans = pre_ref.shape[1]
    own = chans - 2 * N
    rows = BLOCK_LEN

    @pl.when(pl.program_id(0) == 0)
    def _():
        for given, held in zip(carried, carries):
            held[...] = given[...]

    ext[rows:, :] = rim[...]
    blk = Block(index, ends_ref, mix_ref[:, chans:], head_ref, own)
    pre = pre_ref[...]
    sig = 1.0 / (1.0 + jnp.exp(-pre))
    low = (pre * sig).astype(BF)
    x_low, b_low, c_low = low[:, :own], low[:, own : own + N], low[:, own + N :]
    x_wide = x_low.astype(F32)
    dy = dy_ref[...]
    dy_wide = dy.astype(F32)
    x_dt = (x_wide * blk.dt_wide).astype(BF)
    entering = enter_ref[...]
    enter_low = entering.astype(BF)
    leaving = state[...]
    leaving_low = leaving.astype(BF)
    gather = blk.gather.astype(BF)

    scores = mm(c_low, b_low, ((1,), (1,)))
    scores_t = mm(b_low, c_low, ((1,), (1,)))
    penalty_t = blk.penalty.T
    lane = lax.broadcasted_iota(jnp.int32, (1, LANE), 1)
    lane_rows = lax.broadcasted_iota(jnp.int32, (rows, LANE), 1)
    sub_rows = lax.broadcasted_iota(jnp.int32, (LANE, rows), 0)
    grad_scores = jnp.zeros((rows, rows), F32)
    along_rows = jnp.zeros((rows, LANE), F32)
    along_cols = jnp.zeros((LANE, rows), F32)
    grad_xdt = []
    for pair in range(own // LANE):
        at = slice(pair * LANE, (pair + 1) * LANE)
        both, dy_both = x_dt[:, at], dy[:, at]
        parts = []
        for head in (2 * pair, 2 * pair + 1):
            gap = blk.gap(head)
            decay = jnp.exp(gap + blk.penalty)
            mixing_t = scores_t * jnp.exp(penalty_t - gap)
            parts.append(mm(mixing_t.astype(BF), dy_both))
            mine = (lane < P_SIZE) if head % 2 == 0 else (lane >= P_SIZE)
            dy_one = jnp.where(mine, dy_both, jnp.zeros_like(dy_both))
            grad_mixing = mm(dy_one, both, ((1,), (1,))) * decay
            grad_scores = grad_scores + grad_mixing
            moved = grad_mixing * scores
            along_rows = along_rows + jnp.where(lane_rows == head, jnp.sum(moved, axis=1, keepdims=True), 0.0)
            along_cols = along_cols + jnp.where(sub_rows == head, jnp.sum(moved, axis=0, keepdims=True), 0.0)
        grad_xdt.append(jnp.where(lane < P_SIZE, parts[0], parts[1]))
    grad_xdt = jnp.concatenate(grad_xdt, axis=1)
    grad_cum = along_rows - along_cols.T
    grad_low = grad_scores.astype(BF)
    grad_c = mm(grad_low, b_low)
    grad_b = mm(grad_low, c_low, ((0,), (0,)))

    dy_enter = dy_wide * blk.enter_wide
    dy_enter_low = dy_enter.astype(BF)
    seen = mm(c_low, enter_low, ((1,), (1,)))
    grad_cum = grad_cum + mm((dy_enter * seen).astype(BF), gather)
    grad_c = grad_c + mm(dy_enter_low, enter_low)
    grad_enter = mm(dy_enter_low, c_low, ((0,), (0,)))

    taken = mm(b_low, leaving_low, ((1,), (1,)))
    x_tail = x_wide * blk.tail_wide
    grad_tail = mm((x_tail * taken).astype(BF), gather)
    moved = grad_tail * blk.dt
    grad_b = grad_b + mm((x_tail * blk.dt_wide).astype(BF), leaving_low)
    kept = jnp.sum(leaving * entering, axis=1, keepdims=True) * blk.keep_chan
    grad_last = jnp.sum(moved, axis=0, keepdims=True) + jnp.sum(blk.gather * kept, axis=0, keepdims=True)
    grad_cum = grad_cum - moved + jnp.where(row_ids(rows) == rows - 1, grad_last, 0.0)
    state[...] = blk.keep_chan * leaving + grad_enter

    grad_dt = mm((x_wide * grad_xdt).astype(BF), gather) + grad_tail
    upper = (row_ids(rows) <= lax.broadcasted_iota(jnp.int32, (1, rows), 1)).astype(F32).astype(BF)
    grad_steps = split_sum(upper, grad_cum, 3)
    grad_dt = grad_dt + blk.decay * grad_steps
    grad_raw = grad_dt / (1.0 + jnp.exp(-blk.raw))
    small_ref[Small.BIAS_GRAD : Small.BIAS_GRAD + 1, :LANE] += jnp.sum(grad_raw, axis=0, keepdims=True)
    small_ref[Small.LOG_GRAD : Small.LOG_GRAD + 1, :LANE] += (
        jnp.sum(blk.dt * grad_steps, axis=0, keepdims=True) * blk.decay
    )
    small_ref[Small.SKIP_GRAD : Small.SKIP_GRAD + 1, :own] += jnp.sum(dy_wide * x_wide, axis=0, keepdims=True)

    grad_x = blk.dt_wide * (grad_xdt + blk.tail_wide * taken) + skip_ref[Small.HEADS : Small.HEADS + 1, :] * dy_wide
    grad_low = jnp.concatenate([grad_x.astype(BF).astype(F32), grad_b, grad_c], axis=1)
    grad_pre = grad_low * (sig * (1.0 + pre * (1.0 - sig)))
    ext[0:rows, :] = grad_pre
    conv_in = mix_ref[:, :chans]
    small_ref[Small.BIAS : Small.BIAS + 1, :] += jnp.sum(grad_pre, axis=0, keepdims=True)
    grad_in = jnp.zeros((rows, chans), F32)
    for lag in range(CONV_K):
        back = grad_pre if lag == 0 else ext[lag : lag + rows, :]
        if lag:
            _, start = segment_at(blk.position + lag, ends_ref)
            back = back * (blk.position >= start).astype(F32)
        tap = CONV_K - 1 - lag
        grad_in = grad_in + taps_ref[tap : tap + 1, :] * back
        small_ref[tap : tap + 1, :] += jnp.sum(conv_in * back, axis=0, keepdims=True)
    rim[...] = grad_pre[0:8, :]
    grad_ref[...] = jnp.concatenate([grad_in.astype(BF), grad_raw.astype(BF)], axis=1)


def scan_backward(ends, pre, mix, grad_scan, entering, taps, head_rows, skip_row, carries, grad, call, calls):
    length, cols = mix.shape
    chans = cols - LANE
    own = chans - 2 * N
    blocks = length // BLOCK_LEN
    each = blocks // calls
    last = blocks - 1 - call * each
    if call == 0:
        carries = [jnp.zeros(s, F32) for s in ((own, N), (8, chans), (8, chans))]
    held = () if call == 0 else (grad,)

    def rows_of(width, rows=BLOCK_LEN):
        return pl.BlockSpec((rows, width), lambda i, ends: (last - i, 0))

    def whole(array):
        return pl.BlockSpec(array.shape, lambda i, ends: (0, 0))

    grad, *carries = pl.pallas_call(
        functools.partial(scan_backward_kernel, base=last),
        grid_spec=pltpu.PrefetchScalarGridSpec(
            num_scalar_prefetch=1,
            grid=(each,),
            in_specs=[rows_of(chans), rows_of(cols), rows_of(own), rows_of(N, rows=own)]
            + [whole(a) for a in (taps, head_rows, skip_row, *carries)]
            + [pl.BlockSpec(memory_space=pl.ANY)] * len(held),
            out_specs=[rows_of(cols)] + [whole(a) for a in carries],
            scratch_shapes=[pltpu.VMEM((BLOCK_LEN + 8, chans), F32)],
        ),
        out_shape=[jax.ShapeDtypeStruct((length, cols), BF)]
        + [jax.ShapeDtypeStruct(a.shape, F32) for a in carries],
        input_output_aliases={11: 0} if held else {},
        compiler_params=pltpu.CompilerParams(vmem_limit_bytes=SCAN_VMEM),
        cost_estimate=NO_COST,
        name="scan_backward",
    )(ends, pre, mix, grad_scan, entering, taps, head_rows, skip_row, *carries, *held)
    return grad, carries


def shards(
    hidden, seq_lens, norm_w, w_in, conv_w, conv_b, dt_bias, a_log, skip_gain, gate_w, w_out, cotangent
):
    dp, heads = lax.axis_size("dp"), lax.axis_size("heads")
    my_dp, my_head = lax.axis_index("dp"), lax.axis_index("heads")
    me = my_dp * heads + my_head
    rows_dev, width = hidden.shape
    length = rows_dev * heads
    w_rows = w_in.shape[0]
    out_rows = w_out.shape[0]
    own = DI // heads
    own_heads = own // P_SIZE
    chans = own + 2 * N
    taps_dev = conv_b.shape[0]
    ends = jnp.cumsum(seq_lens[0]).astype(jnp.int32)
    where = where_vector(ends)
    owners = [where[RING + heads + k] for k in range(dp)]
    striped = out_rows % P_SIZE == 0
    per_block = own_heads // dp if striped else 0

    def split_own(array, size):
        rows = array.shape[0]
        if striped:
            cut = array.reshape(rows, dp, heads, per_block * size).transpose(2, 0, 1, 3)
        else:
            cut = array.reshape(rows, heads, own_heads * size).transpose(1, 0, 2)
        return cut.reshape(heads, rows, own_heads * size)

    pad = LANE - own_heads
    w_cut = jnp.concatenate(
        [
            split_own(w_in[:, DI : 2 * DI], P_SIZE),
            jnp.broadcast_to(w_in[None, :, 2 * DI : DI + CONV_CH], (heads, w_rows, 2 * N)),
            split_own(w_in[:, DI + CONV_CH :], 1),
            jnp.zeros((heads, w_rows, pad), BF),
            split_own(w_in[:, :DI], P_SIZE),
        ],
        axis=2,
    )

    def to_heads(cut):
        return lax.all_to_all(cut, "heads", split_axis=0, concat_axis=0, tiled=True)

    line = Line()
    small = pack_small(conv_w, conv_b, norm_w, gate_w, dt_bias, a_log, skip_gain)
    for bits in powers("dp"):
        small = doubled(small, "dp", bits)
    hidden_ring = GatherRing(hidden, "heads")
    steps = hidden_ring.half
    w_own = to_heads(w_cut)
    route = [(q, (q % dp) * heads + q // dp) for q in range(dp * heads)]
    out_gather = GatherDp(w_out if striped else lax.ppermute(w_out, ("dp", "heads"), route))
    for step in range(1, steps):
        if step == 1:
            w_own, small, *arrived = hidden_ring.advance(line, w_own, small, *out_gather.moving)
            in_gather = GatherDp(w_own.reshape(heads * w_rows, -1))
            out_gather.relay(line, arrived)
            small = to_heads(jnp.broadcast_to(small[None], (heads,) + small.shape))
        elif step == 3:
            small, *arrived = hidden_ring.advance(line, small, *in_gather.moving)
            in_gather.relay(line, arrived)
        else:
            hidden_ring.advance(line)
    cot_ring = GatherRing(line.take(cotangent), "heads")
    taps, gate_gain, norm_row, head_rows, skip_row = unpack(
        where, dp, heads, striped, own, width, (taps_dev, w_rows, out_rows), line.take(small.reshape(heads * dp * 8, -1))
    )
    line.mark(taps)
    arrived = hidden_ring.advance(line, *in_gather.far, *out_gather.far)
    in_pieces, out_pieces = in_gather.all(arrived[: dp // 2]), out_gather.all(arrived[dp // 2 :])

    normed, mix = project(where, norm_row, hidden_ring.all(), in_pieces, chans + LANE)
    line.mark(mix)
    cot_ring.advance(line)
    pre, scanned, entering = scan_forward(ends, line.take(mix), taps, head_rows, skip_row, 1)
    line.mark(scanned)
    cot_ring.advance(line)
    gate, w_full, branch = gate_forward(
        where, heads, normed, line.take(scanned), gate_gain, in_pieces, out_pieces
    )
    line.mark(gate)
    for step in range(3, steps):
        cot_ring.advance(line)

    branch_ring = ScatterRing(branch, "heads")
    cot_ring.advance(line)
    cot_live, weighted, sums = gate_sums(where, cot_ring.all(), line.take(w_full), scanned, gate, gate_gain)
    line.mark(sums)
    sums_pair = lax.ppermute(sums, "heads", xor_route(heads, 1))
    sums = sums + line.take(sums_pair)
    sums_peers = [lax.ppermute(sums, "heads", xor_route(heads, bits)) for bits in range(2, heads, 2)]
    branch_ring.advance(line)
    for other in line.take(*sums_peers):
        sums = sums + other
    grad_scan, grad_gate, gated = gate_backward(where, sums, weighted, scanned, gate, gate_gain)
    line.mark(grad_gate)
    branch_ring.advance(line)
    piece = width // dp
    in_term = functools.partial(weight_term, where, normed, block=piece // 2, steps=2 * dp, column=lambda i, s: i)
    gate_scatter = ScatterDp(*in_term(line.take(grad_gate)))
    line.mark(gate_scatter.kept)

    carries, grad_mix = None, ()
    calls = 2
    for call in range(calls):
        grad_mix, carries = scan_backward(
            ends, pre, mix, line.take(grad_scan), entering, taps, head_rows, skip_row, carries, grad_mix, call, calls
        )
        line.mark(carries[0])
        if call == 0:
            gate_scatter.relay(line, branch_ring.advance(line, *gate_scatter.moving))
    small_grads = carries[2]
    small_core = other_core(small_grads)
    while branch_ring.left > 1:
        branch_ring.advance(line)
    arrived = branch_ring.advance(line, *gate_scatter.moving)
    gate_cols = to_heads(gate_scatter.all(arrived, BF).reshape(heads, w_rows, own))
    mix_scatter = ScatterDp(*in_term(line.take(grad_mix)))
    line.mark(mix_scatter.kept)
    small_grads = small_grads + line.take(small_core)
    small_moving = [lax.ppermute(small_grads, "dp", xor_route(dp, bits)) for bits in range(2, dp, 2)]
    parts = project_back(where, heads, line.take(grad_gate), grad_mix, in_pieces)
    line.mark(parts[0][0])

    grad_ring = ScatterRings(parts, "heads")
    mix_scatter.relay(line, [line.take(*mix_scatter.moving)])
    for step in range(1, steps):
        if step == 1:
            arrived = grad_ring.advance(line, *small_moving)
            small_grads = sum(arrived, small_grads)
            small_all = to_heads(jnp.broadcast_to(small_grads[None], (heads,) + small_grads.shape))
            if striped:
                out_scatter = ScatterDp(
                    *weight_term(
                        where, line.take(gated), cot_live, out_rows, dp, lambda i, s: s[RING + heads + i]
                    )
                )
            else:
                term = mm(line.take(gated), cot_live, ((0,), (0,))).astype(BF)
                cuts = [lax.dynamic_slice(term, (o * out_rows, 0), (out_rows, width)) for o in owners]
                out_scatter = ScatterDp(jnp.concatenate(cuts[: dp // 2]), jnp.concatenate(cuts[dp // 2 :]))
            line.mark(out_scatter.kept)
        elif step == 2:
            n_out = len(out_scatter.moving)
            arrived = grad_ring.advance(line, *out_scatter.moving, *mix_scatter.moving)
            out_scatter.relay(line, arrived[:n_out])
            mix_cols = to_heads(mix_scatter.all(arrived[n_out:], BF).reshape(heads, w_rows, -1))
        elif step == 3:
            (gate_cols,) = grad_ring.advance(line, gate_cols)
            output = output_of(where, sums, hidden, (*branch[0], *branch_ring.sums))
            line.mark(output)
        else:
            grad_ring.advance(line)
    small_all, *arrived = grad_ring.advance(line, small_all, *out_scatter.moving)
    own_parts = [part for k in range(2) for part in (parts[0][k], *grad_ring.sums[k])]
    input_grad = input_grad_of(where, dp, own_parts, hidden, cotangent, norm_row)
    if not arrived:
        arrived = [jnp.zeros(w_out.shape, BF)]
    if striped:
        w_out_grad, out_sums = out_grad_of(arrived[0], out_scatter.sums[0], w_out)
    else:
        w_out_grad = add_last(arrived[0], out_scatter.sums[0], F32)
        w_out_grad = lax.ppermute(w_out_grad, ("dp", "heads"), [(dst, src) for src, dst in route])
        out_sums = jnp.sum(w_out.astype(F32) * w_out_grad, axis=1, keepdims=True)
    gate_w_grad = out_sums[:, 0] / gate_w.astype(F32)
    line.mark(input_grad)
    w_in_grad, norm_sums = weight_rows(dp, striped, *line.take(gate_cols, mix_cols), w_in)
    norm_w_grad = norm_sums[:, 0] / norm_w.astype(F32)

    taps_grad, bias_grad, by_head = collect(where, dp, heads, striped, taps_dev, small_all.reshape(heads * 8, -1))
    return (
        output,
        input_grad,
        norm_w_grad,
        w_in_grad,
        taps_grad,
        bias_grad.reshape(-1),
        by_head[Small.BIAS_GRAD, :own_heads],
        by_head[Small.LOG_GRAD, :own_heads],
        by_head[Small.SKIP_GRAD, :own_heads],
        gate_w_grad,
        w_out_grad,
    )


def solution(mesh):
    both = ("dp", "heads")
    placed = (
        P(both, None),
        P("dp", None),
        P(both),
        P(both, None),
        P(None, both),
        P(both),
        P("heads"),
        P("heads"),
        P("heads"),
        P(both),
        P(both, None),
        P(both, None),
    )
    return jax.shard_map(
        shards,
        mesh=mesh,
        in_specs=placed,
        out_specs=(
            P(both, None),
            P(both, None),
            P(both),
            P(both, None),
            P(None, both),
            P(both),
            P("heads"),
            P("heads"),
            P("heads"),
            P(both),
            P(both, None),
        ),
        check_vma=False,
    )
```

```python
import functools

import numpy as np

import jax
import jax.numpy as jnp
from jax import lax
from jax.experimental import pallas as pl
from jax.experimental.pallas import tpu as pltpu
from jax.sharding import PartitionSpec as P

P_SIZE = 64
N = 128
CONV_K = 4
BLOCK_LEN = 256
SEQS = 3
DI = 4096
CONV_CH = 4352
LANE = 128
EPS = 1e-05
ROWS = 512
RING = SEQS
SCAN_VMEM = 20 * 2**20

NO_COST = pl.CostEstimate(flops=0, bytes_accessed=0, transcendentals=0)
BF = jnp.bfloat16
F32 = jnp.float32


def ring_order(n):
    return list(range(0, n, 2)) + list(range(n - 1, 0, -2))


def where_vector(ends):
    heads, dp = lax.axis_size("heads"), lax.axis_size("dp")
    order = ring_order(heads)
    ring = np.zeros((heads, heads), np.int32)
    for position, index in enumerate(order):
        ring[index] = [order[(position + distance) % heads] for distance in range(heads)]
    owners = np.array([dp_owners(dp, me) for me in range(dp)], np.int32)
    return jnp.concatenate(
        [ends, jnp.asarray(ring)[lax.axis_index("heads")], jnp.asarray(owners)[lax.axis_index("dp")]]
    )


def ring_route(n, step):
    order = ring_order(n)
    return [(order[i], order[(i + step) % n]) for i in range(n)]


def xor_route(n, bits):
    return [(i, i ^ bits) for i in range(n)]


def together(*values):
    return list(lax.optimization_barrier(values))


def together_with(moving, others):
    values = together(*moving.values(), *others)
    return dict(zip(moving, values)), values[len(moving) :]


class GatherRing:
    def __init__(self, rows, axis):
        self.axis, self.n = axis, lax.axis_size(axis)
        self.half = self.n // 2
        self.step = 0
        self.arrived = {0: [rows]}
        self.moving = {way: self.sent(rows, way) for way in (1, -1)}

    def sent(self, value, way):
        return lax.ppermute(value, self.axis, ring_route(self.n, way))

    def advance(self, *others):
        self.step += 1
        moving, others = together_with(self.moving, others)
        self.moving = {}
        if self.step == self.half:
            self.arrived[self.half] = [moving[1], moving[-1]]
            return others
        for way, value in moving.items():
            self.arrived[-way * self.step % self.n] = [value]
        if self.step == self.half - 1:
            moving = dict(zip((1, -1), halves(moving[1], moving[-1])))
        for way, value in moving.items():
            self.moving[way] = self.sent(value, way)
        return others

    def all(self):
        return [self.arrived[d] for d in range(self.n)]


class ScatterRing:
    def __init__(self, parts, axis):
        self.axis, self.n = axis, lax.axis_size(axis)
        self.half = self.n // 2
        self.parts = parts
        self.left = self.half
        self.moving = {1: self.sent(parts[self.half][0], 1), -1: self.sent(parts[self.half][1], -1)}

    def sent(self, value, way):
        return lax.ppermute(value, self.axis, ring_route(self.n, way))

    def advance(self, *others):
        self.left -= 1
        moving, others = together_with(self.moving, others)
        if not self.left:
            self.sums = [moving[1], moving[-1]]
            return others
        for way, value in moving.items():
            (part,) = self.parts[way * self.left % self.n]
            total = add_rows(value, part, 0 if way == 1 else part.shape[0] - value.shape[0])
            self.moving[way] = self.sent(total, way)
        return others


class ScatterRings:
    def __init__(self, parts, axis):
        self.axis, self.n = axis, lax.axis_size(axis)
        self.half = self.n // 2
        self.parts = parts
        self.left = self.half
        self.sums = [[], []]
        self.moving = {}
        for chunk, way in ((0, 1), (1, -1)):
            self.send(chunk, way, parts[self.half][chunk])

    def send(self, chunk, way, value):
        self.moving[chunk, way] = lax.ppermute(value, self.axis, ring_route(self.n, way))

    def advance(self, *others):
        self.left -= 1
        moving, others = together_with(self.moving, others)
        self.moving = {}
        for (chunk, way), value in moving.items():
            if self.left:
                value = add_rows(value, self.parts[way * self.left % self.n][chunk], 0)
                self.send(chunk, way, value)
                self.last = value
            else:
                self.sums[chunk].append(value)
        if self.left == self.half - 1:
            for chunk, way in ((1, 1), (0, -1)):
                self.send(chunk, way, self.parts[way * self.left % self.n][chunk])
        return others


def dp_owners(n, me):
    return [((me - 2 * s) % n) ^ b for b in range(2) for s in range(n // 2)]


def next_chip(value):
    n = lax.axis_size("dp")
    return lax.ppermute(value, "dp", [(i, (i + 2) % n) for i in range(n)])


def other_core(value):
    return lax.ppermute(value, "dp", xor_route(lax.axis_size("dp"), 1))


class GatherDp:
    def __init__(self, block):
        self.chips = lax.axis_size("dp") // 2
        self.near, self.far = [block], [other_core(block)]
        self.moving = [next_chip(block)] if self.chips > 1 else []

    def relay(self, arrived):
        for step in range(1, self.chips):
            (value,) = arrived if step == 1 else self.moving
            self.near.append(value)
            self.far.append(other_core(value))
            self.moving = [next_chip(value)] if step + 1 < self.chips else []

    def all(self, arrived):
        return self.near + list(arrived)


class ScatterDp:
    def __init__(self, kept, given):
        self.chips = lax.axis_size("dp") // 2
        self.kept = kept
        self.moving = [other_core(given)]

    def relay(self, arrived, *after):
        self.sums = add_core(self.kept, arrived[0], self.chips, after)
        self.moving = [next_chip(self.sums[1])] if self.chips > 1 else []
        for step in range(2, self.chips):
            value = self.moving[0].astype(F32)
            self.moving = [next_chip((value + self.sums[step]).astype(BF))]

    def all(self, arrived, dtype, *after):
        if self.chips == 1:
            return self.sums[0].astype(dtype)
        return add_last(arrived[0], self.sums[0], dtype, after)


def doubled(block, axis, bits):
    return join([block, lax.ppermute(block, axis, xor_route(lax.axis_size(axis), bits))])


def pairs(block, axis):
    n = lax.axis_size(axis)
    return [block] + [lax.ppermute(block, axis, xor_route(n, bits)) for bits in range(2, n, 2)]


def powers(axis):
    return [1 << k for k in range(lax.axis_size(axis).bit_length() - 1)]


def vmem_of(arrays, specs, rest):
    total = rest
    for array, spec in zip(arrays, specs):
        if spec.block_shape is not None:
            copies = 1 if spec.pipeline_mode else 2
            total += copies * int(np.prod(spec.block_shape)) * array.dtype.itemsize
    return total


def call_kernel(body, scalars, grid, ins, in_specs, outs, out_specs, name, scratch=(), flops=0, rest=6 * 2**20, after=()):
    count = 1 + len(ins)
    inner = body
    if after:

        def body(*refs):
            inner(*refs[:count], *refs[count + len(after) :])

    ins = (*ins, *after)
    in_specs = [*in_specs, *(whole(a) for a in after)]
    bytes_moved = sum(int(np.prod(a.shape)) * a.dtype.itemsize for a in outs)
    return pl.pallas_call(
        body,
        grid_spec=pltpu.PrefetchScalarGridSpec(
            num_scalar_prefetch=1, grid=grid, in_specs=in_specs, out_specs=out_specs, scratch_shapes=scratch
        ),
        out_shape=outs,
        compiler_params=pltpu.CompilerParams(
            vmem_limit_bytes=vmem_of((*ins, *outs), (*in_specs, *out_specs), rest)
        ),
        cost_estimate=pl.CostEstimate(flops=flops, bytes_accessed=0, transcendentals=0),
        name=name,
    )(scalars, *ins)


def whole(array):
    return pl.BlockSpec(array.shape, lambda *i: (0, 0))


def once(array):
    return pl.BlockSpec(array.shape, lambda *i: (0, 0), pipeline_mode=pl.Buffered(1))


def rows_of(width, rows=ROWS):
    return pl.BlockSpec((rows, width), lambda i, s: (i, 0))


def call_whole(body, ins, outs, name, rest=2**20):
    specs = [pl.BlockSpec(memory_space=pltpu.VMEM)] * len(ins), [pl.BlockSpec(memory_space=pltpu.VMEM)] * len(outs)
    held = sum(int(np.prod(a.shape)) * a.dtype.itemsize for a in (*ins, *outs))
    return pl.pallas_call(
        body,
        in_specs=specs[0],
        out_specs=specs[1],
        out_shape=outs,
        compiler_params=pltpu.CompilerParams(vmem_limit_bytes=held + rest),
        cost_estimate=NO_COST,
        name=name,
    )(*ins)


def halves_kernel(first, second, top, bottom):
    rows = top.shape[0]
    top[...] = first[:rows, :]
    bottom[...] = second[rows:, :]


def halves(first, second):
    out = jax.ShapeDtypeStruct((first.shape[0] // 2, first.shape[1]), first.dtype)
    return call_whole(halves_kernel, (first, second), [out, out], "halves")


def stand_kernel(value, out):
    out[...] = value[0:8, :].astype(F32)


def stand(value):
    flat = value.reshape(-1, value.shape[-1])
    rows = min(16, flat.shape[0])
    return pl.pallas_call(
        stand_kernel,
        grid=(1,),
        in_specs=[pl.BlockSpec((rows, LANE), lambda i: (0, 0))],
        out_specs=pl.BlockSpec((8, LANE), lambda i: (0, 0)),
        out_shape=jax.ShapeDtypeStruct((8, LANE), F32),
        compiler_params=pltpu.CompilerParams(vmem_limit_bytes=2**20),
        cost_estimate=NO_COST,
        name="stand",
    )(flat)


def join_kernel(*refs):
    *blocks, out = refs
    first = 0
    for block in blocks:
        out[first : first + block.shape[0], :] = block[...]
        first += block.shape[0]


def join(blocks):
    rows = sum(block.shape[0] for block in blocks)
    out = jax.ShapeDtypeStruct((rows, blocks[0].shape[1]), blocks[0].dtype)
    return call_whole(join_kernel, blocks, [out], "join")[0]


def add_rows_kernel(place, sent, part, out):
    rows = sent.shape[0]
    if rows < out.shape[0]:
        out[...] = part[...]
    at = slice(place, place + rows)
    out[at, :] = (sent[...].astype(F32) + part[at, :].astype(F32)).astype(BF)


def add_rows(sent, part, place):
    body = functools.partial(add_rows_kernel, place)
    return call_whole(body, (sent, part), [jax.ShapeDtypeStruct(part.shape, BF)], "add_rows")[0]


def add_core_kernel(chips, kept, given, *refs):
    outs = refs[-chips:]
    rows = outs[0].shape[0]
    for k, out in enumerate(outs):
        at = slice(k * rows, (k + 1) * rows)
        out[...] = (kept[at, :].astype(F32) + given[at, :].astype(F32)).astype(out.dtype)


def add_core(kept, given, chips, after):
    rows, cols = kept.shape[0] // chips, kept.shape[1]
    outs = [jax.ShapeDtypeStruct((rows, cols), BF if k == 1 else F32) for k in range(chips)]
    return call_whole(functools.partial(add_core_kernel, chips), (kept, given, *after), outs, "add_core")


def add_last_kernel(arrived, kept, *refs):
    out = refs[-1]
    out[...] = (arrived[...].astype(F32) + kept[...]).astype(out.dtype)


def add_last(arrived, kept, dtype, after):
    return call_whole(add_last_kernel, (arrived, kept, *after), [jax.ShapeDtypeStruct(kept.shape, dtype)], "add_last")[0]


def weight_term(left, right):
    half = left.shape[1] // 2
    given = mm(left[:, half:], right, ((0,), (0,))).astype(BF)
    kept = mm(left[:, :half], right, ((0,), (0,))).astype(BF)
    return kept, given


class Small:
    BIAS, NORM, GATE, HEADS = CONV_K, CONV_K + 1, CONV_K + 2, CONV_K + 3
    SKIP_GRAD, BIAS_GRAD, LOG_GRAD = CONV_K + 1, CONV_K + 2, CONV_K + 3


def pack_small(conv_w, conv_b, norm_w, gate_w, dt_bias, a_log, skip_gain):
    per_head = jnp.concatenate([dt_bias, a_log, skip_gain])
    rows = [conv_w] + [row.reshape(1, -1) for row in (conv_b, norm_w, gate_w, per_head)]
    lanes = max(row.shape[1] for row in rows)
    lanes = -(-lanes // LANE) * LANE
    return jnp.concatenate([jnp.pad(row.astype(F32), ((0, 0), (0, lanes - row.shape[1]))) for row in rows])


def lanes_of(width):
    return lax.broadcasted_iota(jnp.int32, (8, width), 1)


def own_blocks(dp, heads, head, own, striped):
    if striped:
        size = own // dp
        return [(j * heads + head) * size for j in range(dp)], size
    return [head * own], own


def unpack_kernel(dp, heads, per_device, striped, where, table, taps, gate, norm, head_rows, skip):
    own = gate.shape[1]
    my_head, my_dp = where[RING], where[RING + heads]
    lanes = table.shape[1]

    def tile(at_dp, at_head):
        slot = (at_dp ^ my_dp) * heads + (at_head ^ my_head)
        return table[pl.ds(pl.multiple_of(slot * 8, 8), 8), :]

    def run(first, width):
        lane = lanes_of(LANE)
        start = first // width
        shift = first - start * width
        total = jnp.zeros((8, LANE), F32)
        for k in range((LANE + width - 2) // width + 1):
            device = jnp.minimum(start + k, dp * heads - 1)
            moved = pltpu.roll(tile(device // heads, device % heads), (k * width - shift) % lanes, 1)[:, :LANE]
            source = lane - k * width + shift
            total = jnp.where((source >= 0) & (source < width), moved, total)
        return total

    blocks, size = own_blocks(dp, heads, my_head, own, striped)
    conv_width, norm_width, gate_width = per_device
    at = 0
    for first in blocks:
        for more in range(0, size, LANE):
            taps[:, at : at + LANE] = run(first + more, conv_width)
            gate[:, at : at + LANE] = run(first + more, gate_width)
            at += LANE
    for more in range(0, 2 * N, LANE):
        taps[:, own + more : own + more + LANE] = run(jnp.int32(DI + more), conv_width)
    for more in range(0, norm.shape[1], LANE):
        norm[:, more : more + LANE] = run(jnp.int32(more), norm_width)
    lane = lanes_of(LANE)
    own_heads = own // P_SIZE
    found = [jnp.zeros((8, LANE), F32)] * 3
    for k in range(own_heads):
        each = own_heads // len(blocks)
        head = blocks[k // each] // P_SIZE + k % each
        device = head // own_heads
        values = tile(my_dp, device)
        for kind in range(3):
            source = kind * own_heads + head - device * own_heads
            moved = pltpu.roll(values, (k - source + lanes) % lanes, 1)[:, :LANE]
            found[kind] = jnp.where(lane == k, moved, found[kind])
    row = slice(Small.HEADS, Small.HEADS + 1)
    head_rows[...] = jnp.zeros_like(head_rows)
    head_rows[0:1, :] = found[0][row, :]
    head_rows[1:2, :] = jnp.where(lane[0:1, :] < own_heads, -jnp.exp(found[1][row, :]), 0.0)
    head_of = lax.broadcasted_iota(jnp.int32, (LANE, own), 1) // P_SIZE
    spread = (head_of == lax.broadcasted_iota(jnp.int32, (LANE, own), 0)).astype(F32).astype(BF)
    skip[...] = split_times(found[2], spread, 3)


def unpack(where, dp, heads, striped, own, width, per_device, table):
    outs = [jax.ShapeDtypeStruct((8, w), F32) for w in (own + 2 * N, own, width, LANE, own)]
    return call_kernel(
        functools.partial(unpack_kernel, dp, heads, per_device, striped),
        where,
        (1,),
        (table,),
        [whole(table)],
        outs,
        [whole(o) for o in outs],
        "unpack",
    )


def collect_kernel(dp, heads, striped, taps_dev, where, table, taps, bias, head_out, full, by_head):
    chans = table.shape[1]
    own = chans - 2 * N
    own_heads = own // P_SIZE
    my_head, my_dp = where[RING], where[RING + heads]

    def slot(at_head):
        return pl.multiple_of((at_head ^ my_head) * 8, 8)

    full[...] = jnp.zeros_like(full)
    shared = jnp.zeros((8, 2 * N), F32)
    chan_head = lax.broadcasted_iota(jnp.int32, (own, LANE), 0) // P_SIZE
    gather = (chan_head == lax.broadcasted_iota(jnp.int32, (own, LANE), 1)).astype(F32).astype(BF)
    row = lax.broadcasted_iota(jnp.int32, (8, LANE), 0)
    for head in range(heads):
        tile = table[pl.ds(slot(head), 8), :]
        blocks, size = own_blocks(dp, heads, head, own, striped)
        for k, first in enumerate(blocks):
            full[:, first : first + size] = tile[:, k * size : (k + 1) * size]
        shared = shared + tile[:, own:]
        summed = split_times(tile[:, :own], gather, 3)
        by_head[head * 8 : (head + 1) * 8, :] = jnp.where(row == Small.SKIP_GRAD, summed, tile[:, :LANE])
    full[:, DI : DI + 2 * N] = shared
    first = (my_dp * heads + my_head) * taps_dev
    start = first // LANE
    window = -(-(taps_dev + LANE) // LANE) * LANE
    rows = full[:, pl.ds(pl.multiple_of(start * LANE, LANE), window)]
    rows = pltpu.roll(rows, (window - (first - start * LANE)) % window, 1)[:, :taps_dev]
    taps[...] = rows[:CONV_K, :]
    bias[...] = rows[CONV_K : CONV_K + 1, :]
    lane = lanes_of(LANE)
    total = jnp.zeros((8, LANE), F32)
    per_block = own_heads // dp if striped else own_heads
    for k in range(own_heads):
        head = my_head * own_heads + k
        block = head // per_block
        owner = block % heads
        source = block // heads * per_block + head % per_block
        values = by_head[pl.ds(pl.multiple_of(owner * 8, 8), 8), :]
        total = jnp.where(lane == k, pltpu.roll(values, (k - source + LANE) % LANE, 1), total)
    head_out[...] = total


def collect(where, dp, heads, striped, taps_dev, table):
    outs = [jax.ShapeDtypeStruct(shape, F32) for shape in ((CONV_K, taps_dev), (1, taps_dev), (8, LANE))]
    window = -(-(taps_dev + LANE) // LANE) * LANE
    return call_kernel(
        functools.partial(collect_kernel, dp, heads, striped, taps_dev),
        where,
        (1,),
        (table,),
        [whole(table)],
        outs,
        [whole(o) for o in outs],
        "collect",
        scratch=[pltpu.VMEM((8, CONV_CH + window), F32), pltpu.VMEM((8 * heads, LANE), F32)],
    )


def ring_rows(arrived):
    found = []
    for distance, arrays in enumerate(arrived):
        first = 0
        for array in arrays:
            found.append((distance, first, array))
            first += array.shape[0]
    return found


def place_kernel(places, where, *refs):
    count = len(places)
    out, sems = refs[-2:]
    rows_dev = max(first + ref.shape[0] for (_, first), ref in zip(places, refs))
    copies = []
    for k, ((distance, first), ref) in enumerate(zip(places, refs[:count])):
        to = pl.multiple_of(where[RING + distance] * rows_dev + first, ref.shape[0])
        copies.append(pltpu.make_async_copy(ref, out.at[pl.ds(to, ref.shape[0]), :], sems.at[k]))
    for copy in copies:
        copy.start()
    for copy in copies:
        copy.wait()


def place(where, found, buffer, length, after=()):
    places, arrays = [f[:2] for f in found], [f[2] for f in found]
    held = () if buffer is None else (buffer,)
    anywhere = pl.BlockSpec(memory_space=pl.ANY)
    ins = (*arrays, *held, *after)
    return pl.pallas_call(
        functools.partial(place_kernel, places),
        grid_spec=pltpu.PrefetchScalarGridSpec(
            num_scalar_prefetch=1,
            grid=(1,),
            in_specs=[anywhere] * len(ins),
            out_specs=anywhere,
            scratch_shapes=[pltpu.SemaphoreType.DMA((len(arrays),))],
        ),
        out_shape=jax.ShapeDtypeStruct((length, arrays[0].shape[1]), arrays[0].dtype),
        input_output_aliases={1 + len(arrays): 0} if held else {},
        compiler_params=pltpu.CompilerParams(vmem_limit_bytes=2**20),
        cost_estimate=NO_COST,
        name="place",
    )(where, *ins)


def project_kernel(heads, dp, where, gain, rows, *refs):
    pieces, (normed, out) = refs[:dp], refs[-2:]
    width = rows.shape[1]
    piece = width // dp
    values = rows[...].astype(F32)
    scale = lax.rsqrt(jnp.sum(values * values, axis=-1, keepdims=True) / width + EPS)
    total = None
    for b in range(dp):
        at = pl.ds(pl.multiple_of(where[RING + heads + b] * piece, LANE), piece)
        low = (rows[:, at].astype(F32) * scale * gain[Small.NORM : Small.NORM + 1, at]).astype(BF)
        normed[:, b * piece : (b + 1) * piece] = low
        term = mm(low, pieces[b][...])
        total = term if b == 0 else total + term
    out[...] = total


def project(where, heads, gain, rows, pieces):
    length, width = rows.shape
    cols = pieces[0].shape[1]
    dp = len(pieces)
    return call_kernel(
        functools.partial(project_kernel, heads, dp),
        where,
        (length // ROWS,),
        (gain, rows, *pieces),
        [once(gain), rows_of(width)] + [once(p) for p in pieces],
        [jax.ShapeDtypeStruct((length, width), BF), jax.ShapeDtypeStruct((length, cols), F32)],
        [rows_of(width), rows_of(cols)],
        "project",
        flops=2 * length * width * cols,
        rest=12 * 2**20,
    )


def gate_forward_kernel(dp, first, places, where, rows, scan, gain, *refs):
    gate_pieces, out_pieces, (gate_out, w_full, *parts) = refs[:dp], refs[dp : 2 * dp], refs[2 * dp :]
    depth, each = gate_pieces[0].shape[0], out_pieces[0].shape[0]

    @pl.when(pl.program_id(0) == 0)
    def _():
        for k in range(dp):
            w_full[pl.ds(pl.multiple_of(where[first + k] * each, each), each), :] = out_pieces[k][...]

    gate = mm(rows[:, :depth], gate_pieces[0][...])
    for k in range(1, dp):
        gate = gate + mm(rows[:, k * depth : (k + 1) * depth], gate_pieces[k][...])
    gate_out[...] = gate
    inner = scan[...].astype(F32) * (gate / (1.0 + jnp.exp(-gate)))
    branch = mm((inner * gain[Small.GATE : Small.GATE + 1, :]).astype(BF), w_full[...]).astype(BF)
    put_parts(where, branch, parts, places)


def part_places(heads, rows_dev, halves):
    places = []
    for distance in range(heads):
        count = 2 if distance in halves else 1
        places += [(distance, k * rows_dev // count, rows_dev // count) for k in range(count)]
    return places


def by_distance(places, parts):
    found = {}
    for (distance, _, _), part in zip(places, parts):
        found.setdefault(distance, []).append(part)
    return found


def put_parts(where, block, parts, places):
    size = block.shape[0]
    rows_dev = max(first + rows for _, first, rows in places)
    for (distance, first, rows), part in zip(places, parts):
        start = where[RING + distance] * rows_dev + first - pl.program_id(0) * size
        for at in range(0, size, rows):

            @pl.when(start == at)
            def _(part=part, at=at, rows=rows):
                part[...] = block[at : at + rows, :]


def gate_forward(where, heads, normed, scanned, gain, gate_pieces, out_pieces, after):
    length, width = normed.shape
    own, cols = scanned.shape[1], out_pieces[0].shape[1]
    dp = len(gate_pieces)
    full = jax.ShapeDtypeStruct((own, cols), BF)
    first = where.shape[0] - dp
    places = part_places(heads, length // heads, (heads // 2,))
    parts = [jax.ShapeDtypeStruct((rows, cols), BF) for _, _, rows in places]

    gate, full, *parts = call_kernel(
        functools.partial(gate_forward_kernel, dp, first, places),
        where,
        (length // ROWS,),
        (normed, scanned, gain, *gate_pieces, *out_pieces),
        [rows_of(width), rows_of(own)] + [once(a) for a in (gain, *gate_pieces, *out_pieces)],
        [jax.ShapeDtypeStruct((length, own), F32), full, *parts],
        [rows_of(own)] + [once(a) for a in (full, *parts)],
        "gate_forward",
        rest=10 * 2**20,
        after=after,
    )
    return gate, full, by_distance(places, parts)


def gate_sums_kernel(heads, places, where, w_full, scan, gate_in, gain, *refs):
    chunks, (cot, weighted_out, sums) = refs[: len(places)], refs[-3:]
    rows_dev = cot.shape[0] // heads
    block = scan.shape[0]

    @pl.when(pl.program_id(0) == 0)
    def _():
        for (distance, first), ref in zip(places, chunks):
            rows = ref.shape[0]
            to = pl.multiple_of(where[RING + distance] * rows_dev + first, rows)
            live = to + row_ids(rows) < where[SEQS - 1]
            values = ref[...]
            cot[pl.ds(to, rows), :] = jnp.where(live, values, jnp.zeros_like(values))

    mine = pl.ds(pl.multiple_of(pl.program_id(0) * block, block), block)
    weighted = mm(cot[mine, :], w_full[...], ((1,), (1,))) * gain[Small.GATE : Small.GATE + 1, :]
    weighted_out[...] = weighted
    gate = gate_in[...]
    inner = scan[...].astype(F32) * (gate / (1.0 + jnp.exp(-gate)))
    lane = lax.broadcasted_iota(jnp.int32, (1, LANE), 1)
    squares = jnp.sum(inner * inner, axis=1, keepdims=True)
    along = jnp.sum(inner * weighted, axis=1, keepdims=True)
    both = jnp.where(lane == 0, squares, jnp.where(lane == 1, along, 0.0))
    sums[...] = both.T[0:8, :]


def gate_sums(where, arrived, w_full, scanned, gate, gain, after):
    found = ring_rows(arrived)
    places, chunks = [f[:2] for f in found], [f[2] for f in found]
    own, cols = w_full.shape
    length = scanned.shape[0]
    heads = len(arrived)

    def body(*refs):
        gate_sums_kernel(heads, places, *refs)

    cot = jax.ShapeDtypeStruct((length, cols), BF)
    return call_kernel(
        body,
        where,
        (length // ROWS,),
        (w_full, scanned, gate, gain, *chunks),
        [once(w_full), rows_of(own), rows_of(own), once(gain)] + [once(c) for c in chunks],
        [cot, jax.ShapeDtypeStruct((length, own), F32), jax.ShapeDtypeStruct((8, length), F32)],
        [once(cot), rows_of(own), pl.BlockSpec((8, ROWS), lambda i, s: (0, i))],
        "gate_sums",
        after=after,
        flops=2 * length * own * cols,
    )


def gate_backward_kernel(first, block, where, sums, weighted, scan, gate_in, gain, scan_out, gate_out, gated, held):
    columns = sums[...].T
    ratio = lax.rsqrt(columns[:, 0:1] / DI + EPS)
    pull = ratio * ratio * ratio * columns[:, 1:2] / DI
    gate = gate_in[...]
    sig = 1.0 / (1.0 + jnp.exp(-gate))
    act = gate * sig
    scanned = scan[...].astype(F32)
    inner = scanned * act
    grad = ratio * weighted[...] - pull * inner
    scan_out[...] = (grad * act).astype(BF)
    gate_out[...] = (grad * scanned * (sig * (1.0 + gate * (1.0 - sig)))).astype(BF)
    held[...] = (ratio * inner * gain[Small.GATE : Small.GATE + 1, :]).astype(BF)
    for k in range(gated.shape[1] // block):
        at = slice(k * block, (k + 1) * block)
        if block < gated.shape[1]:
            gated[:, at] = held[:, pl.ds(pl.multiple_of(where[first + k] * block, LANE), block)]
        else:
            gated[...] = held[...]


def gate_backward(where, dp, striped, sums, weighted, scanned, gate, gain):
    length, own = scanned.shape
    return call_kernel(
        functools.partial(gate_backward_kernel, where.shape[0] - dp, own // dp if striped else own),
        where,
        (length // ROWS,),
        (sums, weighted, scanned, gate, gain),
        [pl.BlockSpec((8, ROWS), lambda i, s: (0, i))] + [rows_of(own)] * 3 + [whole(gain)],
        [jax.ShapeDtypeStruct((length, own), BF)] * 3,
        [rows_of(own)] * 3,
        "gate_backward",
        scratch=[pltpu.VMEM((ROWS, own), BF)],
    )


def project_back_kernel(dp, places, where, gate_rows, mix_rows, *refs):
    gate_pieces, mix_pieces, parts, out = refs[:dp], refs[dp : 2 * dp], refs[2 * dp : -1], refs[-1]
    depth = gate_pieces[0].shape[0]
    for k in range(dp):
        total = mm(mix_rows[...], mix_pieces[k][...], ((1,), (1,)))
        total = total + mm(gate_rows[...], gate_pieces[k][...], ((1,), (1,)))
        out[:, k * depth : (k + 1) * depth] = total.astype(BF)
    put_parts(where, out, parts, places)


def project_back(where, heads, grad_gate, grad_mix, gate_pieces, mix_pieces, after):
    length, own = grad_gate.shape
    cols = grad_mix.shape[1]
    pieces = (*gate_pieces, *mix_pieces)
    dp = len(gate_pieces)
    width = dp * gate_pieces[0].shape[0]
    places = part_places(heads, length // heads, range(heads))
    parts = [jax.ShapeDtypeStruct((rows, width), BF) for _, _, rows in places]
    parts = call_kernel(
        functools.partial(project_back_kernel, dp, places),
        where,
        (length // ROWS,),
        (grad_gate, grad_mix, *pieces),
        [rows_of(own), rows_of(cols)] + [once(p) for p in pieces],
        parts,
        [once(p) for p in parts],
        "project_back",
        after=after,
        scratch=[pltpu.VMEM((ROWS, width), BF)],
        rest=10 * 2**20,
    )
    return by_distance(places, parts)


def input_grad_kernel(dp, first, where, *refs):
    parts, (hidden, cot, gain, out, total) = refs[:-5], refs[-5:]
    rows, width = parts[0].shape
    piece = width // dp
    for k in range(2):
        at = slice(k * rows, (k + 1) * rows)
        own, ahead, behind = parts[3 * k : 3 * k + 3]
        grad = own[...].astype(F32) + ahead[...].astype(F32) + behind[...].astype(F32)
        for b in range(dp):
            to = pl.ds(pl.multiple_of(where[first + b] * piece, LANE), piece)
            total[at, to] = grad[:, b * piece : (b + 1) * piece]
    values = hidden[...].astype(F32)
    scale = lax.rsqrt(jnp.sum(values * values, axis=-1, keepdims=True) / width + EPS)
    grad = total[...] * gain[Small.NORM : Small.NORM + 1, :]
    along = jnp.sum(values * grad, axis=-1, keepdims=True) / width
    out[...] = cot[...].astype(F32) + scale * (grad - values * (scale * scale * along))


def input_grad_of(where, dp, parts, hidden, cot, gain):
    first = where.shape[0] - dp
    ins = (*parts, hidden, cot, gain)
    return call_kernel(
        functools.partial(input_grad_kernel, dp, first),
        where,
        (1,),
        ins,
        [once(a) for a in ins],
        [jax.ShapeDtypeStruct(hidden.shape, F32)],
        [once(hidden)],
        "input_grad",
        scratch=[pltpu.VMEM(hidden.shape, F32)],
    )[0]


def output_kernel(where, sums, hidden, own, ahead, behind, *refs):
    out = refs[-1]
    rows = hidden.shape[0]
    branch = own[...].astype(F32) + ahead[...].astype(F32) + behind[...].astype(F32)
    live = where[RING] * rows + row_ids(rows) < where[SEQS - 1]
    ratio = jnp.where(live, lax.rsqrt(sums[...].T[:, 0:1] / DI + EPS), 0.0)
    out[...] = (hidden[...].astype(F32) + ratio * branch).astype(BF)


def output_of(where, sums, hidden, parts):
    rows = hidden.shape[0]
    return call_kernel(
        output_kernel,
        where,
        (1,),
        (sums, hidden, *parts),
        [pl.BlockSpec((8, rows), lambda i, s: (0, s[RING]))] + [once(a) for a in (hidden, *parts)],
        [jax.ShapeDtypeStruct(hidden.shape, BF)],
        [once(hidden)],
        "output",
    )[0]


def out_grad_kernel(arrived, kept, w_out, out, sums):
    total = arrived[...].astype(F32) + kept[...]
    out[...] = total
    sums[...] = jnp.sum(total * w_out[...].astype(F32), axis=1, keepdims=True) + jnp.zeros(sums.shape, F32)


def out_grad_of(arrived, kept, w_out):
    outs = [jax.ShapeDtypeStruct(w_out.shape, F32), jax.ShapeDtypeStruct((w_out.shape[0], LANE), F32)]
    return call_whole(out_grad_kernel, (arrived, kept, w_out), outs, "out_grad", rest=4 * 2**20)


def weight_rows_kernel(dp, striped, gate_cols, mix_cols, w_in, out, norm_out):
    heads, rows, own = gate_cols.shape
    own_heads = own // P_SIZE
    chans = own + 2 * N
    norm = jnp.zeros((rows, 1), F32)

    def put(first, values):
        nonlocal norm
        at = slice(first, first + values.shape[1])
        out[:, at] = values
        norm = norm + jnp.sum(values * w_in[:, at].astype(F32), axis=1, keepdims=True)

    shared = mix_cols[0, :, own:chans].astype(F32)
    for head in range(1, heads):
        shared = shared + mix_cols[head, :, own:chans].astype(F32)
    put(2 * DI, shared)
    steps = jnp.zeros((rows, heads * own_heads), F32)
    source = lax.broadcasted_iota(jnp.int32, (LANE, heads * own_heads), 0)
    target = lax.broadcasted_iota(jnp.int32, (LANE, heads * own_heads), 1)
    count = dp if striped else 1
    for head in range(heads):
        for block in range(count):
            size = own // count
            at = slice(block * size, (block + 1) * size)
            put((block * heads + head) * size, gate_cols[head, :, at].astype(F32))
            put(DI + (block * heads + head) * size, mix_cols[head, :, at].astype(F32))
        each = own_heads // count
        to = (source // each * heads + head) * each + source % each
        picked = ((to == target) & (source < own_heads)).astype(F32).astype(BF)
        steps = steps + mm(mix_cols[head, :, chans:], picked)
    put(DI + CONV_CH, steps)
    norm_out[...] = norm + jnp.zeros(norm_out.shape, F32)


def weight_rows(dp, striped, gate_cols, mix_cols, w_in):
    rows = w_in.shape[0]
    ins = (gate_cols, mix_cols, w_in)

    def body(*refs):
        weight_rows_kernel(dp, striped, *refs)

    return pl.pallas_call(
        body,
        out_shape=[jax.ShapeDtypeStruct(w_in.shape, F32), jax.ShapeDtypeStruct((rows, LANE), F32)],
        compiler_params=pltpu.CompilerParams(vmem_limit_bytes=SCAN_VMEM),
        cost_estimate=NO_COST,
        name="weight_rows",
    )(*ins)


FAR = -1e30


def mm(left, right, contract=((1,), (0,))):
    return lax.dot_general(left, right, (contract, ((), ())), preferred_element_type=F32)


def row_ids(rows):
    return lax.broadcasted_iota(jnp.int32, (rows, 1), 0)


def split_sum(ones, values, count):
    parts, rest = [], values
    for _ in range(count):
        part = rest.astype(BF)
        parts.append(part)
        rest = rest - part.astype(F32)
    product = mm(ones, jnp.concatenate(parts, axis=1))
    width = values.shape[1]
    total = product[:, :width]
    for k in range(1, count):
        total = total + product[:, k * width : (k + 1) * width]
    return total


def split_times(values, ones, count):
    total, rest = jnp.zeros((values.shape[0], ones.shape[1]), F32), values
    for _ in range(count):
        part = rest.astype(BF)
        total = total + mm(part, ones)
        rest = rest - part.astype(F32)
    return total


def widen(values, spread2):
    high = values.astype(BF)
    low = (values - high.astype(F32)).astype(BF)
    return mm(jnp.concatenate([high, low], axis=1), spread2)


def segment_at(position, ends_ref):
    seg = jnp.zeros_like(position)
    start = jnp.zeros_like(position)
    for k in range(SEQS):
        end = ends_ref[k]
        seg = seg + (position >= end).astype(jnp.int32)
        start = jnp.where(position >= end, end, start)
    return seg, start


def scalar_segment(position, ends_ref):
    seg = jnp.int32(0)
    for k in range(SEQS):
        seg = seg + (position >= ends_ref[k]).astype(jnp.int32)
    return jnp.where(position < 0, -1, seg)


class Block:
    def __init__(self, index, ends_ref, dt_part, head_ref, own):
        rows = BLOCK_LEN
        first = index * rows
        seg, self.start = segment_at(first + row_ids(rows), ends_ref)
        self.position = first + row_ids(rows)
        col = lax.broadcasted_iota(jnp.int32, (1, rows), 1)
        seg_row, _ = segment_at(first + col, ends_ref)
        causal = row_ids(rows) >= col
        self.lower = jnp.where(causal, 1.0, 0.0).astype(BF)
        same = seg == seg_row
        self.penalty = jnp.where(causal & same, 0.0, FAR)
        before = scalar_segment(first - 1, ends_ref)
        last = scalar_segment(first + rows - 1, ends_ref)
        self.raw = dt_part.astype(BF).astype(F32) + head_ref[0:1, :]
        self.decay = head_ref[1:2, :]
        self.dt = jnp.maximum(self.raw, 0.0) + jnp.log1p(jnp.exp(-jnp.abs(self.raw)))
        self.cum = split_sum(self.lower, self.dt * self.decay, 3)
        final = self.cum[rows - 1 : rows, :]
        self.enter = jnp.where(seg == before, jnp.exp(self.cum), 0.0)
        self.tail = jnp.where(seg == last, jnp.exp(final - self.cum), 0.0)
        self.keep = jnp.where(before == last, jnp.exp(final), 0.0)
        head_of = lax.broadcasted_iota(jnp.int32, (LANE, own), 1) // P_SIZE
        self.spread = (head_of == lax.broadcasted_iota(jnp.int32, (LANE, own), 0)).astype(F32).astype(BF)
        spread2 = jnp.concatenate([self.spread, self.spread], axis=0)
        self.dt_wide = widen(self.dt, spread2)
        self.enter_wide = widen(self.enter, spread2)
        self.tail_wide = widen(self.tail, spread2)
        self.cum_row = self.cum.T
        chan_head = lax.broadcasted_iota(jnp.int32, (own, LANE), 0) // P_SIZE
        self.gather = (chan_head == lax.broadcasted_iota(jnp.int32, (own, LANE), 1)).astype(F32)
        self.keep_chan = jnp.sum(self.gather * self.keep, axis=1, keepdims=True)

    def gap(self, head):
        return self.cum[:, head : head + 1] - self.cum_row[head : head + 1, :]


def scan_forward_kernel(ends_ref, mix_ref, taps_ref, head_ref, skip_ref, state_in, rim_in, *refs, base):
    pre_ref, scan_ref, enter_ref, state, rim, ext = refs[-6:]
    index = base + pl.program_id(0)
    chans = pre_ref.shape[1]
    own = chans - 2 * N
    rows = BLOCK_LEN

    @pl.when(pl.program_id(0) == 0)
    def _():
        rim[...] = rim_in[...]
        state[...] = state_in[...]

    ext[0:8, :] = rim[...]
    ext[8:, :] = mix_ref[:, :chans]
    blk = Block(index, ends_ref, mix_ref[:, chans:], head_ref, own)
    total = taps_ref[CONV_K : CONV_K + 1, :] + taps_ref[CONV_K - 1 : CONV_K, :] * ext[8:, :]
    for lag in range(1, CONV_K):
        linked = (blk.position - lag >= blk.start).astype(F32)
        tap = taps_ref[CONV_K - 1 - lag : CONV_K - lag, :]
        total = total + tap * (linked * ext[8 - lag : 8 - lag + rows, :])
    rim[...] = ext[rows : rows + 8, :]
    pre_ref[...] = total
    low = (total / (1.0 + jnp.exp(-total))).astype(BF)
    x_low, b_low, c_low = low[:, :own], low[:, own : own + N], low[:, own + N :]
    x_wide = x_low.astype(F32)
    x_dt = (x_wide * blk.dt_wide).astype(BF)
    scores = mm(c_low, b_low, ((1,), (1,)))
    lane = lax.broadcasted_iota(jnp.int32, (1, LANE), 1)
    entering = state[...]
    enter_ref[...] = entering
    outer = mm(c_low, entering.astype(BF), ((1,), (1,))) * blk.enter_wide + skip_ref[Small.HEADS : Small.HEADS + 1, :] * x_wide
    for pair in range(own // LANE):
        both = x_dt[:, pair * LANE : (pair + 1) * LANE]
        parts = []
        for head in (2 * pair, 2 * pair + 1):
            mixing = scores * jnp.exp(blk.gap(head) + blk.penalty)
            parts.append(mm(mixing.astype(BF), both))
        inner = jnp.where(lane < P_SIZE, parts[0], parts[1])
        at = slice(pair * LANE, (pair + 1) * LANE)
        scan_ref[:, at] = (inner + outer[:, at]).astype(BF)
    added = mm((x_wide * blk.dt_wide * blk.tail_wide).astype(BF), b_low, ((0,), (0,)))
    state[...] = blk.keep_chan * entering + added


def scan_forward(ends, mix, taps, head_rows, skip_row, calls, after):
    length, cols = mix.shape
    chans = cols - LANE
    own = chans - 2 * N
    blocks = length // BLOCK_LEN
    each = blocks // calls
    state, rim, kept = jnp.zeros((own, N), F32), jnp.zeros((8, chans), F32), ()
    for call in range(calls):

        def rows_of(width, base=call * each, rows=BLOCK_LEN):
            return pl.BlockSpec((rows, width), lambda i, ends: (base + i, 0))

        def whole(array):
            return pl.BlockSpec(array.shape, lambda i, ends: (0, 0))

        *kept, state, rim = pl.pallas_call(
            functools.partial(scan_forward_kernel, base=call * each),
            grid_spec=pltpu.PrefetchScalarGridSpec(
                num_scalar_prefetch=1,
                grid=(each,),
                in_specs=[rows_of(cols)]
                + [whole(a) for a in (taps, head_rows, skip_row, state, rim)]
                + [pl.BlockSpec(memory_space=pl.ANY)] * len(kept)
                + [whole(a) for a in after],
                out_specs=[rows_of(chans), rows_of(own), rows_of(N, rows=own), whole(state), whole(rim)],
                scratch_shapes=[pltpu.VMEM((BLOCK_LEN + 8, chans), F32)],
            ),
            out_shape=[
                jax.ShapeDtypeStruct((length, chans), F32),
                jax.ShapeDtypeStruct((length, own), BF),
                jax.ShapeDtypeStruct((blocks * own, N), F32),
                jax.ShapeDtypeStruct(state.shape, F32),
                jax.ShapeDtypeStruct(rim.shape, F32),
            ],
            input_output_aliases={7 + k: k for k in range(len(kept))},
            compiler_params=pltpu.CompilerParams(vmem_limit_bytes=SCAN_VMEM),
            cost_estimate=pl.CostEstimate(flops=each * 2**31, bytes_accessed=0, transcendentals=0),
            name="scan_forward",
        )(ends, mix, taps, head_rows, skip_row, state, rim, *kept, *after)
    return kept


def scan_backward_kernel(
    ends_ref, pre_ref, mix_ref, dy_ref, enter_ref, taps_ref, head_ref, skip_ref, *refs, base
):
    carried, (grad_ref, *carries, ext) = refs[:3], refs[-5:]
    state, rim, small_ref = carries
    index = base - pl.program_id(0)
    chans = pre_ref.shape[1]
    own = chans - 2 * N
    rows = BLOCK_LEN

    @pl.when(pl.program_id(0) == 0)
    def _():
        for given, held in zip(carried, carries):
            held[...] = given[...]

    ext[rows:, :] = rim[...]
    blk = Block(index, ends_ref, mix_ref[:, chans:], head_ref, own)
    pre = pre_ref[...]
    sig = 1.0 / (1.0 + jnp.exp(-pre))
    low = (pre * sig).astype(BF)
    x_low, b_low, c_low = low[:, :own], low[:, own : own + N], low[:, own + N :]
    x_wide = x_low.astype(F32)
    dy = dy_ref[...]
    dy_wide = dy.astype(F32)
    x_dt = (x_wide * blk.dt_wide).astype(BF)
    entering = enter_ref[...]
    enter_low = entering.astype(BF)
    leaving = state[...]
    leaving_low = leaving.astype(BF)
    gather = blk.gather.astype(BF)

    scores = mm(c_low, b_low, ((1,), (1,)))
    scores_t = mm(b_low, c_low, ((1,), (1,)))
    penalty_t = blk.penalty.T
    lane = lax.broadcasted_iota(jnp.int32, (1, LANE), 1)
    lane_rows = lax.broadcasted_iota(jnp.int32, (rows, LANE), 1)
    sub_rows = lax.broadcasted_iota(jnp.int32, (LANE, rows), 0)
    grad_scores = jnp.zeros((rows, rows), F32)
    along_rows = jnp.zeros((rows, LANE), F32)
    along_cols = jnp.zeros((LANE, rows), F32)
    grad_xdt = []
    for pair in range(own // LANE):
        at = slice(pair * LANE, (pair + 1) * LANE)
        both, dy_both = x_dt[:, at], dy[:, at]
        parts = []
        for head in (2 * pair, 2 * pair + 1):
            gap = blk.gap(head)
            decay = jnp.exp(gap + blk.penalty)
            mixing_t = scores_t * jnp.exp(penalty_t - gap)
            parts.append(mm(mixing_t.astype(BF), dy_both))
            mine = (lane < P_SIZE) if head % 2 == 0 else (lane >= P_SIZE)
            dy_one = jnp.where(mine, dy_both, jnp.zeros_like(dy_both))
            grad_mixing = mm(dy_one, both, ((1,), (1,))) * decay
            grad_scores = grad_scores + grad_mixing
            moved = grad_mixing * scores
            along_rows = along_rows + jnp.where(lane_rows == head, jnp.sum(moved, axis=1, keepdims=True), 0.0)
            along_cols = along_cols + jnp.where(sub_rows == head, jnp.sum(moved, axis=0, keepdims=True), 0.0)
        grad_xdt.append(jnp.where(lane < P_SIZE, parts[0], parts[1]))
    grad_xdt = jnp.concatenate(grad_xdt, axis=1)
    grad_cum = along_rows - along_cols.T
    grad_low = grad_scores.astype(BF)
    grad_c = mm(grad_low, b_low)
    grad_b = mm(grad_low, c_low, ((0,), (0,)))

    dy_enter = dy_wide * blk.enter_wide
    dy_enter_low = dy_enter.astype(BF)
    seen = mm(c_low, enter_low, ((1,), (1,)))
    grad_cum = grad_cum + mm((dy_enter * seen).astype(BF), gather)
    grad_c = grad_c + mm(dy_enter_low, enter_low)
    grad_enter = mm(dy_enter_low, c_low, ((0,), (0,)))

    taken = mm(b_low, leaving_low, ((1,), (1,)))
    x_tail = x_wide * blk.tail_wide
    grad_tail = mm((x_tail * taken).astype(BF), gather)
    moved = grad_tail * blk.dt
    grad_b = grad_b + mm((x_tail * blk.dt_wide).astype(BF), leaving_low)
    kept = jnp.sum(leaving * entering, axis=1, keepdims=True) * blk.keep_chan
    grad_last = jnp.sum(moved, axis=0, keepdims=True) + jnp.sum(blk.gather * kept, axis=0, keepdims=True)
    grad_cum = grad_cum - moved + jnp.where(row_ids(rows) == rows - 1, grad_last, 0.0)
    state[...] = blk.keep_chan * leaving + grad_enter

    grad_dt = mm((x_wide * grad_xdt).astype(BF), gather) + grad_tail
    upper = (row_ids(rows) <= lax.broadcasted_iota(jnp.int32, (1, rows), 1)).astype(F32).astype(BF)
    grad_steps = split_sum(upper, grad_cum, 3)
    grad_dt = grad_dt + blk.decay * grad_steps
    grad_raw = grad_dt / (1.0 + jnp.exp(-blk.raw))
    small_ref[Small.BIAS_GRAD : Small.BIAS_GRAD + 1, :LANE] += jnp.sum(grad_raw, axis=0, keepdims=True)
    small_ref[Small.LOG_GRAD : Small.LOG_GRAD + 1, :LANE] += (
        jnp.sum(blk.dt * grad_steps, axis=0, keepdims=True) * blk.decay
    )
    small_ref[Small.SKIP_GRAD : Small.SKIP_GRAD + 1, :own] += jnp.sum(dy_wide * x_wide, axis=0, keepdims=True)

    grad_x = blk.dt_wide * (grad_xdt + blk.tail_wide * taken) + skip_ref[Small.HEADS : Small.HEADS + 1, :] * dy_wide
    grad_low = jnp.concatenate([grad_x.astype(BF).astype(F32), grad_b, grad_c], axis=1)
    grad_pre = grad_low * (sig * (1.0 + pre * (1.0 - sig)))
    ext[0:rows, :] = grad_pre
    conv_in = mix_ref[:, :chans]
    small_ref[Small.BIAS : Small.BIAS + 1, :] += jnp.sum(grad_pre, axis=0, keepdims=True)
    grad_in = jnp.zeros((rows, chans), F32)
    for lag in range(CONV_K):
        back = grad_pre if lag == 0 else ext[lag : lag + rows, :]
        if lag:
            _, start = segment_at(blk.position + lag, ends_ref)
            back = back * (blk.position >= start).astype(F32)
        tap = CONV_K - 1 - lag
        grad_in = grad_in + taps_ref[tap : tap + 1, :] * back
        small_ref[tap : tap + 1, :] += jnp.sum(conv_in * back, axis=0, keepdims=True)
    rim[...] = grad_pre[0:8, :]
    grad_ref[...] = jnp.concatenate([grad_in.astype(BF), grad_raw.astype(BF)], axis=1)


def scan_backward(ends, pre, mix, grad_scan, entering, taps, head_rows, skip_row, carries, grad, call, calls, after):
    length, cols = mix.shape
    chans = cols - LANE
    own = chans - 2 * N
    blocks = length // BLOCK_LEN
    each = blocks // calls
    last = blocks - 1 - call * each
    if call == 0:
        carries = [jnp.zeros(s, F32) for s in ((own, N), (8, chans), (8, chans))]
    held = () if call == 0 else (grad,)

    def rows_of(width, rows=BLOCK_LEN):
        return pl.BlockSpec((rows, width), lambda i, ends: (last - i, 0))

    def whole(array):
        return pl.BlockSpec(array.shape, lambda i, ends: (0, 0))

    grad, *carries = pl.pallas_call(
        functools.partial(scan_backward_kernel, base=last),
        grid_spec=pltpu.PrefetchScalarGridSpec(
            num_scalar_prefetch=1,
            grid=(each,),
            in_specs=[rows_of(chans), rows_of(cols), rows_of(own), rows_of(N, rows=own)]
            + [whole(a) for a in (taps, head_rows, skip_row, *carries)]
            + [pl.BlockSpec(memory_space=pl.ANY)] * len(held)
            + [whole(a) for a in after],
            out_specs=[rows_of(cols)] + [whole(a) for a in carries],
            scratch_shapes=[pltpu.VMEM((BLOCK_LEN + 8, chans), F32)],
        ),
        out_shape=[jax.ShapeDtypeStruct((length, cols), BF)]
        + [jax.ShapeDtypeStruct(a.shape, F32) for a in carries],
        input_output_aliases={11: 0} if held else {},
        compiler_params=pltpu.CompilerParams(vmem_limit_bytes=SCAN_VMEM),
        cost_estimate=pl.CostEstimate(flops=each * 2**31, bytes_accessed=0, transcendentals=0),
        name="scan_backward",
    )(ends, pre, mix, grad_scan, entering, taps, head_rows, skip_row, *carries, *held, *after)
    return grad, carries


def shards(
    hidden, seq_lens, norm_w, w_in, conv_w, conv_b, dt_bias, a_log, skip_gain, gate_w, w_out, cotangent
):
    dp, heads = lax.axis_size("dp"), lax.axis_size("heads")
    my_dp, my_head = lax.axis_index("dp"), lax.axis_index("heads")
    me = my_dp * heads + my_head
    rows_dev, width = hidden.shape
    length = rows_dev * heads
    w_rows = w_in.shape[0]
    out_rows = w_out.shape[0]
    own = DI // heads
    own_heads = own // P_SIZE
    chans = own + 2 * N
    taps_dev = conv_b.shape[0]
    ends = jnp.cumsum(seq_lens[0]).astype(jnp.int32)
    where = where_vector(ends)
    owners = [where[RING + heads + k] for k in range(dp)]
    striped = out_rows % P_SIZE == 0
    per_block = own_heads // dp if striped else 0

    def split_own(array, size):
        rows = array.shape[0]
        if striped:
            cut = array.reshape(rows, dp, heads, per_block * size).transpose(2, 0, 1, 3)
        else:
            cut = array.reshape(rows, heads, own_heads * size).transpose(1, 0, 2)
        return cut.reshape(heads, rows, own_heads * size)

    pad = LANE - own_heads
    mix_cut = jnp.concatenate(
        [
            split_own(w_in[:, DI : 2 * DI], P_SIZE),
            jnp.broadcast_to(w_in[None, :, 2 * DI : DI + CONV_CH], (heads, w_rows, 2 * N)),
            split_own(w_in[:, DI + CONV_CH :], 1),
            jnp.zeros((heads, w_rows, pad), BF),
        ],
        axis=2,
    )
    gate_cut = split_own(w_in[:, :DI], P_SIZE)

    def to_heads(cut):
        return lax.all_to_all(cut, "heads", split_axis=0, concat_axis=0, tiled=True)

    hidden_ring = GatherRing(hidden, "heads")
    steps = hidden_ring.half
    w_mix = to_heads(mix_cut)
    route = [(q, (q % dp) * heads + q // dp) for q in range(dp * heads)]
    out_gather = GatherDp(w_out if striped else lax.ppermute(w_out, ("dp", "heads"), route))
    small = pack_small(conv_w, conv_b, norm_w, gate_w, dt_bias, a_log, skip_gain)
    for axis in ("heads", "dp"):
        for bits in powers(axis):
            small = doubled(small, axis, bits)

    def placed(distances, buffer, after=()):
        found = [f for f in ring_rows([hidden_ring.arrived.get(d, []) for d in range(heads)]) if f[0] in distances]
        return place(where, found, buffer, length, after)

    for step in range(1, steps):
        if step == 1:
            w_mix, small, where, gate_cut, *arrived = hidden_ring.advance(
                w_mix, small, where, gate_cut, *out_gather.moving
            )
            mix_gather = GatherDp(w_mix.reshape(heads * w_rows, -1))
            out_gather.relay(arrived)
            tokens = placed((0, 1, heads - 1), None)
        elif step == 2:
            (cot,) = hidden_ring.advance(cotangent)
            tokens = placed((step, heads - step), tokens)
            cot_ring = GatherRing(cot, "heads")
        elif step == 3:
            gate_cut, *arrived = hidden_ring.advance(gate_cut, *mix_gather.moving)
            mix_gather.relay(arrived)
            tokens = placed((step, heads - step), tokens)
            w_gate = to_heads(gate_cut)
        else:
            hidden_ring.advance()
            tokens = placed((step, heads - step), tokens)
    arrived = hidden_ring.advance(*mix_gather.far, *out_gather.far)
    tokens = placed((heads // 2,), tokens)
    mix_pieces, out_pieces = mix_gather.all(arrived[: dp // 2]), out_gather.all(arrived[dp // 2 :])
    taps, gate_gain, norm_row, head_rows, skip_row = unpack(
        where, dp, heads, striped, own, width, (taps_dev, w_rows, out_rows), small
    )

    norm_row, w_gate = cot_ring.advance(norm_row, w_gate)
    gate_gather = GatherDp(w_gate.reshape(heads * w_rows, -1))
    normed, mix = project(where, heads, norm_row, tokens, mix_pieces)
    ready, *arrived = cot_ring.advance(stand(mix), *gate_gather.moving)
    gate_gather.relay(arrived)
    pre, scanned, entering = scan_forward(ends, mix, taps, head_rows, skip_row, 1, [ready])
    ready = stand(scanned)
    for step in range(3, steps):
        (ready,) = cot_ring.advance(ready)
    gate_pieces = gate_gather.all(gate_gather.far)
    gate, w_full, branch = gate_forward(
        where, heads, normed, scanned, gate_gain, gate_pieces, out_pieces, [ready]
    )
    ready = stand(gate)

    branch_ring = ScatterRing(branch, "heads")
    cot_ring.advance()
    cot_live, weighted, sums = gate_sums(where, cot_ring.all(), w_full, scanned, gate, gate_gain, [ready])
    sums = sums + lax.ppermute(sums, "heads", xor_route(heads, 1))
    (sums,) = branch_ring.advance(sums)
    sums = sum(pairs(sums, "heads"))
    grad_scan, grad_gate, gated = gate_backward(where, dp, striped, sums, weighted, scanned, gate, gate_gain)
    (ready,) = branch_ring.advance(stand(grad_gate))
    gate_scatter = ScatterDp(*weight_term(normed, grad_gate))

    def back(call, carries, grad_mix, *after):
        return scan_backward(
            ends, pre, mix, grad_scan, entering, taps, head_rows, skip_row, carries, grad_mix, call, 2, after
        )

    grad_mix, carries = back(0, None, (), stand(gate_scatter.kept), ready)
    ready, *arrived = branch_ring.advance(stand(carries[0]), *gate_scatter.moving)
    gate_scatter.relay(arrived)
    if striped:
        terms = weight_term(gated, cot_live)
    else:
        term = mm(gated, cot_live, ((0,), (0,))).astype(BF)
        cuts = [lax.dynamic_slice(term, (o * out_rows, 0), (out_rows, width)) for o in owners]
        terms = jnp.concatenate(cuts[: dp // 2]), jnp.concatenate(cuts[dp // 2 :])
    out_scatter = ScatterDp(*terms)
    grad_mix, carries = back(1, carries, grad_mix, ready, stand(terms[0]))
    small_grads = carries[2]
    small_core = other_core(small_grads)
    mix_scatter = ScatterDp(*weight_term(normed, grad_mix))
    small_core, ready = together(small_core, stand(mix_scatter.kept))
    small_grads = small_grads + small_core
    small_moving = [lax.ppermute(small_grads, "dp", xor_route(dp, bits)) for bits in range(2, dp, 2)]
    parts = project_back(
        where, heads, grad_gate, grad_mix, gate_pieces, mix_pieces, [ready, stand(small_grads)]
    )

    grad_ring = ScatterRings(parts, "heads")
    while branch_ring.left > 1:
        branch_ring.advance()
    n_gate, n_out, n_mix = len(gate_scatter.moving), len(out_scatter.moving), len(mix_scatter.moving)
    ready, *arrived = branch_ring.advance(
        stand(parts[0][0]), *gate_scatter.moving, *out_scatter.moving, *mix_scatter.moving, *small_moving
    )
    from_gate, arrived = arrived[:n_gate], arrived[n_gate:]
    from_out, arrived = arrived[:n_out], arrived[n_out:]
    mix_scatter.relay(arrived[:n_mix], ready)
    small_grads = doubled(sum(arrived[n_mix:], small_grads), "heads", 1)
    gate_cols = to_heads(gate_scatter.all(from_gate, BF, ready).reshape(heads, w_rows, own))
    out_scatter.relay(from_out, ready)
    for step in range(1, steps):
        if step == 1:
            grad_ring.advance()
        elif step == 2:
            small_grads, *arrived = grad_ring.advance(small_grads, *mix_scatter.moving)
            small_grads = doubled(small_grads, "heads", 2)
            mix_cols = mix_scatter.all(arrived, BF, stand(grad_ring.last))
            mix_cols = to_heads(mix_cols.reshape(heads, w_rows, -1))
        elif step == 3:
            small_grads, *branch_sums = grad_ring.advance(small_grads, *branch_ring.sums)
            for bits in powers("heads")[2:]:
                small_grads = doubled(small_grads, "heads", bits)
            output = output_of(where, sums, hidden, (*branch[0], *branch_sums, stand(grad_ring.last)))
        else:
            grad_ring.advance()
    output, *arrived = grad_ring.advance(output, *out_scatter.moving)
    own_parts = [part for k in range(2) for part in (parts[0][k], *grad_ring.sums[k])]
    input_grad = input_grad_of(where, dp, own_parts, hidden, cotangent, norm_row)
    if not arrived:
        arrived = [jnp.zeros(w_out.shape, BF)]
    if striped:
        w_out_grad, out_sums = out_grad_of(arrived[0], out_scatter.sums[0], w_out)
    else:
        w_out_grad = add_last(arrived[0], out_scatter.sums[0], F32, ())
        w_out_grad = lax.ppermute(w_out_grad, ("dp", "heads"), [(dst, src) for src, dst in route])
        out_sums = jnp.sum(w_out.astype(F32) * w_out_grad, axis=1, keepdims=True)
    gate_w_grad = out_sums[:, 0] / gate_w.astype(F32)
    w_in_grad, norm_sums = weight_rows(dp, striped, gate_cols, mix_cols, w_in)
    norm_w_grad = norm_sums[:, 0] / norm_w.astype(F32)

    taps_grad, bias_grad, by_head = collect(where, dp, heads, striped, taps_dev, small_grads)
    return (
        output,
        input_grad,
        norm_w_grad,
        w_in_grad,
        taps_grad,
        bias_grad.reshape(-1),
        by_head[Small.BIAS_GRAD, :own_heads],
        by_head[Small.LOG_GRAD, :own_heads],
        by_head[Small.SKIP_GRAD, :own_heads],
        gate_w_grad,
        w_out_grad,
    )


def solution(mesh):
    both = ("dp", "heads")
    placed = (
        P(both, None),
        P("dp", None),
        P(both),
        P(both, None),
        P(None, both),
        P(both),
        P("heads"),
        P("heads"),
        P("heads"),
        P(both),
        P(both, None),
        P(both, None),
    )
    return jax.shard_map(
        shards,
        mesh=mesh,
        in_specs=placed,
        out_specs=(
            P(both, None),
            P(both, None),
            P(both),
            P(both, None),
            P(None, both),
            P(both),
            P("heads"),
            P("heads"),
            P("heads"),
            P(both),
            P(both, None),
        ),
        check_vma=False,
    )
```

```python
import functools

import numpy as np

import jax
import jax.numpy as jnp
from jax import lax
from jax.experimental import pallas as pl
from jax.experimental.pallas import tpu as pltpu
from jax.sharding import PartitionSpec as P

P_SIZE = 64
N = 128
CONV_K = 4
BLOCK_LEN = 256
SEQS = 3
DI = 4096
CONV_CH = 4352
LANE = 128
EPS = 1e-05
ROWS = 512
RING = SEQS
SCAN_VMEM = 20 * 2**20

NO_COST = pl.CostEstimate(flops=0, bytes_accessed=0, transcendentals=0)
BF = jnp.bfloat16
F32 = jnp.float32


def ring_order(n):
    return list(range(0, n, 2)) + list(range(n - 1, 0, -2))


def where_vector(ends):
    heads, dp = lax.axis_size("heads"), lax.axis_size("dp")
    order = ring_order(heads)
    ring = np.zeros((heads, heads), np.int32)
    for position, index in enumerate(order):
        ring[index] = [order[(position + distance) % heads] for distance in range(heads)]
    owners = np.array([dp_owners(dp, me) for me in range(dp)], np.int32)
    return jnp.concatenate(
        [ends, jnp.asarray(ring)[lax.axis_index("heads")], jnp.asarray(owners)[lax.axis_index("dp")]]
    )


def ring_route(n, step):
    order = ring_order(n)
    return [(order[i], order[(i + step) % n]) for i in range(n)]


def xor_route(n, bits):
    return [(i, i ^ bits) for i in range(n)]


def together(*values):
    return list(lax.optimization_barrier(values))


def together_with(moving, others):
    values = together(*moving.values(), *others)
    return dict(zip(moving, values)), values[len(moving) :]


class GatherRing:
    def __init__(self, rows, axis):
        self.axis, self.n = axis, lax.axis_size(axis)
        self.half = self.n // 2
        self.step = 0
        self.arrived = {0: [rows]}
        self.moving = {way: self.sent(rows, way) for way in (1, -1)}

    def sent(self, value, way):
        return lax.ppermute(value, self.axis, ring_route(self.n, way))

    def advance(self, *others):
        self.step += 1
        moving, others = together_with(self.moving, others)
        self.moving = {}
        if self.step == self.half:
            self.arrived[self.half] = [moving[1], moving[-1]]
            return others
        for way, value in moving.items():
            self.arrived[-way * self.step % self.n] = [value]
        if self.step == self.half - 1:
            moving = dict(zip((1, -1), halves(moving[1], moving[-1])))
        for way, value in moving.items():
            self.moving[way] = self.sent(value, way)
        return others

    def all(self):
        return [self.arrived[d] for d in range(self.n)]


class ScatterRing:
    def __init__(self, parts, axis):
        self.axis, self.n = axis, lax.axis_size(axis)
        self.half = self.n // 2
        self.parts = parts
        self.left = self.half
        self.moving = {1: self.sent(parts[self.half][0], 1), -1: self.sent(parts[self.half][1], -1)}

    def sent(self, value, way):
        return lax.ppermute(value, self.axis, ring_route(self.n, way))

    def advance(self, *others):
        self.left -= 1
        moving, others = together_with(self.moving, others)
        if not self.left:
            self.sums = [moving[1], moving[-1]]
            return others
        for way, value in moving.items():
            (part,) = self.parts[way * self.left % self.n]
            total = add_rows(value, part, 0 if way == 1 else part.shape[0] - value.shape[0])
            self.moving[way] = self.sent(total, way)
        return others


class ScatterRings:
    def __init__(self, parts, axis):
        self.axis, self.n = axis, lax.axis_size(axis)
        self.half = self.n // 2
        self.parts = parts
        self.left = self.half
        self.sums = [[], []]
        self.moving = {}
        for chunk, way in ((0, 1), (1, -1)):
            self.send(chunk, way, parts[self.half][chunk])

    def send(self, chunk, way, value):
        self.moving[chunk, way] = lax.ppermute(value, self.axis, ring_route(self.n, way))

    def advance(self, *others):
        self.left -= 1
        moving, others = together_with(self.moving, others)
        self.moving = {}
        for (chunk, way), value in moving.items():
            if self.left:
                value = add_rows(value, self.parts[way * self.left % self.n][chunk], 0)
                self.send(chunk, way, value)
                self.last = value
            else:
                self.sums[chunk].append(value)
        if self.left == self.half - 1:
            for chunk, way in ((1, 1), (0, -1)):
                self.send(chunk, way, self.parts[way * self.left % self.n][chunk])
        return others


def dp_owners(n, me):
    return [((me - 2 * s) % n) ^ b for b in range(2) for s in range(n // 2)]


def next_chip(value):
    n = lax.axis_size("dp")
    return lax.ppermute(value, "dp", [(i, (i + 2) % n) for i in range(n)])


def other_core(value):
    return lax.ppermute(value, "dp", xor_route(lax.axis_size("dp"), 1))


class GatherDp:
    def __init__(self, block):
        self.chips = lax.axis_size("dp") // 2
        self.near, self.far = [block], [other_core(block)]
        self.moving = [next_chip(block)] if self.chips > 1 else []

    def relay(self, arrived):
        for step in range(1, self.chips):
            (value,) = arrived if step == 1 else self.moving
            self.near.append(value)
            self.far.append(other_core(value))
            self.moving = [next_chip(value)] if step + 1 < self.chips else []

    def all(self, arrived):
        return self.near + list(arrived)


class ScatterDp:
    def __init__(self, kept, given):
        self.chips = lax.axis_size("dp") // 2
        self.kept = kept
        self.moving = [other_core(given)]

    def relay(self, arrived, *after):
        self.sums = add_core(self.kept, arrived[0], self.chips, after)
        self.moving = [next_chip(self.sums[1])] if self.chips > 1 else []
        for step in range(2, self.chips):
            value = self.moving[0].astype(F32)
            self.moving = [next_chip((value + self.sums[step]).astype(BF))]

    def all(self, arrived, dtype, *after):
        if self.chips == 1:
            return self.sums[0].astype(dtype)
        return add_last(arrived[0], self.sums[0], dtype, after)


def doubled(block, axis, bits):
    return join([block, lax.ppermute(block, axis, xor_route(lax.axis_size(axis), bits))])


def pairs(block, axis):
    n = lax.axis_size(axis)
    return [block] + [lax.ppermute(block, axis, xor_route(n, bits)) for bits in range(2, n, 2)]


def powers(axis):
    return [1 << k for k in range(lax.axis_size(axis).bit_length() - 1)]


def vmem_of(arrays, specs, rest):
    total = rest
    for array, spec in zip(arrays, specs):
        if spec.block_shape is not None:
            copies = 1 if spec.pipeline_mode else 2
            total += copies * int(np.prod(spec.block_shape)) * array.dtype.itemsize
    return total


def call_kernel(body, scalars, grid, ins, in_specs, outs, out_specs, name, scratch=(), flops=0, rest=6 * 2**20, after=()):
    count = 1 + len(ins)
    inner = body
    if after:

        def body(*refs):
            inner(*refs[:count], *refs[count + len(after) :])

    ins = (*ins, *after)
    in_specs = [*in_specs, *(whole(a) for a in after)]
    bytes_moved = sum(int(np.prod(a.shape)) * a.dtype.itemsize for a in outs)
    return pl.pallas_call(
        body,
        grid_spec=pltpu.PrefetchScalarGridSpec(
            num_scalar_prefetch=1, grid=grid, in_specs=in_specs, out_specs=out_specs, scratch_shapes=scratch
        ),
        out_shape=outs,
        compiler_params=pltpu.CompilerParams(
            vmem_limit_bytes=vmem_of((*ins, *outs), (*in_specs, *out_specs), rest)
        ),
        cost_estimate=pl.CostEstimate(flops=flops, bytes_accessed=0, transcendentals=0),
        name=name,
    )(scalars, *ins)


def whole(array):
    return pl.BlockSpec(array.shape, lambda *i: (0, 0))


def once(array):
    return pl.BlockSpec(array.shape, lambda *i: (0, 0), pipeline_mode=pl.Buffered(1))


def rows_of(width, rows=ROWS):
    return pl.BlockSpec((rows, width), lambda i, s: (i, 0))


def call_whole(body, ins, outs, name, rest=2**20):
    specs = [pl.BlockSpec(memory_space=pltpu.VMEM)] * len(ins), [pl.BlockSpec(memory_space=pltpu.VMEM)] * len(outs)
    held = sum(int(np.prod(a.shape)) * a.dtype.itemsize for a in (*ins, *outs))
    return pl.pallas_call(
        body,
        in_specs=specs[0],
        out_specs=specs[1],
        out_shape=outs,
        compiler_params=pltpu.CompilerParams(vmem_limit_bytes=held + rest),
        cost_estimate=NO_COST,
        name=name,
    )(*ins)


def halves_kernel(first, second, top, bottom):
    rows = top.shape[0]
    top[...] = first[:rows, :]
    bottom[...] = second[rows:, :]


def halves(first, second):
    out = jax.ShapeDtypeStruct((first.shape[0] // 2, first.shape[1]), first.dtype)
    return call_whole(halves_kernel, (first, second), [out, out], "halves")


def stand_kernel(value, out):
    out[...] = value[0:8, :].astype(F32)


def stand(value):
    flat = value.reshape(-1, value.shape[-1])
    rows = min(16, flat.shape[0])
    return pl.pallas_call(
        stand_kernel,
        grid=(1,),
        in_specs=[pl.BlockSpec((rows, LANE), lambda i: (0, 0))],
        out_specs=pl.BlockSpec((8, LANE), lambda i: (0, 0)),
        out_shape=jax.ShapeDtypeStruct((8, LANE), F32),
        compiler_params=pltpu.CompilerParams(vmem_limit_bytes=2**20),
        cost_estimate=NO_COST,
        name="stand",
    )(flat)


def join_kernel(*refs):
    *blocks, out = refs
    first = 0
    for block in blocks:
        out[first : first + block.shape[0], :] = block[...]
        first += block.shape[0]


def join(blocks):
    rows = sum(block.shape[0] for block in blocks)
    out = jax.ShapeDtypeStruct((rows, blocks[0].shape[1]), blocks[0].dtype)
    return call_whole(join_kernel, blocks, [out], "join")[0]


def add_rows_kernel(place, sent, part, out):
    rows = sent.shape[0]
    if rows < out.shape[0]:
        out[...] = part[...]
    at = slice(place, place + rows)
    out[at, :] = (sent[...].astype(F32) + part[at, :].astype(F32)).astype(BF)


def add_rows(sent, part, place):
    body = functools.partial(add_rows_kernel, place)
    return call_whole(body, (sent, part), [jax.ShapeDtypeStruct(part.shape, BF)], "add_rows")[0]


def add_core_kernel(chips, kept, given, *refs):
    outs = refs[-chips:]
    rows = outs[0].shape[0]
    for k, out in enumerate(outs):
        at = slice(k * rows, (k + 1) * rows)
        out[...] = (kept[at, :].astype(F32) + given[at, :].astype(F32)).astype(out.dtype)


def add_core(kept, given, chips, after):
    rows, cols = kept.shape[0] // chips, kept.shape[1]
    outs = [jax.ShapeDtypeStruct((rows, cols), BF if k == 1 else F32) for k in range(chips)]
    return call_whole(functools.partial(add_core_kernel, chips), (kept, given, *after), outs, "add_core")


def add_last_kernel(arrived, kept, *refs):
    out = refs[-1]
    out[...] = (arrived[...].astype(F32) + kept[...]).astype(out.dtype)


def add_last(arrived, kept, dtype, after):
    return call_whole(add_last_kernel, (arrived, kept, *after), [jax.ShapeDtypeStruct(kept.shape, dtype)], "add_last")[0]


def weight_term(left, right):
    half = left.shape[1] // 2
    given = mm(left[:, half:], right, ((0,), (0,))).astype(BF)
    kept = mm(left[:, :half], right, ((0,), (0,))).astype(BF)
    return kept, given


class Small:
    BIAS, NORM, GATE, HEADS = CONV_K, CONV_K + 1, CONV_K + 2, CONV_K + 3
    SKIP_GRAD, BIAS_GRAD, LOG_GRAD = CONV_K + 1, CONV_K + 2, CONV_K + 3


def pack_small(conv_w, conv_b, norm_w, gate_w, dt_bias, a_log, skip_gain):
    per_head = jnp.concatenate([dt_bias, a_log, skip_gain])
    rows = [conv_w] + [row.reshape(1, -1) for row in (conv_b, norm_w, gate_w, per_head)]
    lanes = max(row.shape[1] for row in rows)
    lanes = -(-lanes // LANE) * LANE
    return jnp.concatenate([jnp.pad(row.astype(F32), ((0, 0), (0, lanes - row.shape[1]))) for row in rows])


def lanes_of(width):
    return lax.broadcasted_iota(jnp.int32, (8, width), 1)


def own_blocks(dp, heads, head, own, striped):
    if striped:
        size = own // dp
        return [(j * heads + head) * size for j in range(dp)], size
    return [head * own], own


def unpack_kernel(dp, heads, per_device, striped, where, table, taps, gate, norm, head_rows, skip):
    own = gate.shape[1]
    my_head, my_dp = where[RING], where[RING + heads]
    lanes = table.shape[1]

    def tile(at_dp, at_head):
        slot = (at_dp ^ my_dp) * heads + (at_head ^ my_head)
        return table[pl.ds(pl.multiple_of(slot * 8, 8), 8), :]

    def run(first, width):
        lane = lanes_of(LANE)
        start = first // width
        shift = first - start * width
        total = jnp.zeros((8, LANE), F32)
        for k in range((LANE + width - 2) // width + 1):
            device = jnp.minimum(start + k, dp * heads - 1)
            moved = pltpu.roll(tile(device // heads, device % heads), (k * width - shift) % lanes, 1)[:, :LANE]
            source = lane - k * width + shift
            total = jnp.where((source >= 0) & (source < width), moved, total)
        return total

    blocks, size = own_blocks(dp, heads, my_head, own, striped)
    conv_width, norm_width, gate_width = per_device
    at = 0
    for first in blocks:
        for more in range(0, size, LANE):
            taps[:, at : at + LANE] = run(first + more, conv_width)
            gate[:, at : at + LANE] = run(first + more, gate_width)
            at += LANE
    for more in range(0, 2 * N, LANE):
        taps[:, own + more : own + more + LANE] = run(jnp.int32(DI + more), conv_width)
    for more in range(0, norm.shape[1], LANE):
        norm[:, more : more + LANE] = run(jnp.int32(more), norm_width)
    lane = lanes_of(LANE)
    own_heads = own // P_SIZE
    found = [jnp.zeros((8, LANE), F32)] * 3
    for k in range(own_heads):
        each = own_heads // len(blocks)
        head = blocks[k // each] // P_SIZE + k % each
        device = head // own_heads
        values = tile(my_dp, device)
        for kind in range(3):
            source = kind * own_heads + head - device * own_heads
            moved = pltpu.roll(values, (k - source + lanes) % lanes, 1)[:, :LANE]
            found[kind] = jnp.where(lane == k, moved, found[kind])
    row = slice(Small.HEADS, Small.HEADS + 1)
    head_rows[...] = jnp.zeros_like(head_rows)
    head_rows[0:1, :] = found[0][row, :]
    head_rows[1:2, :] = jnp.where(lane[0:1, :] < own_heads, -jnp.exp(found[1][row, :]), 0.0)
    head_of = lax.broadcasted_iota(jnp.int32, (LANE, own), 1) // P_SIZE
    spread = (head_of == lax.broadcasted_iota(jnp.int32, (LANE, own), 0)).astype(F32).astype(BF)
    skip[...] = split_times(found[2], spread, 3)


def unpack(where, dp, heads, striped, own, width, per_device, table):
    outs = [jax.ShapeDtypeStruct((8, w), F32) for w in (own + 2 * N, own, width, LANE, own)]
    return call_kernel(
        functools.partial(unpack_kernel, dp, heads, per_device, striped),
        where,
        (1,),
        (table,),
        [whole(table)],
        outs,
        [whole(o) for o in outs],
        "unpack",
    )


def collect_kernel(dp, heads, striped, taps_dev, where, table, taps, bias, head_out, full, by_head):
    chans = table.shape[1]
    own = chans - 2 * N
    own_heads = own // P_SIZE
    my_head, my_dp = where[RING], where[RING + heads]

    def slot(at_head):
        return pl.multiple_of((at_head ^ my_head) * 8, 8)

    full[...] = jnp.zeros_like(full)
    shared = jnp.zeros((8, 2 * N), F32)
    chan_head = lax.broadcasted_iota(jnp.int32, (own, LANE), 0) // P_SIZE
    gather = (chan_head == lax.broadcasted_iota(jnp.int32, (own, LANE), 1)).astype(F32).astype(BF)
    row = lax.broadcasted_iota(jnp.int32, (8, LANE), 0)
    for head in range(heads):
        tile = table[pl.ds(slot(head), 8), :]
        blocks, size = own_blocks(dp, heads, head, own, striped)
        for k, first in enumerate(blocks):
            full[:, first : first + size] = tile[:, k * size : (k + 1) * size]
        shared = shared + tile[:, own:]
        summed = split_times(tile[:, :own], gather, 3)
        by_head[head * 8 : (head + 1) * 8, :] = jnp.where(row == Small.SKIP_GRAD, summed, tile[:, :LANE])
    full[:, DI : DI + 2 * N] = shared
    first = (my_dp * heads + my_head) * taps_dev
    start = first // LANE
    window = -(-(taps_dev + LANE) // LANE) * LANE
    rows = full[:, pl.ds(pl.multiple_of(start * LANE, LANE), window)]
    rows = pltpu.roll(rows, (window - (first - start * LANE)) % window, 1)[:, :taps_dev]
    taps[...] = rows[:CONV_K, :]
    bias[...] = rows[CONV_K : CONV_K + 1, :]
    lane = lanes_of(LANE)
    total = jnp.zeros((8, LANE), F32)
    per_block = own_heads // dp if striped else own_heads
    for k in range(own_heads):
        head = my_head * own_heads + k
        block = head // per_block
        owner = block % heads
        source = block // heads * per_block + head % per_block
        values = by_head[pl.ds(pl.multiple_of(owner * 8, 8), 8), :]
        total = jnp.where(lane == k, pltpu.roll(values, (k - source + LANE) % LANE, 1), total)
    head_out[...] = total


def collect(where, dp, heads, striped, taps_dev, table):
    outs = [jax.ShapeDtypeStruct(shape, F32) for shape in ((CONV_K, taps_dev), (1, taps_dev), (8, LANE))]
    window = -(-(taps_dev + LANE) // LANE) * LANE
    return call_kernel(
        functools.partial(collect_kernel, dp, heads, striped, taps_dev),
        where,
        (1,),
        (table,),
        [whole(table)],
        outs,
        [whole(o) for o in outs],
        "collect",
        scratch=[pltpu.VMEM((8, CONV_CH + window), F32), pltpu.VMEM((8 * heads, LANE), F32)],
    )


def ring_rows(arrived):
    found = []
    for distance, arrays in enumerate(arrived):
        first = 0
        for array in arrays:
            found.append((distance, first, array))
            first += array.shape[0]
    return found


def place_kernel(places, where, *refs):
    count = len(places)
    out, sems = refs[-2:]
    rows_dev = max(first + ref.shape[0] for (_, first), ref in zip(places, refs))
    copies = []
    for k, ((distance, first), ref) in enumerate(zip(places, refs[:count])):
        to = pl.multiple_of(where[RING + distance] * rows_dev + first, ref.shape[0])
        copies.append(pltpu.make_async_copy(ref, out.at[pl.ds(to, ref.shape[0]), :], sems.at[k]))
    for copy in copies:
        copy.start()
    for copy in copies:
        copy.wait()


def place(where, found, buffer, length, after=()):
    places, arrays = [f[:2] for f in found], [f[2] for f in found]
    held = () if buffer is None else (buffer,)
    anywhere = pl.BlockSpec(memory_space=pl.ANY)
    ins = (*arrays, *held, *after)
    return pl.pallas_call(
        functools.partial(place_kernel, places),
        grid_spec=pltpu.PrefetchScalarGridSpec(
            num_scalar_prefetch=1,
            grid=(1,),
            in_specs=[anywhere] * len(ins),
            out_specs=anywhere,
            scratch_shapes=[pltpu.SemaphoreType.DMA((len(arrays),))],
        ),
        out_shape=jax.ShapeDtypeStruct((length, arrays[0].shape[1]), arrays[0].dtype),
        input_output_aliases={1 + len(arrays): 0} if held else {},
        compiler_params=pltpu.CompilerParams(vmem_limit_bytes=2**20),
        cost_estimate=NO_COST,
        name="place",
    )(where, *ins)


def project_kernel(heads, dp, where, gain, rows, *refs):
    pieces, (normed, out) = refs[:dp], refs[-2:]
    width = rows.shape[1]
    piece = width // dp
    values = rows[...].astype(F32)
    scale = lax.rsqrt(jnp.sum(values * values, axis=-1, keepdims=True) / width + EPS)
    total = None
    for b in range(dp):
        at = pl.ds(pl.multiple_of(where[RING + heads + b] * piece, LANE), piece)
        low = (rows[:, at].astype(F32) * scale * gain[Small.NORM : Small.NORM + 1, at]).astype(BF)
        normed[:, b * piece : (b + 1) * piece] = low
        term = mm(low, pieces[b][...])
        total = term if b == 0 else total + term
    out[...] = total


def project(where, heads, gain, rows, pieces):
    length, width = rows.shape
    cols = pieces[0].shape[1]
    dp = len(pieces)
    return call_kernel(
        functools.partial(project_kernel, heads, dp),
        where,
        (length // ROWS,),
        (gain, rows, *pieces),
        [once(gain), rows_of(width)] + [once(p) for p in pieces],
        [jax.ShapeDtypeStruct((length, width), BF), jax.ShapeDtypeStruct((length, cols), F32)],
        [rows_of(width), rows_of(cols)],
        "project",
        flops=2 * length * width * cols,
        rest=12 * 2**20,
    )


def gate_forward_kernel(dp, first, places, where, rows, scan, gain, *refs):
    gate_pieces, out_pieces, (gate_out, w_full, *parts) = refs[:dp], refs[dp : 2 * dp], refs[2 * dp :]
    depth, each = gate_pieces[0].shape[0], out_pieces[0].shape[0]

    @pl.when(pl.program_id(0) == 0)
    def _():
        for k in range(dp):
            w_full[pl.ds(pl.multiple_of(where[first + k] * each, each), each), :] = out_pieces[k][...]

    gate = mm(rows[:, :depth], gate_pieces[0][...])
    for k in range(1, dp):
        gate = gate + mm(rows[:, k * depth : (k + 1) * depth], gate_pieces[k][...])
    gate_out[...] = gate
    inner = scan[...].astype(F32) * (gate / (1.0 + jnp.exp(-gate)))
    branch = mm((inner * gain[Small.GATE : Small.GATE + 1, :]).astype(BF), w_full[...]).astype(BF)
    put_parts(where, branch, parts, places)


def part_places(heads, rows_dev, halves):
    places = []
    for distance in range(heads):
        count = 2 if distance in halves else 1
        places += [(distance, k * rows_dev // count, rows_dev // count) for k in range(count)]
    return places


def by_distance(places, parts):
    found = {}
    for (distance, _, _), part in zip(places, parts):
        found.setdefault(distance, []).append(part)
    return found


def put_parts(where, block, parts, places):
    size = block.shape[0]
    rows_dev = max(first + rows for _, first, rows in places)
    for (distance, first, rows), part in zip(places, parts):
        start = where[RING + distance] * rows_dev + first - pl.program_id(0) * size
        for at in range(0, size, rows):

            @pl.when(start == at)
            def _(part=part, at=at, rows=rows):
                part[...] = block[at : at + rows, :]


def gate_forward(where, heads, normed, scanned, gain, gate_pieces, out_pieces, after):
    length, width = normed.shape
    own, cols = scanned.shape[1], out_pieces[0].shape[1]
    dp = len(gate_pieces)
    full = jax.ShapeDtypeStruct((own, cols), BF)
    first = where.shape[0] - dp
    places = part_places(heads, length // heads, (heads // 2,))
    parts = [jax.ShapeDtypeStruct((rows, cols), BF) for _, _, rows in places]

    gate, full, *parts = call_kernel(
        functools.partial(gate_forward_kernel, dp, first, places),
        where,
        (length // ROWS,),
        (normed, scanned, gain, *gate_pieces, *out_pieces),
        [rows_of(width), rows_of(own)] + [once(a) for a in (gain, *gate_pieces, *out_pieces)],
        [jax.ShapeDtypeStruct((length, own), F32), full, *parts],
        [rows_of(own)] + [once(a) for a in (full, *parts)],
        "gate_forward",
        rest=10 * 2**20,
        after=after,
    )
    return gate, full, by_distance(places, parts)


def gate_sums_kernel(heads, places, where, w_full, scan, gate_in, gain, *refs):
    chunks, (cot, weighted_out, sums) = refs[: len(places)], refs[-3:]
    rows_dev = cot.shape[0] // heads
    block = scan.shape[0]

    @pl.when(pl.program_id(0) == 0)
    def _():
        for (distance, first), ref in zip(places, chunks):
            rows = ref.shape[0]
            to = pl.multiple_of(where[RING + distance] * rows_dev + first, rows)
            live = to + row_ids(rows) < where[SEQS - 1]
            values = ref[...]
            cot[pl.ds(to, rows), :] = jnp.where(live, values, jnp.zeros_like(values))

    mine = pl.ds(pl.multiple_of(pl.program_id(0) * block, block), block)
    weighted = mm(cot[mine, :], w_full[...], ((1,), (1,))) * gain[Small.GATE : Small.GATE + 1, :]
    weighted_out[...] = weighted
    gate = gate_in[...]
    inner = scan[...].astype(F32) * (gate / (1.0 + jnp.exp(-gate)))
    lane = lax.broadcasted_iota(jnp.int32, (1, LANE), 1)
    squares = jnp.sum(inner * inner, axis=1, keepdims=True)
    along = jnp.sum(inner * weighted, axis=1, keepdims=True)
    both = jnp.where(lane == 0, squares, jnp.where(lane == 1, along, 0.0))
    sums[...] = both.T[0:8, :]


def gate_sums(where, arrived, w_full, scanned, gate, gain, after):
    found = ring_rows(arrived)
    places, chunks = [f[:2] for f in found], [f[2] for f in found]
    own, cols = w_full.shape
    length = scanned.shape[0]
    heads = len(arrived)

    def body(*refs):
        gate_sums_kernel(heads, places, *refs)

    cot = jax.ShapeDtypeStruct((length, cols), BF)
    return call_kernel(
        body,
        where,
        (length // ROWS,),
        (w_full, scanned, gate, gain, *chunks),
        [once(w_full), rows_of(own), rows_of(own), once(gain)] + [once(c) for c in chunks],
        [cot, jax.ShapeDtypeStruct((length, own), F32), jax.ShapeDtypeStruct((8, length), F32)],
        [once(cot), rows_of(own), pl.BlockSpec((8, ROWS), lambda i, s: (0, i))],
        "gate_sums",
        after=after,
        flops=2 * length * own * cols,
    )


def gate_backward_kernel(first, block, where, sums, weighted, scan, gate_in, gain, scan_out, gate_out, gated, held):
    columns = sums[...].T
    ratio = lax.rsqrt(columns[:, 0:1] / DI + EPS)
    pull = ratio * ratio * ratio * columns[:, 1:2] / DI
    gate = gate_in[...]
    sig = 1.0 / (1.0 + jnp.exp(-gate))
    act = gate * sig
    scanned = scan[...].astype(F32)
    inner = scanned * act
    grad = ratio * weighted[...] - pull * inner
    scan_out[...] = (grad * act).astype(BF)
    gate_out[...] = (grad * scanned * (sig * (1.0 + gate * (1.0 - sig)))).astype(BF)
    held[...] = (ratio * inner * gain[Small.GATE : Small.GATE + 1, :]).astype(BF)
    for k in range(gated.shape[1] // block):
        at = slice(k * block, (k + 1) * block)
        if block < gated.shape[1]:
            gated[:, at] = held[:, pl.ds(pl.multiple_of(where[first + k] * block, LANE), block)]
        else:
            gated[...] = held[...]


def gate_backward(where, dp, striped, sums, weighted, scanned, gate, gain):
    length, own = scanned.shape
    return call_kernel(
        functools.partial(gate_backward_kernel, where.shape[0] - dp, own // dp if striped else own),
        where,
        (length // ROWS,),
        (sums, weighted, scanned, gate, gain),
        [pl.BlockSpec((8, ROWS), lambda i, s: (0, i))] + [rows_of(own)] * 3 + [whole(gain)],
        [jax.ShapeDtypeStruct((length, own), BF)] * 3,
        [rows_of(own)] * 3,
        "gate_backward",
        scratch=[pltpu.VMEM((ROWS, own), BF)],
    )


def project_back_kernel(dp, places, where, gate_rows, mix_rows, *refs):
    gate_pieces, mix_pieces, parts, out = refs[:dp], refs[dp : 2 * dp], refs[2 * dp : -1], refs[-1]
    depth = gate_pieces[0].shape[0]
    for k in range(dp):
        total = mm(mix_rows[...], mix_pieces[k][...], ((1,), (1,)))
        total = total + mm(gate_rows[...], gate_pieces[k][...], ((1,), (1,)))
        out[:, k * depth : (k + 1) * depth] = total.astype(BF)
    put_parts(where, out, parts, places)


def project_back(where, heads, grad_gate, grad_mix, gate_pieces, mix_pieces, after):
    length, own = grad_gate.shape
    cols = grad_mix.shape[1]
    pieces = (*gate_pieces, *mix_pieces)
    dp = len(gate_pieces)
    width = dp * gate_pieces[0].shape[0]
    places = part_places(heads, length // heads, range(heads))
    parts = [jax.ShapeDtypeStruct((rows, width), BF) for _, _, rows in places]
    parts = call_kernel(
        functools.partial(project_back_kernel, dp, places),
        where,
        (length // ROWS,),
        (grad_gate, grad_mix, *pieces),
        [rows_of(own), rows_of(cols)] + [once(p) for p in pieces],
        parts,
        [once(p) for p in parts],
        "project_back",
        after=after,
        scratch=[pltpu.VMEM((ROWS, width), BF)],
        rest=10 * 2**20,
    )
    return by_distance(places, parts)


def input_grad_kernel(dp, first, where, *refs):
    parts, (hidden, cot, gain, out, total) = refs[:-5], refs[-5:]
    rows, width = parts[0].shape
    piece = width // dp
    for k in range(2):
        at = slice(k * rows, (k + 1) * rows)
        own, ahead, behind = parts[3 * k : 3 * k + 3]
        grad = own[...].astype(F32) + ahead[...].astype(F32) + behind[...].astype(F32)
        for b in range(dp):
            to = pl.ds(pl.multiple_of(where[first + b] * piece, LANE), piece)
            total[at, to] = grad[:, b * piece : (b + 1) * piece]
    values = hidden[...].astype(F32)
    scale = lax.rsqrt(jnp.sum(values * values, axis=-1, keepdims=True) / width + EPS)
    grad = total[...] * gain[Small.NORM : Small.NORM + 1, :]
    along = jnp.sum(values * grad, axis=-1, keepdims=True) / width
    out[...] = cot[...].astype(F32) + scale * (grad - values * (scale * scale * along))


def input_grad_of(where, dp, parts, hidden, cot, gain):
    first = where.shape[0] - dp
    ins = (*parts, hidden, cot, gain)
    return call_kernel(
        functools.partial(input_grad_kernel, dp, first),
        where,
        (1,),
        ins,
        [once(a) for a in ins],
        [jax.ShapeDtypeStruct(hidden.shape, F32)],
        [once(hidden)],
        "input_grad",
        scratch=[pltpu.VMEM(hidden.shape, F32)],
    )[0]


def output_kernel(where, sums, hidden, own, ahead, behind, *refs):
    out = refs[-1]
    rows = hidden.shape[0]
    branch = own[...].astype(F32) + ahead[...].astype(F32) + behind[...].astype(F32)
    live = where[RING] * rows + row_ids(rows) < where[SEQS - 1]
    ratio = jnp.where(live, lax.rsqrt(sums[...].T[:, 0:1] / DI + EPS), 0.0)
    out[...] = (hidden[...].astype(F32) + ratio * branch).astype(BF)


def output_of(where, sums, hidden, parts):
    rows = hidden.shape[0]
    return call_kernel(
        output_kernel,
        where,
        (1,),
        (sums, hidden, *parts),
        [pl.BlockSpec((8, rows), lambda i, s: (0, s[RING]))] + [once(a) for a in (hidden, *parts)],
        [jax.ShapeDtypeStruct(hidden.shape, BF)],
        [once(hidden)],
        "output",
    )[0]


def out_grad_kernel(arrived, kept, w_out, out, sums):
    total = arrived[...].astype(F32) + kept[...]
    out[...] = total
    sums[...] = jnp.sum(total * w_out[...].astype(F32), axis=1, keepdims=True) + jnp.zeros(sums.shape, F32)


def out_grad_of(arrived, kept, w_out):
    outs = [jax.ShapeDtypeStruct(w_out.shape, F32), jax.ShapeDtypeStruct((w_out.shape[0], LANE), F32)]
    return call_whole(out_grad_kernel, (arrived, kept, w_out), outs, "out_grad", rest=4 * 2**20)


def weight_rows_kernel(dp, striped, gate_cols, mix_cols, w_in, out, norm_out):
    heads, rows, own = gate_cols.shape
    own_heads = own // P_SIZE
    chans = own + 2 * N
    norm = jnp.zeros((rows, 1), F32)

    def put(first, values):
        nonlocal norm
        at = slice(first, first + values.shape[1])
        out[:, at] = values
        norm = norm + jnp.sum(values * w_in[:, at].astype(F32), axis=1, keepdims=True)

    shared = mix_cols[0, :, own:chans].astype(F32)
    for head in range(1, heads):
        shared = shared + mix_cols[head, :, own:chans].astype(F32)
    put(2 * DI, shared)
    steps = jnp.zeros((rows, heads * own_heads), F32)
    source = lax.broadcasted_iota(jnp.int32, (LANE, heads * own_heads), 0)
    target = lax.broadcasted_iota(jnp.int32, (LANE, heads * own_heads), 1)
    count = dp if striped else 1
    for head in range(heads):
        for block in range(count):
            size = own // count
            at = slice(block * size, (block + 1) * size)
            put((block * heads + head) * size, gate_cols[head, :, at].astype(F32))
            put(DI + (block * heads + head) * size, mix_cols[head, :, at].astype(F32))
        each = own_heads // count
        to = (source // each * heads + head) * each + source % each
        picked = ((to == target) & (source < own_heads)).astype(F32).astype(BF)
        steps = steps + mm(mix_cols[head, :, chans:], picked)
    put(DI + CONV_CH, steps)
    norm_out[...] = norm + jnp.zeros(norm_out.shape, F32)


def weight_rows(dp, striped, gate_cols, mix_cols, w_in):
    rows = w_in.shape[0]
    ins = (gate_cols, mix_cols, w_in)

    def body(*refs):
        weight_rows_kernel(dp, striped, *refs)

    return pl.pallas_call(
        body,
        out_shape=[jax.ShapeDtypeStruct(w_in.shape, F32), jax.ShapeDtypeStruct((rows, LANE), F32)],
        compiler_params=pltpu.CompilerParams(vmem_limit_bytes=SCAN_VMEM),
        cost_estimate=NO_COST,
        name="weight_rows",
    )(*ins)


FAR = -1e30


def mm(left, right, contract=((1,), (0,))):
    return lax.dot_general(left, right, (contract, ((), ())), preferred_element_type=F32)


def row_ids(rows):
    return lax.broadcasted_iota(jnp.int32, (rows, 1), 0)


def split_sum(ones, values, count):
    parts, rest = [], values
    for _ in range(count):
        part = rest.astype(BF)
        parts.append(part)
        rest = rest - part.astype(F32)
    product = mm(ones, jnp.concatenate(parts, axis=1))
    width = values.shape[1]
    total = product[:, :width]
    for k in range(1, count):
        total = total + product[:, k * width : (k + 1) * width]
    return total


def split_times(values, ones, count):
    total, rest = jnp.zeros((values.shape[0], ones.shape[1]), F32), values
    for _ in range(count):
        part = rest.astype(BF)
        total = total + mm(part, ones)
        rest = rest - part.astype(F32)
    return total


def widen(values, spread2):
    high = values.astype(BF)
    low = (values - high.astype(F32)).astype(BF)
    return mm(jnp.concatenate([high, low], axis=1), spread2)


def segment_at(position, ends_ref):
    seg = jnp.zeros_like(position)
    start = jnp.zeros_like(position)
    for k in range(SEQS):
        end = ends_ref[k]
        seg = seg + (position >= end).astype(jnp.int32)
        start = jnp.where(position >= end, end, start)
    return seg, start


def scalar_segment(position, ends_ref):
    seg = jnp.int32(0)
    for k in range(SEQS):
        seg = seg + (position >= ends_ref[k]).astype(jnp.int32)
    return jnp.where(position < 0, -1, seg)


class Block:
    def __init__(self, index, ends_ref, dt_part, head_ref, own):
        rows = BLOCK_LEN
        first = index * rows
        seg, self.start = segment_at(first + row_ids(rows), ends_ref)
        self.position = first + row_ids(rows)
        col = lax.broadcasted_iota(jnp.int32, (1, rows), 1)
        seg_row, _ = segment_at(first + col, ends_ref)
        causal = row_ids(rows) >= col
        self.lower = jnp.where(causal, 1.0, 0.0).astype(BF)
        same = seg == seg_row
        self.penalty = jnp.where(causal & same, 0.0, FAR)
        before = scalar_segment(first - 1, ends_ref)
        last = scalar_segment(first + rows - 1, ends_ref)
        self.raw = dt_part.astype(BF).astype(F32) + head_ref[0:1, :]
        self.decay = head_ref[1:2, :]
        self.dt = jnp.maximum(self.raw, 0.0) + jnp.log1p(jnp.exp(-jnp.abs(self.raw)))
        self.cum = split_sum(self.lower, self.dt * self.decay, 3)
        final = self.cum[rows - 1 : rows, :]
        self.enter = jnp.where(seg == before, jnp.exp(self.cum), 0.0)
        self.tail = jnp.where(seg == last, jnp.exp(final - self.cum), 0.0)
        self.keep = jnp.where(before == last, jnp.exp(final), 0.0)
        head_of = lax.broadcasted_iota(jnp.int32, (LANE, own), 1) // P_SIZE
        self.spread = (head_of == lax.broadcasted_iota(jnp.int32, (LANE, own), 0)).astype(F32).astype(BF)
        spread2 = jnp.concatenate([self.spread, self.spread], axis=0)
        self.dt_wide = widen(self.dt, spread2)
        self.enter_wide = widen(self.enter, spread2)
        self.tail_wide = widen(self.tail, spread2)
        self.cum_row = self.cum.T
        chan_head = lax.broadcasted_iota(jnp.int32, (own, LANE), 0) // P_SIZE
        self.gather = (chan_head == lax.broadcasted_iota(jnp.int32, (own, LANE), 1)).astype(F32)
        self.keep_chan = jnp.sum(self.gather * self.keep, axis=1, keepdims=True)

    def gap(self, head):
        return self.cum[:, head : head + 1] - self.cum_row[head : head + 1, :]


def scan_forward_kernel(ends_ref, mix_ref, taps_ref, head_ref, skip_ref, state_in, rim_in, *refs, base):
    pre_ref, scan_ref, enter_ref, state, rim, ext = refs[-6:]
    index = base + pl.program_id(0)
    chans = pre_ref.shape[1]
    own = chans - 2 * N
    rows = BLOCK_LEN

    @pl.when(pl.program_id(0) == 0)
    def _():
        rim[...] = rim_in[...]
        state[...] = state_in[...]

    ext[0:8, :] = rim[...]
    ext[8:, :] = mix_ref[:, :chans]
    blk = Block(index, ends_ref, mix_ref[:, chans:], head_ref, own)
    total = taps_ref[CONV_K : CONV_K + 1, :] + taps_ref[CONV_K - 1 : CONV_K, :] * ext[8:, :]
    for lag in range(1, CONV_K):
        linked = (blk.position - lag >= blk.start).astype(F32)
        tap = taps_ref[CONV_K - 1 - lag : CONV_K - lag, :]
        total = total + tap * (linked * ext[8 - lag : 8 - lag + rows, :])
    rim[...] = ext[rows : rows + 8, :]
    pre_ref[...] = total
    low = (total / (1.0 + jnp.exp(-total))).astype(BF)
    x_low, b_low, c_low = low[:, :own], low[:, own : own + N], low[:, own + N :]
    x_wide = x_low.astype(F32)
    x_dt = (x_wide * blk.dt_wide).astype(BF)
    scores = mm(c_low, b_low, ((1,), (1,)))
    lane = lax.broadcasted_iota(jnp.int32, (1, LANE), 1)
    entering = state[...]
    enter_ref[...] = entering
    outer = mm(c_low, entering.astype(BF), ((1,), (1,))) * blk.enter_wide + skip_ref[Small.HEADS : Small.HEADS + 1, :] * x_wide
    for pair in range(own // LANE):
        both = x_dt[:, pair * LANE : (pair + 1) * LANE]
        parts = []
        for head in (2 * pair, 2 * pair + 1):
            mixing = scores * jnp.exp(blk.gap(head) + blk.penalty)
            parts.append(mm(mixing.astype(BF), both))
        inner = jnp.where(lane < P_SIZE, parts[0], parts[1])
        at = slice(pair * LANE, (pair + 1) * LANE)
        scan_ref[:, at] = (inner + outer[:, at]).astype(BF)
    added = mm((x_wide * blk.dt_wide * blk.tail_wide).astype(BF), b_low, ((0,), (0,)))
    state[...] = blk.keep_chan * entering + added


def scan_forward(ends, mix, taps, head_rows, skip_row, calls, after):
    length, cols = mix.shape
    chans = cols - LANE
    own = chans - 2 * N
    blocks = length // BLOCK_LEN
    each = blocks // calls
    state, rim, kept = jnp.zeros((own, N), F32), jnp.zeros((8, chans), F32), ()
    for call in range(calls):

        def rows_of(width, base=call * each, rows=BLOCK_LEN):
            return pl.BlockSpec((rows, width), lambda i, ends: (base + i, 0))

        def whole(array):
            return pl.BlockSpec(array.shape, lambda i, ends: (0, 0))

        *kept, state, rim = pl.pallas_call(
            functools.partial(scan_forward_kernel, base=call * each),
            grid_spec=pltpu.PrefetchScalarGridSpec(
                num_scalar_prefetch=1,
                grid=(each,),
                in_specs=[rows_of(cols)]
                + [whole(a) for a in (taps, head_rows, skip_row, state, rim)]
                + [pl.BlockSpec(memory_space=pl.ANY)] * len(kept)
                + [whole(a) for a in after],
                out_specs=[rows_of(chans), rows_of(own), rows_of(N, rows=own), whole(state), whole(rim)],
                scratch_shapes=[pltpu.VMEM((BLOCK_LEN + 8, chans), F32)],
            ),
            out_shape=[
                jax.ShapeDtypeStruct((length, chans), F32),
                jax.ShapeDtypeStruct((length, own), BF),
                jax.ShapeDtypeStruct((blocks * own, N), F32),
                jax.ShapeDtypeStruct(state.shape, F32),
                jax.ShapeDtypeStruct(rim.shape, F32),
            ],
            input_output_aliases={7 + k: k for k in range(len(kept))},
            compiler_params=pltpu.CompilerParams(vmem_limit_bytes=SCAN_VMEM),
            cost_estimate=pl.CostEstimate(flops=each * 2**31, bytes_accessed=0, transcendentals=0),
            name="scan_forward",
        )(ends, mix, taps, head_rows, skip_row, state, rim, *kept, *after)
    return kept


def scan_backward_kernel(
    ends_ref, pre_ref, mix_ref, dy_ref, enter_ref, taps_ref, head_ref, skip_ref, *refs, base
):
    carried, (grad_ref, *carries, ext) = refs[:3], refs[-5:]
    state, rim, small_ref = carries
    index = base - pl.program_id(0)
    chans = pre_ref.shape[1]
    own = chans - 2 * N
    rows = BLOCK_LEN

    @pl.when(pl.program_id(0) == 0)
    def _():
        for given, held in zip(carried, carries):
            held[...] = given[...]

    ext[rows:, :] = rim[...]
    blk = Block(index, ends_ref, mix_ref[:, chans:], head_ref, own)
    pre = pre_ref[...]
    sig = 1.0 / (1.0 + jnp.exp(-pre))
    low = (pre * sig).astype(BF)
    x_low, b_low, c_low = low[:, :own], low[:, own : own + N], low[:, own + N :]
    x_wide = x_low.astype(F32)
    dy = dy_ref[...]
    dy_wide = dy.astype(F32)
    x_dt = (x_wide * blk.dt_wide).astype(BF)
    entering = enter_ref[...]
    enter_low = entering.astype(BF)
    leaving = state[...]
    leaving_low = leaving.astype(BF)
    gather = blk.gather.astype(BF)

    scores = mm(c_low, b_low, ((1,), (1,)))
    scores_t = mm(b_low, c_low, ((1,), (1,)))
    penalty_t = blk.penalty.T
    lane = lax.broadcasted_iota(jnp.int32, (1, LANE), 1)
    lane_rows = lax.broadcasted_iota(jnp.int32, (rows, LANE), 1)
    sub_rows = lax.broadcasted_iota(jnp.int32, (LANE, rows), 0)
    grad_scores = jnp.zeros((rows, rows), F32)
    along_rows = jnp.zeros((rows, LANE), F32)
    along_cols = jnp.zeros((LANE, rows), F32)
    grad_xdt = []
    for pair in range(own // LANE):
        at = slice(pair * LANE, (pair + 1) * LANE)
        both, dy_both = x_dt[:, at], dy[:, at]
        parts = []
        for head in (2 * pair, 2 * pair + 1):
            gap = blk.gap(head)
            decay = jnp.exp(gap + blk.penalty)
            mixing_t = scores_t * jnp.exp(penalty_t - gap)
            parts.append(mm(mixing_t.astype(BF), dy_both))
            mine = (lane < P_SIZE) if head % 2 == 0 else (lane >= P_SIZE)
            dy_one = jnp.where(mine, dy_both, jnp.zeros_like(dy_both))
            grad_mixing = mm(dy_one, both, ((1,), (1,))) * decay
            grad_scores = grad_scores + grad_mixing
            moved = grad_mixing * scores
            along_rows = along_rows + jnp.where(lane_rows == head, jnp.sum(moved, axis=1, keepdims=True), 0.0)
            along_cols = along_cols + jnp.where(sub_rows == head, jnp.sum(moved, axis=0, keepdims=True), 0.0)
        grad_xdt.append(jnp.where(lane < P_SIZE, parts[0], parts[1]))
    grad_xdt = jnp.concatenate(grad_xdt, axis=1)
    grad_cum = along_rows - along_cols.T
    grad_low = grad_scores.astype(BF)
    grad_c = mm(grad_low, b_low)
    grad_b = mm(grad_low, c_low, ((0,), (0,)))

    dy_enter = dy_wide * blk.enter_wide
    dy_enter_low = dy_enter.astype(BF)
    seen = mm(c_low, enter_low, ((1,), (1,)))
    grad_cum = grad_cum + mm((dy_enter * seen).astype(BF), gather)
    grad_c = grad_c + mm(dy_enter_low, enter_low)
    grad_enter = mm(dy_enter_low, c_low, ((0,), (0,)))

    taken = mm(b_low, leaving_low, ((1,), (1,)))
    x_tail = x_wide * blk.tail_wide
    grad_tail = mm((x_tail * taken).astype(BF), gather)
    moved = grad_tail * blk.dt
    grad_b = grad_b + mm((x_tail * blk.dt_wide).astype(BF), leaving_low)
    kept = jnp.sum(leaving * entering, axis=1, keepdims=True) * blk.keep_chan
    grad_last = jnp.sum(moved, axis=0, keepdims=True) + jnp.sum(blk.gather * kept, axis=0, keepdims=True)
    grad_cum = grad_cum - moved + jnp.where(row_ids(rows) == rows - 1, grad_last, 0.0)
    state[...] = blk.keep_chan * leaving + grad_enter

    grad_dt = mm((x_wide * grad_xdt).astype(BF), gather) + grad_tail
    upper = (row_ids(rows) <= lax.broadcasted_iota(jnp.int32, (1, rows), 1)).astype(F32).astype(BF)
    grad_steps = split_sum(upper, grad_cum, 3)
    grad_dt = grad_dt + blk.decay * grad_steps
    grad_raw = grad_dt / (1.0 + jnp.exp(-blk.raw))
    small_ref[Small.BIAS_GRAD : Small.BIAS_GRAD + 1, :LANE] += jnp.sum(grad_raw, axis=0, keepdims=True)
    small_ref[Small.LOG_GRAD : Small.LOG_GRAD + 1, :LANE] += (
        jnp.sum(blk.dt * grad_steps, axis=0, keepdims=True) * blk.decay
    )
    small_ref[Small.SKIP_GRAD : Small.SKIP_GRAD + 1, :own] += jnp.sum(dy_wide * x_wide, axis=0, keepdims=True)

    grad_x = blk.dt_wide * (grad_xdt + blk.tail_wide * taken) + skip_ref[Small.HEADS : Small.HEADS + 1, :] * dy_wide
    grad_low = jnp.concatenate([grad_x.astype(BF).astype(F32), grad_b, grad_c], axis=1)
    grad_pre = grad_low * (sig * (1.0 + pre * (1.0 - sig)))
    ext[0:rows, :] = grad_pre
    conv_in = mix_ref[:, :chans]
    small_ref[Small.BIAS : Small.BIAS + 1, :] += jnp.sum(grad_pre, axis=0, keepdims=True)
    grad_in = jnp.zeros((rows, chans), F32)
    for lag in range(CONV_K):
        back = grad_pre if lag == 0 else ext[lag : lag + rows, :]
        if lag:
            _, start = segment_at(blk.position + lag, ends_ref)
            back = back * (blk.position >= start).astype(F32)
        tap = CONV_K - 1 - lag
        grad_in = grad_in + taps_ref[tap : tap + 1, :] * back
        small_ref[tap : tap + 1, :] += jnp.sum(conv_in * back, axis=0, keepdims=True)
    rim[...] = grad_pre[0:8, :]
    grad_ref[...] = jnp.concatenate([grad_in.astype(BF), grad_raw.astype(BF)], axis=1)


def scan_backward(ends, pre, mix, grad_scan, entering, taps, head_rows, skip_row, carries, grad, call, calls, after):
    length, cols = mix.shape
    chans = cols - LANE
    own = chans - 2 * N
    blocks = length // BLOCK_LEN
    each = blocks // calls
    last = blocks - 1 - call * each
    if call == 0:
        carries = [jnp.zeros(s, F32) for s in ((own, N), (8, chans), (8, chans))]
    held = () if call == 0 else (grad,)

    def rows_of(width, rows=BLOCK_LEN):
        return pl.BlockSpec((rows, width), lambda i, ends: (last - i, 0))

    def whole(array):
        return pl.BlockSpec(array.shape, lambda i, ends: (0, 0))

    grad, *carries = pl.pallas_call(
        functools.partial(scan_backward_kernel, base=last),
        grid_spec=pltpu.PrefetchScalarGridSpec(
            num_scalar_prefetch=1,
            grid=(each,),
            in_specs=[rows_of(chans), rows_of(cols), rows_of(own), rows_of(N, rows=own)]
            + [whole(a) for a in (taps, head_rows, skip_row, *carries)]
            + [pl.BlockSpec(memory_space=pl.ANY)] * len(held)
            + [whole(a) for a in after],
            out_specs=[rows_of(cols)] + [whole(a) for a in carries],
            scratch_shapes=[pltpu.VMEM((BLOCK_LEN + 8, chans), F32)],
        ),
        out_shape=[jax.ShapeDtypeStruct((length, cols), BF)]
        + [jax.ShapeDtypeStruct(a.shape, F32) for a in carries],
        input_output_aliases={11: 0} if held else {},
        compiler_params=pltpu.CompilerParams(vmem_limit_bytes=SCAN_VMEM),
        cost_estimate=pl.CostEstimate(flops=each * 2**31, bytes_accessed=0, transcendentals=0),
        name="scan_backward",
    )(ends, pre, mix, grad_scan, entering, taps, head_rows, skip_row, *carries, *held, *after)
    return grad, carries


def shards(
    hidden, seq_lens, norm_w, w_in, conv_w, conv_b, dt_bias, a_log, skip_gain, gate_w, w_out, cotangent
):
    dp, heads = lax.axis_size("dp"), lax.axis_size("heads")
    my_dp, my_head = lax.axis_index("dp"), lax.axis_index("heads")
    me = my_dp * heads + my_head
    rows_dev, width = hidden.shape
    length = rows_dev * heads
    w_rows = w_in.shape[0]
    out_rows = w_out.shape[0]
    own = DI // heads
    own_heads = own // P_SIZE
    chans = own + 2 * N
    taps_dev = conv_b.shape[0]
    ends = jnp.cumsum(seq_lens[0]).astype(jnp.int32)
    where = where_vector(ends)
    owners = [where[RING + heads + k] for k in range(dp)]
    striped = out_rows % P_SIZE == 0
    per_block = own_heads // dp if striped else 0

    def split_own(array, size):
        rows = array.shape[0]
        if striped:
            cut = array.reshape(rows, dp, heads, per_block * size).transpose(2, 0, 1, 3)
        else:
            cut = array.reshape(rows, heads, own_heads * size).transpose(1, 0, 2)
        return cut.reshape(heads, rows, own_heads * size)

    pad = LANE - own_heads
    mix_cut = jnp.concatenate(
        [
            split_own(w_in[:, DI : 2 * DI], P_SIZE),
            jnp.broadcast_to(w_in[None, :, 2 * DI : DI + CONV_CH], (heads, w_rows, 2 * N)),
            split_own(w_in[:, DI + CONV_CH :], 1),
            jnp.zeros((heads, w_rows, pad), BF),
        ],
        axis=2,
    )
    gate_cut = split_own(w_in[:, :DI], P_SIZE)

    def to_heads(cut):
        return lax.all_to_all(cut, "heads", split_axis=0, concat_axis=0, tiled=True)

    hidden_ring = GatherRing(hidden, "heads")
    steps = hidden_ring.half
    w_mix = to_heads(mix_cut)
    route = [(q, (q % dp) * heads + q // dp) for q in range(dp * heads)]
    out_gather = GatherDp(w_out if striped else lax.ppermute(w_out, ("dp", "heads"), route))
    small = pack_small(conv_w, conv_b, norm_w, gate_w, dt_bias, a_log, skip_gain)
    for axis in ("heads", "dp"):
        for bits in powers(axis):
            small = doubled(small, axis, bits)

    def placed(distances, buffer, after=()):
        found = [f for f in ring_rows([hidden_ring.arrived.get(d, []) for d in range(heads)]) if f[0] in distances]
        return place(where, found, buffer, length, after)

    placing = []
    for step in range(1, steps):
        if step == 1:
            w_mix, small, where, gate_cut, *arrived = hidden_ring.advance(
                w_mix, small, where, gate_cut, *out_gather.moving
            )
            mix_gather = GatherDp(w_mix.reshape(heads * w_rows, -1))
            out_gather.relay(arrived)
            tokens = placed((0, 1, heads - 1), None)
        elif step == 2:
            cot, *placing = hidden_ring.advance(cotangent, stand(tokens))
            tokens = placed((step, heads - step), tokens, placing)
            cot_ring = GatherRing(cot, "heads")
        elif step == 3:
            ready, *arrived = hidden_ring.advance(stand(tokens), *mix_gather.moving)
            mix_gather.relay(arrived)
            tokens = placed((step, heads - step), tokens, [ready])
        else:
            placing = hidden_ring.advance(stand(tokens))
            tokens = placed((step, heads - step), tokens, placing)
    taps, gate_gain, norm_row, head_rows, skip_row = unpack(
        where, dp, heads, striped, own, width, (taps_dev, w_rows, out_rows), small
    )
    ready, norm_row, gate_cut, *arrived = hidden_ring.advance(
        stand(tokens), norm_row, gate_cut, *mix_gather.far, *out_gather.far
    )
    tokens = placed((heads // 2,), tokens, [ready])
    mix_pieces, out_pieces = mix_gather.all(arrived[: dp // 2]), out_gather.all(arrived[dp // 2 :])
    w_gate = to_heads(gate_cut)

    (norm_row,) = cot_ring.advance(norm_row)
    normed, mix = project(where, heads, norm_row, tokens, mix_pieces)
    ready, w_gate = cot_ring.advance(stand(mix), w_gate)
    gate_gather = GatherDp(w_gate.reshape(heads * w_rows, -1))
    pre, scanned, entering = scan_forward(ends, mix, taps, head_rows, skip_row, 1, [ready])
    ready = stand(scanned)
    for step in range(3, steps):
        ready, *gate_gather.moving = cot_ring.advance(ready, *gate_gather.moving)
    gate_gather.relay(gate_gather.moving)
    gate_pieces = gate_gather.all(gate_gather.far)
    gate, w_full, branch = gate_forward(
        where, heads, normed, scanned, gate_gain, gate_pieces, out_pieces, [ready]
    )
    ready = stand(gate)

    branch_ring = ScatterRing(branch, "heads")
    cot_ring.advance()
    cot_live, weighted, sums = gate_sums(where, cot_ring.all(), w_full, scanned, gate, gate_gain, [ready])
    sums = sums + lax.ppermute(sums, "heads", xor_route(heads, 1))
    (sums,) = branch_ring.advance(sums)
    sums = sum(pairs(sums, "heads"))
    grad_scan, grad_gate, gated = gate_backward(where, dp, striped, sums, weighted, scanned, gate, gate_gain)
    (ready,) = branch_ring.advance(stand(grad_gate))
    gate_scatter = ScatterDp(*weight_term(normed, grad_gate))

    def back(call, carries, grad_mix, *after):
        return scan_backward(
            ends, pre, mix, grad_scan, entering, taps, head_rows, skip_row, carries, grad_mix, call, 2, after
        )

    grad_mix, carries = back(0, None, (), stand(gate_scatter.kept), ready)
    ready, *arrived = branch_ring.advance(stand(carries[0]), *gate_scatter.moving)
    gate_scatter.relay(arrived)
    if striped:
        terms = weight_term(gated, cot_live)
    else:
        term = mm(gated, cot_live, ((0,), (0,))).astype(BF)
        cuts = [lax.dynamic_slice(term, (o * out_rows, 0), (out_rows, width)) for o in owners]
        terms = jnp.concatenate(cuts[: dp // 2]), jnp.concatenate(cuts[dp // 2 :])
    out_scatter = ScatterDp(*terms)
    grad_mix, carries = back(1, carries, grad_mix, ready, stand(terms[0]))
    small_grads = carries[2]
    small_core = other_core(small_grads)
    mix_scatter = ScatterDp(*weight_term(normed, grad_mix))
    small_core, ready = together(small_core, stand(mix_scatter.kept))
    small_grads = small_grads + small_core
    small_moving = [lax.ppermute(small_grads, "dp", xor_route(dp, bits)) for bits in range(2, dp, 2)]
    parts = project_back(
        where, heads, grad_gate, grad_mix, gate_pieces, mix_pieces, [ready, stand(small_grads)]
    )

    grad_ring = ScatterRings(parts, "heads")
    while branch_ring.left > 1:
        branch_ring.advance()
    n_gate, n_out, n_mix = len(gate_scatter.moving), len(out_scatter.moving), len(mix_scatter.moving)
    ready, *arrived = branch_ring.advance(
        stand(parts[0][0]), *gate_scatter.moving, *out_scatter.moving, *mix_scatter.moving, *small_moving
    )
    from_gate, arrived = arrived[:n_gate], arrived[n_gate:]
    from_out, arrived = arrived[:n_out], arrived[n_out:]
    mix_scatter.relay(arrived[:n_mix], ready)
    small_grads = doubled(sum(arrived[n_mix:], small_grads), "heads", 1)
    for step in range(1, steps):
        if step == 1:
            grad_ring.advance()
            ready = stand(grad_ring.last)
            gate_cols = to_heads(gate_scatter.all(from_gate, BF, ready).reshape(heads, w_rows, own))
            out_scatter.relay(from_out, ready)
        elif step == 2:
            (small_grads,) = grad_ring.advance(small_grads)
            small_grads = doubled(small_grads, "heads", 2)
        elif step == 3:
            n_mix = len(mix_scatter.moving)
            small_grads, *arrived = grad_ring.advance(small_grads, *mix_scatter.moving, *branch_ring.sums)
            arrived, branch_sums = arrived[:n_mix], arrived[n_mix:]
            mix_cols = mix_scatter.all(arrived, BF, stand(grad_ring.last))
            mix_cols = to_heads(mix_cols.reshape(heads, w_rows, -1))
            for bits in powers("heads")[2:]:
                small_grads = doubled(small_grads, "heads", bits)
            output = output_of(where, sums, hidden, (*branch[0], *branch_sums, stand(grad_ring.last)))
        else:
            grad_ring.advance()
    output, *arrived = grad_ring.advance(output, *out_scatter.moving)
    own_parts = [part for k in range(2) for part in (parts[0][k], *grad_ring.sums[k])]
    input_grad = input_grad_of(where, dp, own_parts, hidden, cotangent, norm_row)
    if not arrived:
        arrived = [jnp.zeros(w_out.shape, BF)]
    if striped:
        w_out_grad, out_sums = out_grad_of(arrived[0], out_scatter.sums[0], w_out)
    else:
        w_out_grad = add_last(arrived[0], out_scatter.sums[0], F32, ())
        w_out_grad = lax.ppermute(w_out_grad, ("dp", "heads"), [(dst, src) for src, dst in route])
        out_sums = jnp.sum(w_out.astype(F32) * w_out_grad, axis=1, keepdims=True)
    gate_w_grad = out_sums[:, 0] / gate_w.astype(F32)
    w_in_grad, norm_sums = weight_rows(dp, striped, gate_cols, mix_cols, w_in)
    norm_w_grad = norm_sums[:, 0] / norm_w.astype(F32)

    taps_grad, bias_grad, by_head = collect(where, dp, heads, striped, taps_dev, small_grads)
    return (
        output,
        input_grad,
        norm_w_grad,
        w_in_grad,
        taps_grad,
        bias_grad.reshape(-1),
        by_head[Small.BIAS_GRAD, :own_heads],
        by_head[Small.LOG_GRAD, :own_heads],
        by_head[Small.SKIP_GRAD, :own_heads],
        gate_w_grad,
        w_out_grad,
    )


def solution(mesh):
    both = ("dp", "heads")
    placed = (
        P(both, None),
        P("dp", None),
        P(both),
        P(both, None),
        P(None, both),
        P(both),
        P("heads"),
        P("heads"),
        P("heads"),
        P(both),
        P(both, None),
        P(both, None),
    )
    return jax.shard_map(
        shards,
        mesh=mesh,
        in_specs=placed,
        out_specs=(
            P(both, None),
            P(both, None),
            P(both),
            P(both, None),
            P(None, both),
            P(both),
            P("heads"),
            P("heads"),
            P("heads"),
            P(both),
            P(both, None),
        ),
        check_vma=False,
    )
```

```python
import functools

import numpy as np

import jax
import jax.numpy as jnp
from jax import lax
from jax.experimental import pallas as pl
from jax.experimental.pallas import tpu as pltpu
from jax.sharding import PartitionSpec as P

P_SIZE = 64
N = 128
CONV_K = 4
BLOCK_LEN = 256
SEQS = 3
DI = 4096
CONV_CH = 4352
LANE = 128
EPS = 1e-05
ROWS = 512
RING = SEQS
SCAN_VMEM = 20 * 2**20

NO_COST = pl.CostEstimate(flops=0, bytes_accessed=0, transcendentals=0)
BF = jnp.bfloat16
F32 = jnp.float32


def ring_order(n):
    return list(range(0, n, 2)) + list(range(n - 1, 0, -2))


def where_vector(ends):
    heads, dp = lax.axis_size("heads"), lax.axis_size("dp")
    order = ring_order(heads)
    ring = np.zeros((heads, heads), np.int32)
    for position, index in enumerate(order):
        ring[index] = [order[(position + distance) % heads] for distance in range(heads)]
    owners = np.array([dp_owners(dp, me) for me in range(dp)], np.int32)
    return jnp.concatenate(
        [ends, jnp.asarray(ring)[lax.axis_index("heads")], jnp.asarray(owners)[lax.axis_index("dp")]]
    )


def ring_route(n, step):
    order = ring_order(n)
    return [(order[i], order[(i + step) % n]) for i in range(n)]


def xor_route(n, bits):
    return [(i, i ^ bits) for i in range(n)]


def together(*values):
    return list(lax.optimization_barrier(values))


def together_with(moving, others):
    values = together(*moving.values(), *others)
    return dict(zip(moving, values)), values[len(moving) :]


class GatherRing:
    def __init__(self, rows, axis):
        self.axis, self.n = axis, lax.axis_size(axis)
        self.half = self.n // 2
        self.step = 0
        self.arrived = {0: [rows]}
        self.moving = {way: self.sent(rows, way) for way in (1, -1)}

    def sent(self, value, way):
        return lax.ppermute(value, self.axis, ring_route(self.n, way))

    def advance(self, *others):
        self.step += 1
        moving, others = together_with(self.moving, others)
        self.moving = {}
        if self.step == self.half:
            self.arrived[self.half] = [moving[1], moving[-1]]
            return others
        for way, value in moving.items():
            self.arrived[-way * self.step % self.n] = [value]
        if self.step == self.half - 1:
            moving = dict(zip((1, -1), halves(moving[1], moving[-1])))
        for way, value in moving.items():
            self.moving[way] = self.sent(value, way)
        return others

    def all(self):
        return [self.arrived[d] for d in range(self.n)]


class ScatterRing:
    def __init__(self, parts, axis):
        self.axis, self.n = axis, lax.axis_size(axis)
        self.half = self.n // 2
        self.parts = parts
        self.left = self.half
        self.moving = {1: self.sent(parts[self.half][0], 1), -1: self.sent(parts[self.half][1], -1)}

    def sent(self, value, way):
        return lax.ppermute(value, self.axis, ring_route(self.n, way))

    def advance(self, *others):
        self.left -= 1
        moving, others = together_with(self.moving, others)
        if not self.left:
            self.sums = [moving[1], moving[-1]]
            return others
        for way, value in moving.items():
            (part,) = self.parts[way * self.left % self.n]
            total = add_rows(value, part, 0 if way == 1 else part.shape[0] - value.shape[0])
            self.moving[way] = self.sent(total, way)
        return others


class ScatterRings:
    def __init__(self, parts, axis):
        self.axis, self.n = axis, lax.axis_size(axis)
        self.half = self.n // 2
        self.parts = parts
        self.left = self.half
        self.sums = [[], []]
        self.moving = {}
        for chunk, way in ((0, 1), (1, -1)):
            self.send(chunk, way, parts[self.half][chunk])

    def send(self, chunk, way, value):
        self.moving[chunk, way] = lax.ppermute(value, self.axis, ring_route(self.n, way))

    def advance(self, *others):
        self.left -= 1
        moving, others = together_with(self.moving, others)
        self.moving = {}
        for (chunk, way), value in moving.items():
            if self.left:
                value = add_rows(value, self.parts[way * self.left % self.n][chunk], 0)
                self.send(chunk, way, value)
                self.last = value
            else:
                self.sums[chunk].append(value)
        if self.left == self.half - 1:
            for chunk, way in ((1, 1), (0, -1)):
                self.send(chunk, way, self.parts[way * self.left % self.n][chunk])
        return others


def dp_owners(n, me):
    return [((me - 2 * s) % n) ^ b for b in range(2) for s in range(n // 2)]


def next_chip(value):
    n = lax.axis_size("dp")
    return lax.ppermute(value, "dp", [(i, (i + 2) % n) for i in range(n)])


def other_core(value):
    return lax.ppermute(value, "dp", xor_route(lax.axis_size("dp"), 1))


class GatherDp:
    def __init__(self, block):
        self.chips = lax.axis_size("dp") // 2
        self.near, self.far = [block], [other_core(block)]
        self.moving = [next_chip(block)] if self.chips > 1 else []

    def relay(self, arrived):
        for step in range(1, self.chips):
            (value,) = arrived if step == 1 else self.moving
            self.near.append(value)
            self.far.append(other_core(value))
            self.moving = [next_chip(value)] if step + 1 < self.chips else []

    def all(self, arrived):
        return self.near + list(arrived)


class ScatterDp:
    def __init__(self, kept, given):
        self.chips = lax.axis_size("dp") // 2
        self.kept = kept
        self.moving = [other_core(given)]

    def relay(self, arrived, *after):
        self.sums = add_core(self.kept, arrived[0], self.chips, after)
        self.moving = [next_chip(self.sums[1])] if self.chips > 1 else []
        for step in range(2, self.chips):
            value = self.moving[0].astype(F32)
            self.moving = [next_chip((value + self.sums[step]).astype(BF))]

    def all(self, arrived, dtype, *after):
        if self.chips == 1:
            return self.sums[0].astype(dtype)
        return add_last(arrived[0], self.sums[0], dtype, after)


def doubled(block, axis, bits):
    return join([block, lax.ppermute(block, axis, xor_route(lax.axis_size(axis), bits))])


def pairs(block, axis):
    n = lax.axis_size(axis)
    return [block] + [lax.ppermute(block, axis, xor_route(n, bits)) for bits in range(2, n, 2)]


def powers(axis):
    return [1 << k for k in range(lax.axis_size(axis).bit_length() - 1)]


def vmem_of(arrays, specs, rest):
    total = rest
    for array, spec in zip(arrays, specs):
        if spec.block_shape is not None:
            copies = 1 if spec.pipeline_mode else 2
            total += copies * int(np.prod(spec.block_shape)) * array.dtype.itemsize
    return total


def call_kernel(body, scalars, grid, ins, in_specs, outs, out_specs, name, scratch=(), flops=0, rest=6 * 2**20, after=()):
    count = 1 + len(ins)
    inner = body
    if after:

        def body(*refs):
            inner(*refs[:count], *refs[count + len(after) :])

    ins = (*ins, *after)
    in_specs = [*in_specs, *(whole(a) for a in after)]
    bytes_moved = sum(int(np.prod(a.shape)) * a.dtype.itemsize for a in outs)
    return pl.pallas_call(
        body,
        grid_spec=pltpu.PrefetchScalarGridSpec(
            num_scalar_prefetch=1, grid=grid, in_specs=in_specs, out_specs=out_specs, scratch_shapes=scratch
        ),
        out_shape=outs,
        compiler_params=pltpu.CompilerParams(
            vmem_limit_bytes=vmem_of((*ins, *outs), (*in_specs, *out_specs), rest)
        ),
        cost_estimate=pl.CostEstimate(flops=flops, bytes_accessed=0, transcendentals=0),
        name=name,
    )(scalars, *ins)


def whole(array):
    return pl.BlockSpec(array.shape, lambda *i: (0, 0))


def once(array):
    return pl.BlockSpec(array.shape, lambda *i: (0, 0), pipeline_mode=pl.Buffered(1))


def rows_of(width, rows=ROWS):
    return pl.BlockSpec((rows, width), lambda i, s: (i, 0))


def call_whole(body, ins, outs, name, rest=2**20):
    specs = [pl.BlockSpec(memory_space=pltpu.VMEM)] * len(ins), [pl.BlockSpec(memory_space=pltpu.VMEM)] * len(outs)
    held = sum(int(np.prod(a.shape)) * a.dtype.itemsize for a in (*ins, *outs))
    return pl.pallas_call(
        body,
        in_specs=specs[0],
        out_specs=specs[1],
        out_shape=outs,
        compiler_params=pltpu.CompilerParams(vmem_limit_bytes=held + rest),
        cost_estimate=NO_COST,
        name=name,
    )(*ins)


def halves_kernel(first, second, top, bottom):
    rows = top.shape[0]
    top[...] = first[:rows, :]
    bottom[...] = second[rows:, :]


def halves(first, second):
    out = jax.ShapeDtypeStruct((first.shape[0] // 2, first.shape[1]), first.dtype)
    return call_whole(halves_kernel, (first, second), [out, out], "halves")


def stand_kernel(value, out):
    out[...] = value[0:8, :].astype(F32)


def stand(value):
    flat = value.reshape(-1, value.shape[-1])
    rows = min(16, flat.shape[0])
    return pl.pallas_call(
        stand_kernel,
        grid=(1,),
        in_specs=[pl.BlockSpec((rows, LANE), lambda i: (0, 0))],
        out_specs=pl.BlockSpec((8, LANE), lambda i: (0, 0)),
        out_shape=jax.ShapeDtypeStruct((8, LANE), F32),
        compiler_params=pltpu.CompilerParams(vmem_limit_bytes=2**20),
        cost_estimate=NO_COST,
        name="stand",
    )(flat)


def join_kernel(*refs):
    *blocks, out = refs
    first = 0
    for block in blocks:
        out[first : first + block.shape[0], :] = block[...]
        first += block.shape[0]


def join(blocks):
    rows = sum(block.shape[0] for block in blocks)
    out = jax.ShapeDtypeStruct((rows, blocks[0].shape[1]), blocks[0].dtype)
    return call_whole(join_kernel, blocks, [out], "join")[0]


def add_rows_kernel(place, sent, part, out):
    rows = sent.shape[0]
    if rows < out.shape[0]:
        out[...] = part[...]
    at = slice(place, place + rows)
    out[at, :] = (sent[...].astype(F32) + part[at, :].astype(F32)).astype(BF)


def add_rows(sent, part, place):
    body = functools.partial(add_rows_kernel, place)
    return call_whole(body, (sent, part), [jax.ShapeDtypeStruct(part.shape, BF)], "add_rows")[0]


def add_core_kernel(chips, kept, given, *refs):
    outs = refs[-chips:]
    rows = outs[0].shape[0]
    for k, out in enumerate(outs):
        at = slice(k * rows, (k + 1) * rows)
        out[...] = (kept[at, :].astype(F32) + given[at, :].astype(F32)).astype(out.dtype)


def add_core(kept, given, chips, after):
    rows, cols = kept.shape[0] // chips, kept.shape[1]
    outs = [jax.ShapeDtypeStruct((rows, cols), BF if k == 1 else F32) for k in range(chips)]
    return call_whole(functools.partial(add_core_kernel, chips), (kept, given, *after), outs, "add_core")


def add_last_kernel(arrived, kept, *refs):
    out = refs[-1]
    out[...] = (arrived[...].astype(F32) + kept[...]).astype(out.dtype)


def add_last(arrived, kept, dtype, after):
    return call_whole(add_last_kernel, (arrived, kept, *after), [jax.ShapeDtypeStruct(kept.shape, dtype)], "add_last")[0]


def weight_term(left, right):
    half = left.shape[1] // 2
    given = mm(left[:, half:], right, ((0,), (0,))).astype(BF)
    kept = mm(left[:, :half], right, ((0,), (0,))).astype(BF)
    return kept, given


class Small:
    BIAS, NORM, GATE, HEADS = CONV_K, CONV_K + 1, CONV_K + 2, CONV_K + 3
    SKIP_GRAD, BIAS_GRAD, LOG_GRAD = CONV_K + 1, CONV_K + 2, CONV_K + 3


def pack_small(conv_w, conv_b, norm_w, gate_w, dt_bias, a_log, skip_gain):
    per_head = jnp.concatenate([dt_bias, a_log, skip_gain])
    rows = [conv_w] + [row.reshape(1, -1) for row in (conv_b, norm_w, gate_w, per_head)]
    lanes = max(row.shape[1] for row in rows)
    lanes = -(-lanes // LANE) * LANE
    return jnp.concatenate([jnp.pad(row.astype(F32), ((0, 0), (0, lanes - row.shape[1]))) for row in rows])


def lanes_of(width):
    return lax.broadcasted_iota(jnp.int32, (8, width), 1)


def own_blocks(dp, heads, head, own, striped):
    if striped:
        size = own // dp
        return [(j * heads + head) * size for j in range(dp)], size
    return [head * own], own


def unpack_kernel(dp, heads, per_device, striped, where, table, taps, gate, norm, head_rows, skip):
    own = gate.shape[1]
    my_head, my_dp = where[RING], where[RING + heads]
    lanes = table.shape[1]

    def tile(at_dp, at_head):
        slot = (at_dp ^ my_dp) * heads + (at_head ^ my_head)
        return table[pl.ds(pl.multiple_of(slot * 8, 8), 8), :]

    def run(first, width):
        lane = lanes_of(LANE)
        start = first // width
        shift = first - start * width
        total = jnp.zeros((8, LANE), F32)
        for k in range((LANE + width - 2) // width + 1):
            device = jnp.minimum(start + k, dp * heads - 1)
            moved = pltpu.roll(tile(device // heads, device % heads), (k * width - shift) % lanes, 1)[:, :LANE]
            source = lane - k * width + shift
            total = jnp.where((source >= 0) & (source < width), moved, total)
        return total

    blocks, size = own_blocks(dp, heads, my_head, own, striped)
    conv_width, norm_width, gate_width = per_device
    at = 0
    for first in blocks:
        for more in range(0, size, LANE):
            taps[:, at : at + LANE] = run(first + more, conv_width)
            gate[:, at : at + LANE] = run(first + more, gate_width)
            at += LANE
    for more in range(0, 2 * N, LANE):
        taps[:, own + more : own + more + LANE] = run(jnp.int32(DI + more), conv_width)
    for more in range(0, norm.shape[1], LANE):
        norm[:, more : more + LANE] = run(jnp.int32(more), norm_width)
    lane = lanes_of(LANE)
    own_heads = own // P_SIZE
    found = [jnp.zeros((8, LANE), F32)] * 3
    for k in range(own_heads):
        each = own_heads // len(blocks)
        head = blocks[k // each] // P_SIZE + k % each
        device = head // own_heads
        values = tile(my_dp, device)
        for kind in range(3):
            source = kind * own_heads + head - device * own_heads
            moved = pltpu.roll(values, (k - source + lanes) % lanes, 1)[:, :LANE]
            found[kind] = jnp.where(lane == k, moved, found[kind])
    row = slice(Small.HEADS, Small.HEADS + 1)
    head_rows[...] = jnp.zeros_like(head_rows)
    head_rows[0:1, :] = found[0][row, :]
    head_rows[1:2, :] = jnp.where(lane[0:1, :] < own_heads, -jnp.exp(found[1][row, :]), 0.0)
    head_of = lax.broadcasted_iota(jnp.int32, (LANE, own), 1) // P_SIZE
    spread = (head_of == lax.broadcasted_iota(jnp.int32, (LANE, own), 0)).astype(F32).astype(BF)
    skip[...] = split_times(found[2], spread, 3)


def unpack(where, dp, heads, striped, own, width, per_device, table):
    outs = [jax.ShapeDtypeStruct((8, w), F32) for w in (own + 2 * N, own, width, LANE, own)]
    return call_kernel(
        functools.partial(unpack_kernel, dp, heads, per_device, striped),
        where,
        (1,),
        (table,),
        [whole(table)],
        outs,
        [whole(o) for o in outs],
        "unpack",
    )


def collect_kernel(dp, heads, striped, taps_dev, where, table, taps, bias, head_out, full, by_head):
    chans = table.shape[1]
    own = chans - 2 * N
    own_heads = own // P_SIZE
    my_head, my_dp = where[RING], where[RING + heads]

    def slot(at_head):
        return pl.multiple_of((at_head ^ my_head) * 8, 8)

    full[...] = jnp.zeros_like(full)
    shared = jnp.zeros((8, 2 * N), F32)
    chan_head = lax.broadcasted_iota(jnp.int32, (own, LANE), 0) // P_SIZE
    gather = (chan_head == lax.broadcasted_iota(jnp.int32, (own, LANE), 1)).astype(F32).astype(BF)
    row = lax.broadcasted_iota(jnp.int32, (8, LANE), 0)
    for head in range(heads):
        tile = table[pl.ds(slot(head), 8), :]
        blocks, size = own_blocks(dp, heads, head, own, striped)
        for k, first in enumerate(blocks):
            full[:, first : first + size] = tile[:, k * size : (k + 1) * size]
        shared = shared + tile[:, own:]
        summed = split_times(tile[:, :own], gather, 3)
        by_head[head * 8 : (head + 1) * 8, :] = jnp.where(row == Small.SKIP_GRAD, summed, tile[:, :LANE])
    full[:, DI : DI + 2 * N] = shared
    first = (my_dp * heads + my_head) * taps_dev
    start = first // LANE
    window = -(-(taps_dev + LANE) // LANE) * LANE
    rows = full[:, pl.ds(pl.multiple_of(start * LANE, LANE), window)]
    rows = pltpu.roll(rows, (window - (first - start * LANE)) % window, 1)[:, :taps_dev]
    taps[...] = rows[:CONV_K, :]
    bias[...] = rows[CONV_K : CONV_K + 1, :]
    lane = lanes_of(LANE)
    total = jnp.zeros((8, LANE), F32)
    per_block = own_heads // dp if striped else own_heads
    for k in range(own_heads):
        head = my_head * own_heads + k
        block = head // per_block
        owner = block % heads
        source = block // heads * per_block + head % per_block
        values = by_head[pl.ds(pl.multiple_of(owner * 8, 8), 8), :]
        total = jnp.where(lane == k, pltpu.roll(values, (k - source + LANE) % LANE, 1), total)
    head_out[...] = total


def collect(where, dp, heads, striped, taps_dev, table):
    outs = [jax.ShapeDtypeStruct(shape, F32) for shape in ((CONV_K, taps_dev), (1, taps_dev), (8, LANE))]
    window = -(-(taps_dev + LANE) // LANE) * LANE
    return call_kernel(
        functools.partial(collect_kernel, dp, heads, striped, taps_dev),
        where,
        (1,),
        (table,),
        [whole(table)],
        outs,
        [whole(o) for o in outs],
        "collect",
        scratch=[pltpu.VMEM((8, CONV_CH + window), F32), pltpu.VMEM((8 * heads, LANE), F32)],
    )


def ring_rows(arrived):
    found = []
    for distance, arrays in enumerate(arrived):
        first = 0
        for array in arrays:
            found.append((distance, first, array))
            first += array.shape[0]
    return found


def place_kernel(places, where, *refs):
    count = len(places)
    out, sems = refs[-2:]
    rows_dev = max(first + ref.shape[0] for (_, first), ref in zip(places, refs))
    copies = []
    for k, ((distance, first), ref) in enumerate(zip(places, refs[:count])):
        to = pl.multiple_of(where[RING + distance] * rows_dev + first, ref.shape[0])
        copies.append(pltpu.make_async_copy(ref, out.at[pl.ds(to, ref.shape[0]), :], sems.at[k]))
    for copy in copies:
        copy.start()
    for copy in copies:
        copy.wait()


def place(where, found, buffer, length, after=()):
    places, arrays = [f[:2] for f in found], [f[2] for f in found]
    held = () if buffer is None else (buffer,)
    anywhere = pl.BlockSpec(memory_space=pl.ANY)
    ins = (*arrays, *held, *after)
    return pl.pallas_call(
        functools.partial(place_kernel, places),
        grid_spec=pltpu.PrefetchScalarGridSpec(
            num_scalar_prefetch=1,
            grid=(1,),
            in_specs=[anywhere] * len(ins),
            out_specs=anywhere,
            scratch_shapes=[pltpu.SemaphoreType.DMA((len(arrays),))],
        ),
        out_shape=jax.ShapeDtypeStruct((length, arrays[0].shape[1]), arrays[0].dtype),
        input_output_aliases={1 + len(arrays): 0} if held else {},
        compiler_params=pltpu.CompilerParams(vmem_limit_bytes=2**20),
        cost_estimate=NO_COST,
        name="place",
    )(where, *ins)


def project_kernel(heads, dp, where, gain, rows, *refs):
    pieces, (normed, out) = refs[:dp], refs[-2:]
    width = rows.shape[1]
    piece = width // dp
    values = rows[...].astype(F32)
    scale = lax.rsqrt(jnp.sum(values * values, axis=-1, keepdims=True) / width + EPS)
    total = None
    for b in range(dp):
        at = pl.ds(pl.multiple_of(where[RING + heads + b] * piece, LANE), piece)
        low = (rows[:, at].astype(F32) * scale * gain[Small.NORM : Small.NORM + 1, at]).astype(BF)
        normed[:, b * piece : (b + 1) * piece] = low
        term = mm(low, pieces[b][...])
        total = term if b == 0 else total + term
    out[...] = total


def project(where, heads, gain, rows, pieces):
    length, width = rows.shape
    cols = pieces[0].shape[1]
    dp = len(pieces)
    return call_kernel(
        functools.partial(project_kernel, heads, dp),
        where,
        (length // ROWS,),
        (gain, rows, *pieces),
        [once(gain), rows_of(width)] + [once(p) for p in pieces],
        [jax.ShapeDtypeStruct((length, width), BF), jax.ShapeDtypeStruct((length, cols), F32)],
        [rows_of(width), rows_of(cols)],
        "project",
        flops=2 * length * width * cols,
        rest=12 * 2**20,
    )


def gate_forward_kernel(dp, first, places, where, rows, scan, gain, *refs):
    gate_pieces, out_pieces, (gate_out, w_full, *parts) = refs[:dp], refs[dp : 2 * dp], refs[2 * dp :]
    depth, each = gate_pieces[0].shape[0], out_pieces[0].shape[0]

    @pl.when(pl.program_id(0) == 0)
    def _():
        for k in range(dp):
            w_full[pl.ds(pl.multiple_of(where[first + k] * each, each), each), :] = out_pieces[k][...]

    gate = mm(rows[:, :depth], gate_pieces[0][...])
    for k in range(1, dp):
        gate = gate + mm(rows[:, k * depth : (k + 1) * depth], gate_pieces[k][...])
    gate_out[...] = gate
    inner = scan[...].astype(F32) * (gate / (1.0 + jnp.exp(-gate)))
    branch = mm((inner * gain[Small.GATE : Small.GATE + 1, :]).astype(BF), w_full[...]).astype(BF)
    put_parts(where, branch, parts, places)


def part_places(heads, rows_dev, halves):
    places = []
    for distance in range(heads):
        count = 2 if distance in halves else 1
        places += [(distance, k * rows_dev // count, rows_dev // count) for k in range(count)]
    return places


def by_distance(places, parts):
    found = {}
    for (distance, _, _), part in zip(places, parts):
        found.setdefault(distance, []).append(part)
    return found


def put_parts(where, block, parts, places):
    size = block.shape[0]
    rows_dev = max(first + rows for _, first, rows in places)
    for (distance, first, rows), part in zip(places, parts):
        start = where[RING + distance] * rows_dev + first - pl.program_id(0) * size
        for at in range(0, size, rows):

            @pl.when(start == at)
            def _(part=part, at=at, rows=rows):
                part[...] = block[at : at + rows, :]


def gate_forward(where, heads, normed, scanned, gain, gate_pieces, out_pieces, after):
    length, width = normed.shape
    own, cols = scanned.shape[1], out_pieces[0].shape[1]
    dp = len(gate_pieces)
    full = jax.ShapeDtypeStruct((own, cols), BF)
    first = where.shape[0] - dp
    places = part_places(heads, length // heads, (heads // 2,))
    parts = [jax.ShapeDtypeStruct((rows, cols), BF) for _, _, rows in places]

    gate, full, *parts = call_kernel(
        functools.partial(gate_forward_kernel, dp, first, places),
        where,
        (length // ROWS,),
        (normed, scanned, gain, *gate_pieces, *out_pieces),
        [rows_of(width), rows_of(own)] + [once(a) for a in (gain, *gate_pieces, *out_pieces)],
        [jax.ShapeDtypeStruct((length, own), F32), full, *parts],
        [rows_of(own)] + [once(a) for a in (full, *parts)],
        "gate_forward",
        rest=10 * 2**20,
        after=after,
    )
    return gate, full, by_distance(places, parts)


def gate_sums_kernel(heads, places, where, w_full, scan, gate_in, gain, *refs):
    chunks, (cot, weighted_out, sums) = refs[: len(places)], refs[-3:]
    rows_dev = cot.shape[0] // heads
    block = scan.shape[0]

    @pl.when(pl.program_id(0) == 0)
    def _():
        for (distance, first), ref in zip(places, chunks):
            rows = ref.shape[0]
            to = pl.multiple_of(where[RING + distance] * rows_dev + first, rows)
            live = to + row_ids(rows) < where[SEQS - 1]
            values = ref[...]
            cot[pl.ds(to, rows), :] = jnp.where(live, values, jnp.zeros_like(values))

    mine = pl.ds(pl.multiple_of(pl.program_id(0) * block, block), block)
    weighted = mm(cot[mine, :], w_full[...], ((1,), (1,))) * gain[Small.GATE : Small.GATE + 1, :]
    weighted_out[...] = weighted
    gate = gate_in[...]
    inner = scan[...].astype(F32) * (gate / (1.0 + jnp.exp(-gate)))
    lane = lax.broadcasted_iota(jnp.int32, (1, LANE), 1)
    squares = jnp.sum(inner * inner, axis=1, keepdims=True)
    along = jnp.sum(inner * weighted, axis=1, keepdims=True)
    both = jnp.where(lane == 0, squares, jnp.where(lane == 1, along, 0.0))
    sums[...] = both.T[0:8, :]


def gate_sums(where, arrived, w_full, scanned, gate, gain, after):
    found = ring_rows(arrived)
    places, chunks = [f[:2] for f in found], [f[2] for f in found]
    own, cols = w_full.shape
    length = scanned.shape[0]
    heads = len(arrived)

    def body(*refs):
        gate_sums_kernel(heads, places, *refs)

    cot = jax.ShapeDtypeStruct((length, cols), BF)
    return call_kernel(
        body,
        where,
        (length // ROWS,),
        (w_full, scanned, gate, gain, *chunks),
        [once(w_full), rows_of(own), rows_of(own), once(gain)] + [once(c) for c in chunks],
        [cot, jax.ShapeDtypeStruct((length, own), F32), jax.ShapeDtypeStruct((8, length), F32)],
        [once(cot), rows_of(own), pl.BlockSpec((8, ROWS), lambda i, s: (0, i))],
        "gate_sums",
        after=after,
        flops=2 * length * own * cols,
    )


def gate_backward_kernel(first, block, where, sums, weighted, scan, gate_in, gain, scan_out, gate_out, gated, held):
    columns = sums[...].T
    ratio = lax.rsqrt(columns[:, 0:1] / DI + EPS)
    pull = ratio * ratio * ratio * columns[:, 1:2] / DI
    gate = gate_in[...]
    sig = 1.0 / (1.0 + jnp.exp(-gate))
    act = gate * sig
    scanned = scan[...].astype(F32)
    inner = scanned * act
    grad = ratio * weighted[...] - pull * inner
    scan_out[...] = (grad * act).astype(BF)
    gate_out[...] = (grad * scanned * (sig * (1.0 + gate * (1.0 - sig)))).astype(BF)
    held[...] = (ratio * inner * gain[Small.GATE : Small.GATE + 1, :]).astype(BF)
    for k in range(gated.shape[1] // block):
        at = slice(k * block, (k + 1) * block)
        if block < gated.shape[1]:
            gated[:, at] = held[:, pl.ds(pl.multiple_of(where[first + k] * block, LANE), block)]
        else:
            gated[...] = held[...]


def gate_backward(where, dp, striped, sums, weighted, scanned, gate, gain):
    length, own = scanned.shape
    return call_kernel(
        functools.partial(gate_backward_kernel, where.shape[0] - dp, own // dp if striped else own),
        where,
        (length // ROWS,),
        (sums, weighted, scanned, gate, gain),
        [pl.BlockSpec((8, ROWS), lambda i, s: (0, i))] + [rows_of(own)] * 3 + [whole(gain)],
        [jax.ShapeDtypeStruct((length, own), BF)] * 3,
        [rows_of(own)] * 3,
        "gate_backward",
        scratch=[pltpu.VMEM((ROWS, own), BF)],
    )


def project_back_kernel(dp, places, where, gate_rows, mix_rows, *refs):
    gate_pieces, mix_pieces, parts, out = refs[:dp], refs[dp : 2 * dp], refs[2 * dp : -1], refs[-1]
    depth = gate_pieces[0].shape[0]
    for k in range(dp):
        total = mm(mix_rows[...], mix_pieces[k][...], ((1,), (1,)))
        total = total + mm(gate_rows[...], gate_pieces[k][...], ((1,), (1,)))
        out[:, k * depth : (k + 1) * depth] = total.astype(BF)
    put_parts(where, out, parts, places)


def project_back(where, heads, grad_gate, grad_mix, gate_pieces, mix_pieces, after):
    length, own = grad_gate.shape
    cols = grad_mix.shape[1]
    pieces = (*gate_pieces, *mix_pieces)
    dp = len(gate_pieces)
    width = dp * gate_pieces[0].shape[0]
    places = part_places(heads, length // heads, range(heads))
    parts = [jax.ShapeDtypeStruct((rows, width), BF) for _, _, rows in places]
    parts = call_kernel(
        functools.partial(project_back_kernel, dp, places),
        where,
        (length // ROWS,),
        (grad_gate, grad_mix, *pieces),
        [rows_of(own), rows_of(cols)] + [once(p) for p in pieces],
        parts,
        [once(p) for p in parts],
        "project_back",
        after=after,
        scratch=[pltpu.VMEM((ROWS, width), BF)],
        rest=10 * 2**20,
    )
    return by_distance(places, parts)


def input_grad_kernel(dp, first, where, *refs):
    parts, (hidden, cot, gain, out, total) = refs[:-5], refs[-5:]
    rows, width = parts[0].shape
    piece = width // dp
    for k in range(2):
        at = slice(k * rows, (k + 1) * rows)
        own, ahead, behind = parts[3 * k : 3 * k + 3]
        grad = own[...].astype(F32) + ahead[...].astype(F32) + behind[...].astype(F32)
        for b in range(dp):
            to = pl.ds(pl.multiple_of(where[first + b] * piece, LANE), piece)
            total[at, to] = grad[:, b * piece : (b + 1) * piece]
    values = hidden[...].astype(F32)
    scale = lax.rsqrt(jnp.sum(values * values, axis=-1, keepdims=True) / width + EPS)
    grad = total[...] * gain[Small.NORM : Small.NORM + 1, :]
    along = jnp.sum(values * grad, axis=-1, keepdims=True) / width
    out[...] = cot[...].astype(F32) + scale * (grad - values * (scale * scale * along))


def input_grad_of(where, dp, parts, hidden, cot, gain):
    first = where.shape[0] - dp
    ins = (*parts, hidden, cot, gain)
    return call_kernel(
        functools.partial(input_grad_kernel, dp, first),
        where,
        (1,),
        ins,
        [once(a) for a in ins],
        [jax.ShapeDtypeStruct(hidden.shape, F32)],
        [once(hidden)],
        "input_grad",
        scratch=[pltpu.VMEM(hidden.shape, F32)],
    )[0]


def output_kernel(where, sums, hidden, own, ahead, behind, *refs):
    out = refs[-1]
    rows = hidden.shape[0]
    branch = own[...].astype(F32) + ahead[...].astype(F32) + behind[...].astype(F32)
    live = where[RING] * rows + row_ids(rows) < where[SEQS - 1]
    ratio = jnp.where(live, lax.rsqrt(sums[...].T[:, 0:1] / DI + EPS), 0.0)
    out[...] = (hidden[...].astype(F32) + ratio * branch).astype(BF)


def output_of(where, sums, hidden, parts):
    rows = hidden.shape[0]
    return call_kernel(
        output_kernel,
        where,
        (1,),
        (sums, hidden, *parts),
        [pl.BlockSpec((8, rows), lambda i, s: (0, s[RING]))] + [once(a) for a in (hidden, *parts)],
        [jax.ShapeDtypeStruct(hidden.shape, BF)],
        [once(hidden)],
        "output",
    )[0]


def out_grad_kernel(arrived, kept, w_out, out, sums):
    total = arrived[...].astype(F32) + kept[...]
    out[...] = total
    sums[...] = jnp.sum(total * w_out[...].astype(F32), axis=1, keepdims=True) + jnp.zeros(sums.shape, F32)


def out_grad_of(arrived, kept, w_out):
    outs = [jax.ShapeDtypeStruct(w_out.shape, F32), jax.ShapeDtypeStruct((w_out.shape[0], LANE), F32)]
    return call_whole(out_grad_kernel, (arrived, kept, w_out), outs, "out_grad", rest=4 * 2**20)


def weight_rows_kernel(dp, striped, gate_cols, mix_cols, w_in, out, norm_out):
    heads, rows, own = gate_cols.shape
    own_heads = own // P_SIZE
    chans = own + 2 * N
    norm = jnp.zeros((rows, 1), F32)

    def put(first, values):
        nonlocal norm
        at = slice(first, first + values.shape[1])
        out[:, at] = values
        norm = norm + jnp.sum(values * w_in[:, at].astype(F32), axis=1, keepdims=True)

    shared = mix_cols[0, :, own:chans].astype(F32)
    for head in range(1, heads):
        shared = shared + mix_cols[head, :, own:chans].astype(F32)
    put(2 * DI, shared)
    steps = jnp.zeros((rows, heads * own_heads), F32)
    source = lax.broadcasted_iota(jnp.int32, (LANE, heads * own_heads), 0)
    target = lax.broadcasted_iota(jnp.int32, (LANE, heads * own_heads), 1)
    count = dp if striped else 1
    for head in range(heads):
        for block in range(count):
            size = own // count
            at = slice(block * size, (block + 1) * size)
            put((block * heads + head) * size, gate_cols[head, :, at].astype(F32))
            put(DI + (block * heads + head) * size, mix_cols[head, :, at].astype(F32))
        each = own_heads // count
        to = (source // each * heads + head) * each + source % each
        picked = ((to == target) & (source < own_heads)).astype(F32).astype(BF)
        steps = steps + mm(mix_cols[head, :, chans:], picked)
    put(DI + CONV_CH, steps)
    norm_out[...] = norm + jnp.zeros(norm_out.shape, F32)


def weight_rows(dp, striped, gate_cols, mix_cols, w_in):
    rows = w_in.shape[0]
    ins = (gate_cols, mix_cols, w_in)

    def body(*refs):
        weight_rows_kernel(dp, striped, *refs)

    return pl.pallas_call(
        body,
        out_shape=[jax.ShapeDtypeStruct(w_in.shape, F32), jax.ShapeDtypeStruct((rows, LANE), F32)],
        compiler_params=pltpu.CompilerParams(vmem_limit_bytes=SCAN_VMEM),
        cost_estimate=NO_COST,
        name="weight_rows",
    )(*ins)


FAR = -1e30


def mm(left, right, contract=((1,), (0,))):
    return lax.dot_general(left, right, (contract, ((), ())), preferred_element_type=F32)


def row_ids(rows):
    return lax.broadcasted_iota(jnp.int32, (rows, 1), 0)


def split_sum(ones, values, count):
    parts, rest = [], values
    for _ in range(count):
        part = rest.astype(BF)
        parts.append(part)
        rest = rest - part.astype(F32)
    product = mm(ones, jnp.concatenate(parts, axis=1))
    width = values.shape[1]
    total = product[:, :width]
    for k in range(1, count):
        total = total + product[:, k * width : (k + 1) * width]
    return total


def split_times(values, ones, count):
    total, rest = jnp.zeros((values.shape[0], ones.shape[1]), F32), values
    for _ in range(count):
        part = rest.astype(BF)
        total = total + mm(part, ones)
        rest = rest - part.astype(F32)
    return total


def widen(values, spread2):
    high = values.astype(BF)
    low = (values - high.astype(F32)).astype(BF)
    return mm(jnp.concatenate([high, low], axis=1), spread2)


def segment_at(position, ends_ref):
    seg = jnp.zeros_like(position)
    start = jnp.zeros_like(position)
    for k in range(SEQS):
        end = ends_ref[k]
        seg = seg + (position >= end).astype(jnp.int32)
        start = jnp.where(position >= end, end, start)
    return seg, start


def scalar_segment(position, ends_ref):
    seg = jnp.int32(0)
    for k in range(SEQS):
        seg = seg + (position >= ends_ref[k]).astype(jnp.int32)
    return jnp.where(position < 0, -1, seg)


class Block:
    def __init__(self, index, ends_ref, dt_part, head_ref, own):
        rows = BLOCK_LEN
        first = index * rows
        seg, self.start = segment_at(first + row_ids(rows), ends_ref)
        self.position = first + row_ids(rows)
        col = lax.broadcasted_iota(jnp.int32, (1, rows), 1)
        seg_row, _ = segment_at(first + col, ends_ref)
        causal = row_ids(rows) >= col
        self.lower = jnp.where(causal, 1.0, 0.0).astype(BF)
        same = seg == seg_row
        self.penalty = jnp.where(causal & same, 0.0, FAR)
        before = scalar_segment(first - 1, ends_ref)
        last = scalar_segment(first + rows - 1, ends_ref)
        self.raw = dt_part.astype(BF).astype(F32) + head_ref[0:1, :]
        self.decay = head_ref[1:2, :]
        self.dt = jnp.maximum(self.raw, 0.0) + jnp.log1p(jnp.exp(-jnp.abs(self.raw)))
        self.cum = split_sum(self.lower, self.dt * self.decay, 3)
        final = self.cum[rows - 1 : rows, :]
        self.enter = jnp.where(seg == before, jnp.exp(self.cum), 0.0)
        self.tail = jnp.where(seg == last, jnp.exp(final - self.cum), 0.0)
        self.keep = jnp.where(before == last, jnp.exp(final), 0.0)
        head_of = lax.broadcasted_iota(jnp.int32, (LANE, own), 1) // P_SIZE
        self.spread = (head_of == lax.broadcasted_iota(jnp.int32, (LANE, own), 0)).astype(F32).astype(BF)
        spread2 = jnp.concatenate([self.spread, self.spread], axis=0)
        self.dt_wide = widen(self.dt, spread2)
        self.enter_wide = widen(self.enter, spread2)
        self.tail_wide = widen(self.tail, spread2)
        self.cum_row = self.cum.T
        chan_head = lax.broadcasted_iota(jnp.int32, (own, LANE), 0) // P_SIZE
        self.gather = (chan_head == lax.broadcasted_iota(jnp.int32, (own, LANE), 1)).astype(F32)
        self.keep_chan = jnp.sum(self.gather * self.keep, axis=1, keepdims=True)

    def gap(self, head):
        return self.cum[:, head : head + 1] - self.cum_row[head : head + 1, :]


def scan_forward_kernel(ends_ref, mix_ref, taps_ref, head_ref, skip_ref, state_in, rim_in, *refs, base):
    pre_ref, scan_ref, enter_ref, state, rim, ext = refs[-6:]
    index = base + pl.program_id(0)
    chans = pre_ref.shape[1]
    own = chans - 2 * N
    rows = BLOCK_LEN

    @pl.when(pl.program_id(0) == 0)
    def _():
        rim[...] = rim_in[...]
        state[...] = state_in[...]

    ext[0:8, :] = rim[...]
    ext[8:, :] = mix_ref[:, :chans]
    blk = Block(index, ends_ref, mix_ref[:, chans:], head_ref, own)
    total = taps_ref[CONV_K : CONV_K + 1, :] + taps_ref[CONV_K - 1 : CONV_K, :] * ext[8:, :]
    for lag in range(1, CONV_K):
        linked = (blk.position - lag >= blk.start).astype(F32)
        tap = taps_ref[CONV_K - 1 - lag : CONV_K - lag, :]
        total = total + tap * (linked * ext[8 - lag : 8 - lag + rows, :])
    rim[...] = ext[rows : rows + 8, :]
    pre_ref[...] = total
    low = (total / (1.0 + jnp.exp(-total))).astype(BF)
    x_low, b_low, c_low = low[:, :own], low[:, own : own + N], low[:, own + N :]
    x_wide = x_low.astype(F32)
    x_dt = (x_wide * blk.dt_wide).astype(BF)
    scores = mm(c_low, b_low, ((1,), (1,)))
    lane = lax.broadcasted_iota(jnp.int32, (1, LANE), 1)
    entering = state[...]
    enter_ref[...] = entering
    outer = mm(c_low, entering.astype(BF), ((1,), (1,))) * blk.enter_wide + skip_ref[Small.HEADS : Small.HEADS + 1, :] * x_wide
    for pair in range(own // LANE):
        both = x_dt[:, pair * LANE : (pair + 1) * LANE]
        parts = []
        for head in (2 * pair, 2 * pair + 1):
            mixing = scores * jnp.exp(blk.gap(head) + blk.penalty)
            parts.append(mm(mixing.astype(BF), both))
        inner = jnp.where(lane < P_SIZE, parts[0], parts[1])
        at = slice(pair * LANE, (pair + 1) * LANE)
        scan_ref[:, at] = (inner + outer[:, at]).astype(BF)
    added = mm((x_wide * blk.dt_wide * blk.tail_wide).astype(BF), b_low, ((0,), (0,)))
    state[...] = blk.keep_chan * entering + added


def scan_forward(ends, mix, taps, head_rows, skip_row, calls, after):
    length, cols = mix.shape
    chans = cols - LANE
    own = chans - 2 * N
    blocks = length // BLOCK_LEN
    each = blocks // calls
    state, rim, kept = jnp.zeros((own, N), F32), jnp.zeros((8, chans), F32), ()
    for call in range(calls):

        def rows_of(width, base=call * each, rows=BLOCK_LEN):
            return pl.BlockSpec((rows, width), lambda i, ends: (base + i, 0))

        def whole(array):
            return pl.BlockSpec(array.shape, lambda i, ends: (0, 0))

        *kept, state, rim = pl.pallas_call(
            functools.partial(scan_forward_kernel, base=call * each),
            grid_spec=pltpu.PrefetchScalarGridSpec(
                num_scalar_prefetch=1,
                grid=(each,),
                in_specs=[rows_of(cols)]
                + [whole(a) for a in (taps, head_rows, skip_row, state, rim)]
                + [pl.BlockSpec(memory_space=pl.ANY)] * len(kept)
                + [whole(a) for a in after],
                out_specs=[rows_of(chans), rows_of(own), rows_of(N, rows=own), whole(state), whole(rim)],
                scratch_shapes=[pltpu.VMEM((BLOCK_LEN + 8, chans), F32)],
            ),
            out_shape=[
                jax.ShapeDtypeStruct((length, chans), F32),
                jax.ShapeDtypeStruct((length, own), BF),
                jax.ShapeDtypeStruct((blocks * own, N), F32),
                jax.ShapeDtypeStruct(state.shape, F32),
                jax.ShapeDtypeStruct(rim.shape, F32),
            ],
            input_output_aliases={7 + k: k for k in range(len(kept))},
            compiler_params=pltpu.CompilerParams(vmem_limit_bytes=SCAN_VMEM),
            cost_estimate=pl.CostEstimate(flops=each * 2**31, bytes_accessed=0, transcendentals=0),
            name="scan_forward",
        )(ends, mix, taps, head_rows, skip_row, state, rim, *kept, *after)
    return kept


def scan_backward_kernel(
    ends_ref, pre_ref, mix_ref, dy_ref, enter_ref, taps_ref, head_ref, skip_ref, *refs, base
):
    carried, (grad_ref, *carries, ext) = refs[:3], refs[-5:]
    state, rim, small_ref = carries
    index = base - pl.program_id(0)
    chans = pre_ref.shape[1]
    own = chans - 2 * N
    rows = BLOCK_LEN

    @pl.when(pl.program_id(0) == 0)
    def _():
        for given, held in zip(carried, carries):
            held[...] = given[...]

    ext[rows:, :] = rim[...]
    blk = Block(index, ends_ref, mix_ref[:, chans:], head_ref, own)
    pre = pre_ref[...]
    sig = 1.0 / (1.0 + jnp.exp(-pre))
    low = (pre * sig).astype(BF)
    x_low, b_low, c_low = low[:, :own], low[:, own : own + N], low[:, own + N :]
    x_wide = x_low.astype(F32)
    dy = dy_ref[...]
    dy_wide = dy.astype(F32)
    x_dt = (x_wide * blk.dt_wide).astype(BF)
    entering = enter_ref[...]
    enter_low = entering.astype(BF)
    leaving = state[...]
    leaving_low = leaving.astype(BF)
    gather = blk.gather.astype(BF)

    scores = mm(c_low, b_low, ((1,), (1,)))
    scores_t = mm(b_low, c_low, ((1,), (1,)))
    penalty_t = blk.penalty.T
    lane = lax.broadcasted_iota(jnp.int32, (1, LANE), 1)
    lane_rows = lax.broadcasted_iota(jnp.int32, (rows, LANE), 1)
    sub_rows = lax.broadcasted_iota(jnp.int32, (LANE, rows), 0)
    grad_scores = jnp.zeros((rows, rows), F32)
    along_rows = jnp.zeros((rows, LANE), F32)
    along_cols = jnp.zeros((LANE, rows), F32)
    grad_xdt = []
    for pair in range(own // LANE):
        at = slice(pair * LANE, (pair + 1) * LANE)
        both, dy_both = x_dt[:, at], dy[:, at]
        parts = []
        for head in (2 * pair, 2 * pair + 1):
            gap = blk.gap(head)
            decay = jnp.exp(gap + blk.penalty)
            mixing_t = scores_t * jnp.exp(penalty_t - gap)
            parts.append(mm(mixing_t.astype(BF), dy_both))
            mine = (lane < P_SIZE) if head % 2 == 0 else (lane >= P_SIZE)
            dy_one = jnp.where(mine, dy_both, jnp.zeros_like(dy_both))
            grad_mixing = mm(dy_one, both, ((1,), (1,))) * decay
            grad_scores = grad_scores + grad_mixing
            moved = grad_mixing * scores
            along_rows = along_rows + jnp.where(lane_rows == head, jnp.sum(moved, axis=1, keepdims=True), 0.0)
            along_cols = along_cols + jnp.where(sub_rows == head, jnp.sum(moved, axis=0, keepdims=True), 0.0)
        grad_xdt.append(jnp.where(lane < P_SIZE, parts[0], parts[1]))
    grad_xdt = jnp.concatenate(grad_xdt, axis=1)
    grad_cum = along_rows - along_cols.T
    grad_low = grad_scores.astype(BF)
    grad_c = mm(grad_low, b_low)
    grad_b = mm(grad_low, c_low, ((0,), (0,)))

    dy_enter = dy_wide * blk.enter_wide
    dy_enter_low = dy_enter.astype(BF)
    seen = mm(c_low, enter_low, ((1,), (1,)))
    grad_cum = grad_cum + mm((dy_enter * seen).astype(BF), gather)
    grad_c = grad_c + mm(dy_enter_low, enter_low)
    grad_enter = mm(dy_enter_low, c_low, ((0,), (0,)))

    taken = mm(b_low, leaving_low, ((1,), (1,)))
    x_tail = x_wide * blk.tail_wide
    grad_tail = mm((x_tail * taken).astype(BF), gather)
    moved = grad_tail * blk.dt
    grad_b = grad_b + mm((x_tail * blk.dt_wide).astype(BF), leaving_low)
    kept = jnp.sum(leaving * entering, axis=1, keepdims=True) * blk.keep_chan
    grad_last = jnp.sum(moved, axis=0, keepdims=True) + jnp.sum(blk.gather * kept, axis=0, keepdims=True)
    grad_cum = grad_cum - moved + jnp.where(row_ids(rows) == rows - 1, grad_last, 0.0)
    state[...] = blk.keep_chan * leaving + grad_enter

    grad_dt = mm((x_wide * grad_xdt).astype(BF), gather) + grad_tail
    upper = (row_ids(rows) <= lax.broadcasted_iota(jnp.int32, (1, rows), 1)).astype(F32).astype(BF)
    grad_steps = split_sum(upper, grad_cum, 3)
    grad_dt = grad_dt + blk.decay * grad_steps
    grad_raw = grad_dt / (1.0 + jnp.exp(-blk.raw))
    small_ref[Small.BIAS_GRAD : Small.BIAS_GRAD + 1, :LANE] += jnp.sum(grad_raw, axis=0, keepdims=True)
    small_ref[Small.LOG_GRAD : Small.LOG_GRAD + 1, :LANE] += (
        jnp.sum(blk.dt * grad_steps, axis=0, keepdims=True) * blk.decay
    )
    small_ref[Small.SKIP_GRAD : Small.SKIP_GRAD + 1, :own] += jnp.sum(dy_wide * x_wide, axis=0, keepdims=True)

    grad_x = blk.dt_wide * (grad_xdt + blk.tail_wide * taken) + skip_ref[Small.HEADS : Small.HEADS + 1, :] * dy_wide
    grad_low = jnp.concatenate([grad_x.astype(BF).astype(F32), grad_b, grad_c], axis=1)
    grad_pre = grad_low * (sig * (1.0 + pre * (1.0 - sig)))
    ext[0:rows, :] = grad_pre
    conv_in = mix_ref[:, :chans]
    small_ref[Small.BIAS : Small.BIAS + 1, :] += jnp.sum(grad_pre, axis=0, keepdims=True)
    grad_in = jnp.zeros((rows, chans), F32)
    for lag in range(CONV_K):
        back = grad_pre if lag == 0 else ext[lag : lag + rows, :]
        if lag:
            _, start = segment_at(blk.position + lag, ends_ref)
            back = back * (blk.position >= start).astype(F32)
        tap = CONV_K - 1 - lag
        grad_in = grad_in + taps_ref[tap : tap + 1, :] * back
        small_ref[tap : tap + 1, :] += jnp.sum(conv_in * back, axis=0, keepdims=True)
    rim[...] = grad_pre[0:8, :]
    grad_ref[...] = jnp.concatenate([grad_in.astype(BF), grad_raw.astype(BF)], axis=1)


def scan_backward(ends, pre, mix, grad_scan, entering, taps, head_rows, skip_row, carries, grad, call, calls, after):
    length, cols = mix.shape
    chans = cols - LANE
    own = chans - 2 * N
    blocks = length // BLOCK_LEN
    each = blocks // calls
    last = blocks - 1 - call * each
    if call == 0:
        carries = [jnp.zeros(s, F32) for s in ((own, N), (8, chans), (8, chans))]
    held = () if call == 0 else (grad,)

    def rows_of(width, rows=BLOCK_LEN):
        return pl.BlockSpec((rows, width), lambda i, ends: (last - i, 0))

    def whole(array):
        return pl.BlockSpec(array.shape, lambda i, ends: (0, 0))

    grad, *carries = pl.pallas_call(
        functools.partial(scan_backward_kernel, base=last),
        grid_spec=pltpu.PrefetchScalarGridSpec(
            num_scalar_prefetch=1,
            grid=(each,),
            in_specs=[rows_of(chans), rows_of(cols), rows_of(own), rows_of(N, rows=own)]
            + [whole(a) for a in (taps, head_rows, skip_row, *carries)]
            + [pl.BlockSpec(memory_space=pl.ANY)] * len(held)
            + [whole(a) for a in after],
            out_specs=[rows_of(cols)] + [whole(a) for a in carries],
            scratch_shapes=[pltpu.VMEM((BLOCK_LEN + 8, chans), F32)],
        ),
        out_shape=[jax.ShapeDtypeStruct((length, cols), BF)]
        + [jax.ShapeDtypeStruct(a.shape, F32) for a in carries],
        input_output_aliases={11: 0} if held else {},
        compiler_params=pltpu.CompilerParams(vmem_limit_bytes=SCAN_VMEM),
        cost_estimate=pl.CostEstimate(flops=each * 2**31, bytes_accessed=0, transcendentals=0),
        name="scan_backward",
    )(ends, pre, mix, grad_scan, entering, taps, head_rows, skip_row, *carries, *held, *after)
    return grad, carries


def shards(
    hidden, seq_lens, norm_w, w_in, conv_w, conv_b, dt_bias, a_log, skip_gain, gate_w, w_out, cotangent
):
    dp, heads = lax.axis_size("dp"), lax.axis_size("heads")
    my_dp, my_head = lax.axis_index("dp"), lax.axis_index("heads")
    me = my_dp * heads + my_head
    rows_dev, width = hidden.shape
    length = rows_dev * heads
    w_rows = w_in.shape[0]
    out_rows = w_out.shape[0]
    own = DI // heads
    own_heads = own // P_SIZE
    chans = own + 2 * N
    taps_dev = conv_b.shape[0]
    ends = jnp.cumsum(seq_lens[0]).astype(jnp.int32)
    where = where_vector(ends)
    owners = [where[RING + heads + k] for k in range(dp)]
    striped = out_rows % P_SIZE == 0
    per_block = own_heads // dp if striped else 0

    def split_own(array, size):
        rows = array.shape[0]
        if striped:
            cut = array.reshape(rows, dp, heads, per_block * size).transpose(2, 0, 1, 3)
        else:
            cut = array.reshape(rows, heads, own_heads * size).transpose(1, 0, 2)
        return cut.reshape(heads, rows, own_heads * size)

    pad = LANE - own_heads
    mix_cut = jnp.concatenate(
        [
            split_own(w_in[:, DI : 2 * DI], P_SIZE),
            jnp.broadcast_to(w_in[None, :, 2 * DI : DI + CONV_CH], (heads, w_rows, 2 * N)),
            split_own(w_in[:, DI + CONV_CH :], 1),
            jnp.zeros((heads, w_rows, pad), BF),
        ],
        axis=2,
    )
    gate_cut = split_own(w_in[:, :DI], P_SIZE)

    def to_heads(cut):
        return lax.all_to_all(cut, "heads", split_axis=0, concat_axis=0, tiled=True)

    hidden_ring = GatherRing(hidden, "heads")
    steps = hidden_ring.half
    w_mix = to_heads(mix_cut)
    route = [(q, (q % dp) * heads + q // dp) for q in range(dp * heads)]
    out_gather = GatherDp(w_out if striped else lax.ppermute(w_out, ("dp", "heads"), route))
    small = pack_small(conv_w, conv_b, norm_w, gate_w, dt_bias, a_log, skip_gain)
    for axis in ("heads", "dp"):
        for bits in powers(axis):
            small = doubled(small, axis, bits)

    def placed(distances, buffer, after=()):
        found = [f for f in ring_rows([hidden_ring.arrived.get(d, []) for d in range(heads)]) if f[0] in distances]
        return place(where, found, buffer, length, after)

    placing = []
    for step in range(1, steps):
        if step == 1:
            w_mix, small, where, gate_cut, *arrived = hidden_ring.advance(
                w_mix, small, where, gate_cut, *out_gather.moving
            )
            mix_gather = GatherDp(w_mix.reshape(heads * w_rows, -1))
            out_gather.relay(arrived)
            tokens = placed((0, 1, heads - 1), None)
        elif step == 2:
            cot, *placing = hidden_ring.advance(cotangent, stand(tokens))
            tokens = placed((step, heads - step), tokens, placing)
            cot_ring = GatherRing(cot, "heads")
        elif step == 3:
            ready, *arrived = hidden_ring.advance(stand(tokens), *mix_gather.moving)
            mix_gather.relay(arrived)
            tokens = placed((step, heads - step), tokens, [ready])
        else:
            placing = hidden_ring.advance(stand(tokens))
            tokens = placed((step, heads - step), tokens, placing)
    taps, gate_gain, norm_row, head_rows, skip_row = unpack(
        where, dp, heads, striped, own, width, (taps_dev, w_rows, out_rows), small
    )
    ready, norm_row, gate_cut, *arrived = hidden_ring.advance(
        stand(tokens), norm_row, gate_cut, *mix_gather.far, *out_gather.far
    )
    tokens = placed((heads // 2,), tokens, [ready])
    mix_pieces, out_pieces = mix_gather.all(arrived[: dp // 2]), out_gather.all(arrived[dp // 2 :])
    w_gate = to_heads(gate_cut)

    (norm_row,) = cot_ring.advance(norm_row)
    normed, mix = project(where, heads, norm_row, tokens, mix_pieces)
    ready, w_gate = cot_ring.advance(stand(mix), w_gate)
    gate_gather = GatherDp(w_gate.reshape(heads * w_rows, -1))
    pre, scanned, entering = scan_forward(ends, mix, taps, head_rows, skip_row, 1, [ready])
    ready = stand(scanned)
    for step in range(3, steps):
        ready, *gate_gather.moving = cot_ring.advance(ready, *gate_gather.moving)
    gate_gather.relay(gate_gather.moving)
    gate_pieces = gate_gather.all(gate_gather.far)
    gate, w_full, branch = gate_forward(
        where, heads, normed, scanned, gate_gain, gate_pieces, out_pieces, [ready]
    )
    ready = stand(gate)

    branch_ring = ScatterRing(branch, "heads")
    cot_ring.advance()
    cot_live, weighted, sums = gate_sums(where, cot_ring.all(), w_full, scanned, gate, gate_gain, [ready])
    sums = sums + lax.ppermute(sums, "heads", xor_route(heads, 1))
    (sums,) = branch_ring.advance(sums)
    sums = sum(pairs(sums, "heads"))
    grad_scan, grad_gate, gated = gate_backward(where, dp, striped, sums, weighted, scanned, gate, gate_gain)
    (ready,) = branch_ring.advance(stand(grad_gate))
    gate_scatter = ScatterDp(*weight_term(normed, grad_gate))

    def back(call, carries, grad_mix, *after):
        return scan_backward(
            ends, pre, mix, grad_scan, entering, taps, head_rows, skip_row, carries, grad_mix, call, 2, after
        )

    grad_mix, carries = back(0, None, (), stand(gate_scatter.kept), ready)
    ready, *arrived = branch_ring.advance(stand(carries[0]), *gate_scatter.moving)
    gate_scatter.relay(arrived)
    if striped:
        terms = weight_term(gated, cot_live)
    else:
        term = mm(gated, cot_live, ((0,), (0,))).astype(BF)
        cuts = [lax.dynamic_slice(term, (o * out_rows, 0), (out_rows, width)) for o in owners]
        terms = jnp.concatenate(cuts[: dp // 2]), jnp.concatenate(cuts[dp // 2 :])
    out_scatter = ScatterDp(*terms)
    grad_mix, carries = back(1, carries, grad_mix, ready, stand(terms[0]))
    small_grads = carries[2]
    small_core = other_core(small_grads)
    mix_scatter = ScatterDp(*weight_term(normed, grad_mix))
    small_core, ready = together(small_core, stand(mix_scatter.kept))
    small_grads = small_grads + small_core
    small_moving = [lax.ppermute(small_grads, "dp", xor_route(dp, bits)) for bits in range(2, dp, 2)]
    parts = project_back(
        where, heads, grad_gate, grad_mix, gate_pieces, mix_pieces, [ready, stand(small_grads)]
    )

    grad_ring = ScatterRings(parts, "heads")
    while branch_ring.left > 1:
        branch_ring.advance()
    n_gate, n_out, n_mix = len(gate_scatter.moving), len(out_scatter.moving), len(mix_scatter.moving)
    ready, *arrived = branch_ring.advance(
        stand(parts[0][0]), *gate_scatter.moving, *out_scatter.moving, *mix_scatter.moving, *small_moving
    )
    from_gate, arrived = arrived[:n_gate], arrived[n_gate:]
    from_out, arrived = arrived[:n_out], arrived[n_out:]
    mix_scatter.relay(arrived[:n_mix], ready)
    small_grads = doubled(sum(arrived[n_mix:], small_grads), "heads", 1)
    for step in range(1, steps):
        if step == 1:
            grad_ring.advance()
            ready = stand(grad_ring.last)
            gate_cols = to_heads(gate_scatter.all(from_gate, BF, ready).reshape(heads, w_rows, own))
            out_scatter.relay(from_out, ready)
        elif step == 2:
            (small_grads,) = grad_ring.advance(small_grads)
            small_grads = doubled(small_grads, "heads", 2)
        elif step == 3:
            n_mix = len(mix_scatter.moving)
            small_grads, *arrived = grad_ring.advance(small_grads, *mix_scatter.moving, *branch_ring.sums)
            arrived, branch_sums = arrived[:n_mix], arrived[n_mix:]
            mix_cols = mix_scatter.all(arrived, BF, stand(grad_ring.last))
            mix_cols = to_heads(mix_cols.reshape(heads, w_rows, -1))
            for bits in powers("heads")[2:]:
                small_grads = doubled(small_grads, "heads", bits)
            output = output_of(where, sums, hidden, (*branch[0], *branch_sums, stand(grad_ring.last)))
        else:
            grad_ring.advance()
    w_in_grad, norm_sums = weight_rows(dp, striped, gate_cols, mix_cols, w_in)
    output, norm_sums, *arrived = grad_ring.advance(output, norm_sums, *out_scatter.moving)
    own_parts = [part for k in range(2) for part in (parts[0][k], *grad_ring.sums[k])]
    input_grad = input_grad_of(where, dp, own_parts, hidden, cotangent, norm_row)
    if not arrived:
        arrived = [jnp.zeros(w_out.shape, BF)]
    if striped:
        w_out_grad, out_sums = out_grad_of(arrived[0], out_scatter.sums[0], w_out)
    else:
        w_out_grad = add_last(arrived[0], out_scatter.sums[0], F32, ())
        w_out_grad = lax.ppermute(w_out_grad, ("dp", "heads"), [(dst, src) for src, dst in route])
        out_sums = jnp.sum(w_out.astype(F32) * w_out_grad, axis=1, keepdims=True)
    gate_w_grad = out_sums[:, 0] / gate_w.astype(F32)
    norm_w_grad = norm_sums[:, 0] / norm_w.astype(F32)

    taps_grad, bias_grad, by_head = collect(where, dp, heads, striped, taps_dev, small_grads)
    return (
        output,
        input_grad,
        norm_w_grad,
        w_in_grad,
        taps_grad,
        bias_grad.reshape(-1),
        by_head[Small.BIAS_GRAD, :own_heads],
        by_head[Small.LOG_GRAD, :own_heads],
        by_head[Small.SKIP_GRAD, :own_heads],
        gate_w_grad,
        w_out_grad,
    )


def solution(mesh):
    both = ("dp", "heads")
    placed = (
        P(both, None),
        P("dp", None),
        P(both),
        P(both, None),
        P(None, both),
        P(both),
        P("heads"),
        P("heads"),
        P("heads"),
        P(both),
        P(both, None),
        P(both, None),
    )
    return jax.shard_map(
        shards,
        mesh=mesh,
        in_specs=placed,
        out_specs=(
            P(both, None),
            P(both, None),
            P(both),
            P(both, None),
            P(None, both),
            P(both),
            P("heads"),
            P("heads"),
            P("heads"),
            P(both),
            P(both, None),
        ),
        check_vma=False,
    )
```
